32 devices in a mesh: scene: 2 (over x), blk: 4 (over y, core), grp: 4 (over z).
Axes of the slice: x: 2, y: 2, z: 4, core: 2. Of those that a mesh axis runs over, the one named last changes fastest.
Arguments:
- unary: float32 [32, 8192], P(None, ('scene', 'blk', 'grp')), parts along dimension 1, may hold values from -6 to 6
- member: int32 [8192], P(('scene', 'blk', 'grp')), parts along dimension 0, may hold values from 0 to 4095, each once
- features: bfloat16 [6, 8192], P(None, 'scene'), parts along dimension 1, may hold values from 0 to 3, as said below
- compat: float32 [32, 32], replicated, may hold values from -0.3125 to 0.3125
Outputs:
- marginals: float32 [32, 8192], P(None, ('scene', 'blk', 'grp')), parts along dimension 1
- pairwise: float32 [32, 8192], P(None, ('scene', 'blk', 'grp')), parts along dimension 1
The draws below stay inside these ranges and needn't reach their ends.
There are 2 independent parts, one for each index of `scene`. The reference program is written for one: setup_inputs(seed, part) draws one part's arguments, and reference() takes and returns one part's arrays. A program takes and returns all parts, laid end to end along the dimension named above; an argument that names none is the same for every part. Nothing has to cross between parts.
Inputs may be any that keep to these rules, and one draw needn't show every extreme that they name: `member`: each superpoint appears in exactly one slot. features are non-negative.
All inputs are finite; a program needn't handle non-finite values.
Results may differ from the reference program's by a relative error of at most 0.0004.
Values may be sent and summed in bfloat16 or wider, within the bound.
No kernel may reach another device: no remote copies, remote signals or barrier semaphores. Data moves between devices by JAX's collectives and lax.ppermute only.
A program may use at most 64 MiB of HBM per device.

```python
import math
import jax
import jax.numpy as jnp
from jax import lax

LABELS = 32
FEATS = 6
ITERS = 2
POINTS = 4096


def draw_features(key, part):
    key = jax.random.fold_in(key, 11)
    span = 3.0
    unit = jax.random.uniform(key, (FEATS, POINTS), jnp.float32)
    return (unit * span).astype(jnp.bfloat16)


def shard_levels(own_key, dims, shards, least, high):
    level, own = 1.0, jax.random.fold_in(own_key, 6)
    for dim, shards_of in shards:
        heights = jnp.exp(jax.random.uniform(jax.random.fold_in(own, dim), (shards_of,), jnp.float32, least / len(shards), high / len(shards)))
        level = level * jnp.repeat(heights, dims[dim] // shards_of).reshape([-1 if axis == dim else 1 for axis in range(len(dims))])
    return level


def normal_values(key, dims, deviation, bound, split=(), kind=jnp.bfloat16):
    level = shard_levels(key, dims, split, -0.22, 0.18) if split else 1.0
    drawn = jax.random.normal(key, dims, jnp.float32) * deviation * level
    return jnp.minimum(jnp.maximum(drawn, -bound), bound).astype(kind)


def setup_inputs(seed: int = 0, part: int = 0) -> dict:
    seeds = jax.random.split(jax.random.key(seed), 5)
    own_keys = jax.random.split(jax.random.fold_in(seeds[4], part), 5)
    unary = normal_values(own_keys[0], (LABELS, POINTS), 2.0, 6.0, ((1, 16),), jnp.float32)
    member = jax.random.permutation(own_keys[1], POINTS).astype(jnp.int32)
    features = draw_features(jax.random.fold_in(jax.random.fold_in(seeds[4], part), 71), part)
    compat = normal_values(seeds[3], (LABELS, LABELS), (max(1, POINTS * POINTS // 45000)) ** -0.5, 0.3125, (), jnp.float32)
    return {"unary": unary, "member": member, "features": features, "compat": compat}


def normalize(logits):
    raised = jnp.exp(logits)
    return raised / jnp.sum(raised, axis=0, keepdims=True)


def reference(unary, member, features, compat):
    feats = jnp.take(features, member, axis=1).astype(jnp.float32)
    norms = jnp.sum(feats * feats, axis=0)
    size = math.gcd(512, POINTS)
    starts = jnp.arange(0, POINTS, size).astype(jnp.int32)
    probs = normalize(-unary)
    pairwise = jnp.zeros_like(unary)
    for sweep_index in range(ITERS):
        qb = probs.astype(jnp.bfloat16)

        def one_block(start):
            rows_f = lax.dynamic_slice_in_dim(feats, start, size, 1)
            rows_n = lax.dynamic_slice_in_dim(norms, start, size, 0)
            cross = jnp.dot(rows_f.T, feats, precision=lax.Precision.HIGHEST, preferred_element_type=jnp.float32)
            dist = rows_n[:, None] + norms[None, :] - 2.0 * cross
            tile = jnp.exp(-0.5 * dist).astype(jnp.bfloat16)
            return lax.dot_general(qb, tile, (((1,), (1,)), ((), ())), preferred_element_type=jnp.float32)

        blocks = lax.map(one_block, starts)
        message = jnp.transpose(blocks, (1, 0, 2)).reshape(LABELS, POINTS) - qb.astype(jnp.float32)
        pairwise = jnp.dot(compat, message, precision=lax.Precision.HIGHEST, preferred_element_type=jnp.float32)
        probs = normalize(-unary - pairwise)
    return probs, pairwise
```

```python
import jax
import jax.numpy as jnp
from jax import lax
from jax.experimental import pallas as pl
from jax.experimental.pallas import tpu as pltpu
from jax.sharding import PartitionSpec as P

AUX = 16
VMEM_LIMIT = 56 * 1024 * 1024


def normalize(logits):
    raised = jnp.exp(logits)
    return raised / jnp.sum(raised, axis=0, keepdims=True)


def three_parts(value):
    high = value.astype(jnp.bfloat16).astype(jnp.float32)
    middle = (value - high).astype(jnp.bfloat16).astype(jnp.float32)
    return [high, middle, value - high - middle]


def prepare_kernel(feats_ref, unary_ref, packed_ref, rows_ref):
    labels, own = unary_ref.shape
    feats = feats_ref[...].astype(jnp.float32)
    norms = three_parts(-0.5 * jnp.sum(feats * feats, axis=0, keepdims=True))
    ones = jnp.ones((3, own), jnp.float32)
    spare = jnp.zeros((AUX - feats.shape[0] - 6, own), jnp.float32)
    columns = jnp.concatenate([feats] + norms + [ones, spare], axis=0)
    rows = jnp.concatenate([feats, ones] + norms + [spare], axis=0)
    packed_ref[pl.ds(0, labels), :] = normalize(-unary_ref[...]).astype(jnp.bfloat16)
    packed_ref[pl.ds(labels, AUX), :] = columns.astype(jnp.bfloat16)
    rows_ref[...] = rows.astype(jnp.bfloat16)


def over_blocks(count, body, start):
    if count <= 16:
        for index in range(count):
            start = body(index, start)
        return start
    return lax.fori_loop(0, count, body, start)


def finish(message, qb, unary_ref, compat_ref):
    message = message - qb.astype(jnp.float32)
    pairwise = jnp.dot(
        compat_ref[...], message, precision=lax.Precision.HIGHEST,
        preferred_element_type=jnp.float32,
    )
    return normalize(-unary_ref[...] - pairwise), pairwise


def first_kernel(labels, count, rows_ref, own_ref, unary_ref, compat_ref, packed_ref, tile_ref, q_ref):
    rows = rows_ref[...]

    def body(index, total):
        columns = packed_ref[index, pl.ds(labels, AUX), :]
        exponent = lax.dot_general(
            columns, rows, (((0,), (0,)), ((), ())), preferred_element_type=jnp.float32
        )
        tile = jnp.exp(exponent).astype(jnp.bfloat16)
        tile_ref[index] = tile
        return total + jnp.dot(
            packed_ref[index, pl.ds(0, labels), :], tile, preferred_element_type=jnp.float32
        )

    total = over_blocks(count, body, jnp.zeros(unary_ref.shape, jnp.float32))
    probs, _ = finish(total, own_ref[pl.ds(0, labels), :], unary_ref, compat_ref)
    q_ref[...] = probs.astype(jnp.bfloat16)


def second_kernel(count, own_ref, unary_ref, compat_ref, q_ref, tile_ref, probs_ref, pairwise_ref):
    def body(index, total):
        return total + jnp.dot(q_ref[index], tile_ref[index], preferred_element_type=jnp.float32)

    total = over_blocks(count, body, jnp.zeros(unary_ref.shape, jnp.float32))
    probs, pairwise = finish(total, own_ref[...], unary_ref, compat_ref)
    probs_ref[...] = probs
    pairwise_ref[...] = pairwise


def exchange(value):
    for axis in ("grp", "blk"):
        count = lax.axis_size(axis)
        copies = jnp.broadcast_to(value[None], (count,) + value.shape)
        value = lax.all_to_all(copies, axis, 0, 0)
    return value.reshape((-1,) + value.shape[2:])


def shards(unary, member, features, compat):
    labels, own = unary.shape
    count = lax.axis_size("blk") * lax.axis_size("grp")
    own_feat = jnp.take(features, member, axis=1)
    params = pltpu.CompilerParams(vmem_limit_bytes=VMEM_LIMIT)
    packed, rows = pl.pallas_call(
        prepare_kernel,
        out_shape=(
            jax.ShapeDtypeStruct((labels + AUX, own), jnp.bfloat16),
            jax.ShapeDtypeStruct((AUX, own), jnp.bfloat16),
        ),
        compiler_params=params,
    )(own_feat, unary)
    everything = exchange(packed)
    tile, qb = pl.pallas_call(
        lambda *refs: first_kernel(labels, count, *refs),
        out_shape=(
            jax.ShapeDtypeStruct((count, own, own), jnp.bfloat16),
            jax.ShapeDtypeStruct((labels, own), jnp.bfloat16),
        ),
        compiler_params=params,
    )(rows, packed, unary, compat, everything)
    return pl.pallas_call(
        lambda *refs: second_kernel(count, *refs),
        out_shape=(
            jax.ShapeDtypeStruct((labels, own), jnp.float32),
            jax.ShapeDtypeStruct((labels, own), jnp.float32),
        ),
        compiler_params=params,
    )(qb, unary, compat, exchange(qb), tile)


def solution(mesh):
    in_specs = (P(None, ("scene", "blk", "grp")), P(("scene", "blk", "grp")), P(None, "scene"), P())
    out_specs = (P(None, ("scene", "blk", "grp")), P(None, ("scene", "blk", "grp")))
    return jax.shard_map(shards, mesh=mesh, in_specs=in_specs, out_specs=out_specs, check_vma=False)
```

```python
import functools
import jax
import jax.numpy as jnp
from jax import lax
from jax.experimental import pallas as pl
from jax.experimental.pallas import tpu as pltpu
from jax.sharding import PartitionSpec as P

AUX = 16
VMEM_LIMIT = 56 * 1024 * 1024


def normalize(logits):
    raised = jnp.exp(logits)
    return raised / jnp.sum(raised, axis=0, keepdims=True)


def three_parts(value):
    high = value.astype(jnp.bfloat16).astype(jnp.float32)
    middle = (value - high).astype(jnp.bfloat16).astype(jnp.float32)
    return [high, middle, value - high - middle]


def prepare_kernel(feats_ref, unary_ref, packed_ref, rows_ref):
    labels, own = unary_ref.shape
    feats = feats_ref[...].astype(jnp.float32)
    norms = three_parts(-0.5 * jnp.sum(feats * feats, axis=0, keepdims=True))
    ones = jnp.ones((3, own), jnp.float32)
    spare = jnp.zeros((AUX - feats.shape[0] - 6, own), jnp.float32)
    columns = jnp.concatenate([feats] + norms + [ones, spare], axis=0)
    rows = jnp.concatenate([feats, ones] + norms + [spare], axis=0)
    packed_ref[pl.ds(0, labels), :] = normalize(-unary_ref[...]).astype(jnp.bfloat16)
    packed_ref[pl.ds(labels, AUX), :] = columns.astype(jnp.bfloat16)
    rows_ref[...] = rows.astype(jnp.bfloat16)


def over_blocks(refs, body, start):
    base = 0
    for ref in refs:
        size = ref.shape[0]
        if size <= 16:
            for index in range(size):
                start = body(ref, index, base + index, start)
        else:
            step = lambda index, total, ref=ref, base=base: body(ref, index, base + index, total)
            start = lax.fori_loop(0, size, step, start)
        base += size
    return start


def finish(message, qb, unary_ref, compat_ref):
    message = message - qb.astype(jnp.float32)
    pairwise = jnp.dot(
        compat_ref[...], message, precision=lax.Precision.HIGHEST,
        preferred_element_type=jnp.float32,
    )
    return normalize(-unary_ref[...] - pairwise), pairwise


def first_kernel(labels, *refs):
    rows_ref, own_ref, unary_ref, compat_ref, *packed_refs = refs[:-2]
    tile_ref, q_ref = refs[-2:]
    rows = rows_ref[...]

    def body(packed_ref, index, place, total):
        columns = packed_ref[index, pl.ds(labels, AUX), :]
        exponent = lax.dot_general(
            columns, rows, (((0,), (0,)), ((), ())), preferred_element_type=jnp.float32
        )
        tile = jnp.exp(exponent).astype(jnp.bfloat16)
        tile_ref[place] = tile
        return total + jnp.dot(
            packed_ref[index, pl.ds(0, labels), :], tile, preferred_element_type=jnp.float32
        )

    total = over_blocks(packed_refs, body, jnp.zeros(unary_ref.shape, jnp.float32))
    probs, _ = finish(total, own_ref[pl.ds(0, labels), :], unary_ref, compat_ref)
    q_ref[...] = probs.astype(jnp.bfloat16)


def second_kernel(*refs):
    own_ref, unary_ref, compat_ref, tile_ref, *q_refs = refs[:-2]
    probs_ref, pairwise_ref = refs[-2:]

    def body(q_ref, index, place, total):
        return total + jnp.dot(
            q_ref[index], tile_ref[place], preferred_element_type=jnp.float32
        )

    total = over_blocks(q_refs, body, jnp.zeros(unary_ref.shape, jnp.float32))
    probs, pairwise = finish(total, own_ref[...], unary_ref, compat_ref)
    probs_ref[...] = probs
    pairwise_ref[...] = pairwise


def shifted(value, blk_steps, grp_steps):
    blks, grps = lax.axis_size("blk"), lax.axis_size("grp")
    pairs = [
        (blk * grps + grp, (blk + blk_steps) % blks * grps + (grp + grp_steps) % grps)
        for blk in range(blks)
        for grp in range(grps)
    ]
    return lax.ppermute(value, ("blk", "grp"), pairs)


def direct(value):
    value = value[None]
    return [
        shifted(value, blk_steps, grp_steps) if blk_steps or grp_steps else value
        for blk_steps in range(lax.axis_size("blk"))
        for grp_steps in range(lax.axis_size("grp"))
    ]


def two_phase(value):
    near = [value] + [shifted(value, 0, steps) for steps in range(1, lax.axis_size("grp"))]
    near = jnp.stack(near)
    return [near] + [shifted(near, steps, 0) for steps in range(1, lax.axis_size("blk"))]


def shards(unary, member, features, compat):
    labels, own = unary.shape
    count = lax.axis_size("blk") * lax.axis_size("grp")
    own_feat = jnp.take(features, member, axis=1)
    params = pltpu.CompilerParams(vmem_limit_bytes=VMEM_LIMIT)
    packed, rows = pl.pallas_call(
        prepare_kernel,
        out_shape=(
            jax.ShapeDtypeStruct((labels + AUX, own), jnp.bfloat16),
            jax.ShapeDtypeStruct((AUX, own), jnp.bfloat16),
        ),
        compiler_params=params,
    )(own_feat, unary)
    spread = direct if count <= 16 else two_phase
    tile, qb = pl.pallas_call(
        functools.partial(first_kernel, labels),
        out_shape=(
            jax.ShapeDtypeStruct((count, own, own), jnp.bfloat16),
            jax.ShapeDtypeStruct((labels, own), jnp.bfloat16),
        ),
        compiler_params=params,
    )(rows, packed, unary, compat, *spread(packed))
    return pl.pallas_call(
        second_kernel,
        out_shape=(
            jax.ShapeDtypeStruct((labels, own), jnp.float32),
            jax.ShapeDtypeStruct((labels, own), jnp.float32),
        ),
        compiler_params=params,
    )(qb, unary, compat, tile, *two_phase(qb))


def solution(mesh):
    in_specs = (P(None, ("scene", "blk", "grp")), P(("scene", "blk", "grp")), P(None, "scene"), P())
    out_specs = (P(None, ("scene", "blk", "grp")), P(None, ("scene", "blk", "grp")))
    return jax.shard_map(shards, mesh=mesh, in_specs=in_specs, out_specs=out_specs, check_vma=False)
```

```python
import functools
import jax
import jax.numpy as jnp
from jax import lax
from jax.experimental import pallas as pl
from jax.experimental.pallas import tpu as pltpu
from jax.sharding import PartitionSpec as P

AUX = 16
VMEM_LIMIT = 56 * 1024 * 1024


def normalize(logits):
    raised = jnp.exp(logits)
    return raised / jnp.sum(raised, axis=0, keepdims=True)


def three_parts(value):
    high = value.astype(jnp.bfloat16).astype(jnp.float32)
    middle = (value - high).astype(jnp.bfloat16).astype(jnp.float32)
    return [high, middle, value - high - middle]


def prepare_kernel(feats_ref, unary_ref, packed_ref, rows_ref):
    labels, own = unary_ref.shape
    feats = feats_ref[...].astype(jnp.float32)
    norms = three_parts(-0.5 * jnp.sum(feats * feats, axis=0, keepdims=True))
    ones = jnp.ones((3, own), jnp.float32)
    spare = jnp.zeros((AUX - feats.shape[0] - 6, own), jnp.float32)
    columns = jnp.concatenate([feats] + norms + [ones, spare], axis=0)
    rows = jnp.concatenate([feats, ones] + norms + [spare], axis=0)
    packed_ref[pl.ds(0, labels), :] = normalize(-unary_ref[...]).astype(jnp.bfloat16)
    packed_ref[pl.ds(labels, AUX), :] = columns.astype(jnp.bfloat16)
    rows_ref[...] = rows.astype(jnp.bfloat16)


def over_blocks(refs, body, start):
    base = 0
    for ref in refs:
        size = ref.shape[0]
        if size <= 16:
            for index in range(size):
                start = body(ref, index, base + index, start)
        else:
            step = lambda index, total, ref=ref, base=base: body(ref, index, base + index, total)
            start = lax.fori_loop(0, size, step, start)
        base += size
    return start


def finish(message, qb, unary_ref, compat_ref):
    message = message - qb.astype(jnp.float32)
    pairwise = jnp.dot(
        compat_ref[...], message, precision=lax.Precision.HIGHEST,
        preferred_element_type=jnp.float32,
    )
    return normalize(-unary_ref[...] - pairwise), pairwise


def first_kernel(labels, *refs):
    rows_ref, own_ref, unary_ref, compat_ref, *packed_refs = refs[:-2]
    tile_ref, q_ref = refs[-2:]
    rows = rows_ref[...]

    def body(packed_ref, index, place, total):
        columns = packed_ref[index, pl.ds(labels, AUX), :]
        exponent = lax.dot_general(
            columns, rows, (((0,), (0,)), ((), ())), preferred_element_type=jnp.float32
        )
        tile = jnp.exp(exponent).astype(jnp.bfloat16)
        tile_ref[place] = tile
        return total + jnp.dot(
            packed_ref[index, pl.ds(0, labels), :], tile, preferred_element_type=jnp.float32
        )

    total = over_blocks(packed_refs, body, jnp.zeros(unary_ref.shape, jnp.float32))
    probs, _ = finish(total, own_ref[pl.ds(0, labels), :], unary_ref, compat_ref)
    q_ref[...] = probs.astype(jnp.bfloat16)


def second_kernel(*refs):
    own_ref, unary_ref, compat_ref, tile_ref, *q_refs = refs[:-2]
    probs_ref, pairwise_ref = refs[-2:]

    def body(q_ref, index, place, total):
        return total + jnp.dot(
            q_ref[index], tile_ref[place], preferred_element_type=jnp.float32
        )

    total = over_blocks(q_refs, body, jnp.zeros(unary_ref.shape, jnp.float32))
    probs, pairwise = finish(total, own_ref[...], unary_ref, compat_ref)
    probs_ref[...] = probs
    pairwise_ref[...] = pairwise


def gathered(value):
    return lax.all_gather(value, ("blk", "grp"), axis=0, tiled=False)


def shards(unary, member, features, compat):
    labels, own = unary.shape
    count = lax.axis_size("blk") * lax.axis_size("grp")
    own_feat = jnp.take(features, member, axis=1)
    params = pltpu.CompilerParams(vmem_limit_bytes=VMEM_LIMIT)
    packed, rows = pl.pallas_call(
        prepare_kernel,
        out_shape=(
            jax.ShapeDtypeStruct((labels + AUX, own), jnp.bfloat16),
            jax.ShapeDtypeStruct((AUX, own), jnp.bfloat16),
        ),
        compiler_params=params,
    )(own_feat, unary)
    tile, qb = pl.pallas_call(
        functools.partial(first_kernel, labels),
        out_shape=(
            jax.ShapeDtypeStruct((count, own, own), jnp.bfloat16),
            jax.ShapeDtypeStruct((labels, own), jnp.bfloat16),
        ),
        compiler_params=params,
    )(rows, packed, unary, compat, gathered(packed))
    return pl.pallas_call(
        second_kernel,
        out_shape=(
            jax.ShapeDtypeStruct((labels, own), jnp.float32),
            jax.ShapeDtypeStruct((labels, own), jnp.float32),
        ),
        compiler_params=params,
    )(qb, unary, compat, tile, gathered(qb))


def solution(mesh):
    in_specs = (P(None, ("scene", "blk", "grp")), P(("scene", "blk", "grp")), P(None, "scene"), P())
    out_specs = (P(None, ("scene", "blk", "grp")), P(None, ("scene", "blk", "grp")))
    return jax.shard_map(shards, mesh=mesh, in_specs=in_specs, out_specs=out_specs, check_vma=False)
```

```python
import functools
import math

import jax
import jax.numpy as jnp
from jax import lax
from jax.experimental import pallas as pl
from jax.experimental.pallas import tpu as pltpu
from jax.sharding import PartitionSpec as P

AUX = 16
LANES = 128
VMEM_LIMIT = 56 * 1024 * 1024
KEPT_BYTES = 4 * 1024 * 1024


def normalize(logits):
    raised = jnp.exp(logits)
    return raised / jnp.sum(raised, axis=0, keepdims=True)


def three_parts(value):
    high = value.astype(jnp.bfloat16).astype(jnp.float32)
    middle = (value - high).astype(jnp.bfloat16).astype(jnp.float32)
    return [high, middle, value - high - middle]


def pick_features(features_ref, member):
    feats, points = features_ref.shape
    own = member.shape[1]
    groups = points // LANES
    wide = features_ref[...].astype(jnp.float32)
    wide = jnp.concatenate([wide, jnp.zeros((8 - feats, points), jnp.float32)], axis=0)
    table = jnp.concatenate(
        [wide[:, group * LANES:(group + 1) * LANES] for group in range(groups)], axis=0
    ).astype(jnp.bfloat16)
    lane = lax.broadcasted_iota(jnp.int32, (LANES, own), 0)
    chosen = jnp.where(lane == member % LANES, 1.0, 0.0).astype(jnp.bfloat16)
    found = jnp.dot(table, chosen, preferred_element_type=jnp.float32)
    found = found.reshape(groups, 8, own)
    group = lax.broadcasted_iota(jnp.int32, (groups, 8, own), 0)
    return jnp.sum(jnp.where(group == (member // LANES)[None], found, 0.0), axis=0)


def prepare_kernel(features_ref, member_ref, unary_ref, sent_ref):
    labels = unary_ref.shape[0]
    sent_ref[pl.ds(0, labels), :] = unary_ref[...]
    sent_ref[pl.ds(labels, 8), :] = pick_features(features_ref, member_ref[...])


def pack_kernel(labels, feats, *refs):
    near_refs, packed_ref, rows_ref = refs[:-2], refs[-2], refs[-1]
    for place, near_ref in enumerate(near_refs):
        own = near_ref.shape[1]
        chosen = near_ref[pl.ds(labels, 8), :][:feats]
        norms = three_parts(-0.5 * jnp.sum(chosen * chosen, axis=0, keepdims=True))
        ones = jnp.ones((3, own), jnp.float32)
        spare = jnp.zeros((AUX - feats - 6, own), jnp.float32)
        columns = jnp.concatenate([chosen] + norms + [ones, spare], axis=0)
        rows = jnp.concatenate([chosen, ones] + norms + [spare], axis=0)
        labels_now = normalize(-near_ref[pl.ds(0, labels), :])
        packed_ref[place, pl.ds(0, labels), :] = labels_now.astype(jnp.bfloat16)
        packed_ref[place, pl.ds(labels, AUX), :] = columns.astype(jnp.bfloat16)
        rows_ref[:, pl.ds(place * own, own)] = rows.astype(jnp.bfloat16)


def over_blocks(refs, body, start):
    base = 0
    unrolled = sum(ref.shape[0] for ref in refs) <= 16
    for ref in refs:
        size = ref.shape[0]
        if unrolled:
            for index in range(size):
                start = body(ref, index, base + index, start)
        else:
            step = lambda index, total, ref=ref, base=base: body(ref, index, base + index, total)
            start = lax.fori_loop(0, size, step, start)
        base += size
    return start


def finish(message, qb, unary, compat_ref):
    message = message - qb.astype(jnp.float32)
    pairwise = jnp.dot(
        compat_ref[...], message, precision=lax.Precision.HIGHEST,
        preferred_element_type=jnp.float32,
    )
    return normalize(-unary - pairwise), pairwise


def first_kernel(labels, nears, *refs):
    rows_ref, compat_ref = refs[:2]
    near_refs = refs[2:2 + nears]
    packed_refs = refs[2 + nears:-2]
    tile_ref, q_ref = refs[-2:]
    own = near_refs[0].shape[1]
    rows = rows_ref[...]

    def body(packed_ref, index, place, total):
        columns = packed_ref[index, pl.ds(labels, AUX), :]
        exponent = lax.dot_general(
            columns, rows, (((0,), (0,)), ((), ())), preferred_element_type=jnp.float32
        )
        tile = jnp.exp(exponent).astype(jnp.bfloat16)
        tile_ref[place] = tile[:, :own]
        return total + jnp.dot(
            packed_ref[index, pl.ds(0, labels), :], tile, preferred_element_type=jnp.float32
        )

    total = over_blocks(packed_refs, body, jnp.zeros((labels, nears * own), jnp.float32))
    labels_now = [packed_refs[0][near, pl.ds(0, labels), :] for near in range(nears)]
    unary = [near_ref[pl.ds(0, labels), :] for near_ref in near_refs]
    probs, _ = finish(
        total, jnp.concatenate(labels_now, axis=1), jnp.concatenate(unary, axis=1), compat_ref
    )
    for near in range(nears):
        q_ref[near] = probs[:, near * own:(near + 1) * own].astype(jnp.bfloat16)


def second_kernel(*refs):
    unary_ref, compat_ref, tile_ref, *q_refs = refs[:-2]
    probs_ref, pairwise_ref = refs[-2:]

    def body(q_ref, index, place, total):
        return total + jnp.dot(
            q_ref[index], tile_ref[place], preferred_element_type=jnp.float32
        )

    total = over_blocks(q_refs, body, jnp.zeros(unary_ref.shape, jnp.float32))
    probs, pairwise = finish(total, q_refs[0][0], unary_ref[...], compat_ref)
    probs_ref[...] = probs
    pairwise_ref[...] = pairwise


def all_shifts(value, axis):
    count = lax.axis_size(axis)
    found = [value]
    for steps in range(1, count):
        pairs = [(source, (source + steps) % count) for source in range(count)]
        found.append(lax.ppermute(value, axis, pairs))
    return found


def small(dims, kind):
    return math.prod(dims) * jnp.dtype(kind).itemsize <= KEPT_BYTES


def call(kernel, out_shapes, *operands):
    held = [
        pltpu.with_memory_space_constraint(operand, pltpu.VMEM)
        if small(operand.shape, operand.dtype) else operand
        for operand in operands
    ]
    return pl.pallas_call(
        kernel,
        out_shape=tuple(out_shapes),
        compiler_params=pltpu.CompilerParams(vmem_limit_bytes=VMEM_LIMIT),
    )(*held)


def kept(dims, kind):
    return pltpu.VMEM(dims, kind) if small(dims, kind) else jax.ShapeDtypeStruct(dims, kind)


def shards(unary, member, features, compat):
    labels, own = unary.shape
    nears = lax.axis_size("grp")
    count = lax.axis_size("blk") * nears
    (sent,) = call(
        prepare_kernel, [kept((labels + 8, own), jnp.float32)], features, member[None], unary
    )
    near = all_shifts(sent, "grp")
    packed, rows = call(
        functools.partial(pack_kernel, labels, features.shape[0]),
        [kept((nears, labels + AUX, own), jnp.bfloat16), kept((AUX, nears * own), jnp.bfloat16)],
        *near,
    )
    tile, q_near = call(
        functools.partial(first_kernel, labels, nears),
        [kept((count, own, own), jnp.bfloat16), kept((nears, labels, own), jnp.bfloat16)],
        rows, compat, *near, *all_shifts(packed, "blk"),
    )
    return call(
        second_kernel,
        [jax.ShapeDtypeStruct((labels, own), jnp.float32)] * 2,
        unary, compat, tile, *all_shifts(q_near, "blk"),
    )


def solution(mesh):
    in_specs = (P(None, ("scene", "blk", "grp")), P(("scene", "blk", "grp")), P(None, "scene"), P())
    out_specs = (P(None, ("scene", "blk", "grp")), P(None, ("scene", "blk", "grp")))
    return jax.shard_map(shards, mesh=mesh, in_specs=in_specs, out_specs=out_specs, check_vma=False)
```

```python
import functools
import math

import jax
import jax.numpy as jnp
from jax import lax
from jax.experimental import pallas as pl
from jax.experimental.pallas import tpu as pltpu
from jax.sharding import PartitionSpec as P

AUX = 16
LANES = 128
VMEM_LIMIT = 56 * 1024 * 1024
KEPT_BYTES = 4 * 1024 * 1024


def normalize(logits):
    raised = jnp.exp(logits)
    return raised / jnp.sum(raised, axis=0, keepdims=True)


def three_parts(value):
    high = value.astype(jnp.bfloat16).astype(jnp.float32)
    middle = (value - high).astype(jnp.bfloat16).astype(jnp.float32)
    return [high, middle, value - high - middle]


def pick_features(features_ref, member):
    feats, points = features_ref.shape
    own = member.shape[1]
    groups = points // LANES
    wide = features_ref[...].astype(jnp.float32)
    wide = jnp.concatenate([wide, jnp.zeros((8 - feats, points), jnp.float32)], axis=0)
    table = jnp.concatenate(
        [wide[:, group * LANES:(group + 1) * LANES] for group in range(groups)], axis=0
    ).astype(jnp.bfloat16)
    lane = lax.broadcasted_iota(jnp.int32, (LANES, own), 0)
    chosen = jnp.where(lane == member % LANES, 1.0, 0.0).astype(jnp.bfloat16)
    found = jnp.dot(table, chosen, preferred_element_type=jnp.float32)
    found = found.reshape(groups, 8, own)
    group = lax.broadcasted_iota(jnp.int32, (groups, 8, own), 0)
    return jnp.sum(jnp.where(group == (member // LANES)[None], found, 0.0), axis=0)


def prepare_kernel(features_ref, member_ref, unary_ref, compat_ref, sent_ref, held_ref):
    labels = unary_ref.shape[0]
    sent_ref[pl.ds(0, labels), :] = unary_ref[...]
    sent_ref[pl.ds(labels, 8), :] = pick_features(features_ref, member_ref[...])
    held_ref[...] = compat_ref[...]


def half_norms(feats):
    return three_parts(-0.5 * jnp.sum(feats * feats, axis=0, keepdims=True))


def product_sides(feats):
    own = feats.shape[1]
    norms = half_norms(feats)
    ones = jnp.ones((3, own), jnp.float32)
    spare = jnp.zeros((AUX - 8 - 6, own), jnp.float32)
    columns = jnp.concatenate([feats] + norms + [ones, spare], axis=0)
    rows = jnp.concatenate([feats, ones] + norms + [spare], axis=0)
    return columns.astype(jnp.bfloat16), rows.astype(jnp.bfloat16)


def pack_kernel(labels, *refs):
    near_refs, packed_ref, rows_ref = refs[:-2], refs[-2], refs[-1]
    for place, near_ref in enumerate(near_refs):
        own = near_ref.shape[1]
        feats = near_ref[pl.ds(labels, 8), :]
        probs = normalize(-near_ref[pl.ds(0, labels), :])
        packed_ref[place] = jnp.concatenate([probs, feats], axis=0).astype(jnp.bfloat16)
        rows_ref[:, pl.ds(place * own, own)] = product_sides(feats)[1]


def over_blocks(refs, body, start):
    base = 0
    unrolled = sum(ref.shape[0] for ref in refs) <= 16
    for ref in refs:
        size = ref.shape[0]
        if unrolled:
            for index in range(size):
                start = body(ref, index, base + index, start)
        else:
            step = lambda index, total, ref=ref, base=base: body(ref, index, base + index, total)
            start = lax.fori_loop(0, size, step, start)
        base += size
    return start


def finish(message, qb, unary, compat_ref):
    message = message - qb.astype(jnp.float32)
    pairwise = jnp.dot(
        compat_ref[...], message, precision=lax.Precision.HIGHEST,
        preferred_element_type=jnp.float32,
    )
    return normalize(-unary - pairwise), pairwise


def first_kernel(labels, nears, *refs):
    rows_ref, compat_ref = refs[:2]
    near_refs = refs[2:2 + nears]
    packed_refs = refs[2 + nears:-3]
    tile_ref, q_ref, columns_ref = refs[-3:]
    own = near_refs[0].shape[1]

    def transpose(packed_ref, index, place, done):
        feats = packed_ref[index][labels:].astype(jnp.float32)
        columns_ref[place] = product_sides(feats)[0].T
        return done

    over_blocks(packed_refs, transpose, 0)
    for near in range(nears):
        rows = rows_ref[:, pl.ds(near * own, own)]

        def body(packed_ref, index, place, total, near=near, rows=rows):
            pieces = []
            for piece in range(own // LANES):
                exponent = jnp.dot(
                    columns_ref[place, pl.ds(piece * LANES, LANES), :], rows,
                    preferred_element_type=jnp.float32,
                )
                pieces.append(jnp.exp(exponent).astype(jnp.bfloat16))
            tile = jnp.concatenate(pieces, axis=0)
            if near == 0:
                tile_ref[place] = tile
            return total + jnp.dot(
                packed_ref[index][:labels], tile, preferred_element_type=jnp.float32
            )

        total = over_blocks(packed_refs, body, jnp.zeros((labels, own), jnp.float32))
        probs, _ = finish(
            total, packed_refs[0][near][:labels], near_refs[near][pl.ds(0, labels), :], compat_ref
        )
        q_ref[near] = probs.astype(jnp.bfloat16)


def second_kernel(near_ref, compat_ref, tile_ref, *refs):
    q_refs = refs[:-2]
    probs_ref, pairwise_ref = refs[-2:]
    unary = near_ref[pl.ds(0, probs_ref.shape[0]), :]

    def body(q_ref, index, place, total):
        return total + jnp.dot(
            q_ref[index], tile_ref[place], preferred_element_type=jnp.float32
        )

    total = over_blocks(q_refs, body, jnp.zeros(unary.shape, jnp.float32))
    probs, pairwise = finish(total, q_refs[0][0], unary, compat_ref)
    probs_ref[...] = probs
    pairwise_ref[...] = pairwise


def swap(value, axis, steps):
    count = lax.axis_size(axis)
    paired = count & (count - 1) == 0
    pairs = [
        (source, source ^ steps if paired else (source + steps) % count)
        for source in range(count)
    ]
    return lax.ppermute(value, axis, pairs)


def group_partners(value):
    return [value] + [swap(value, "grp", steps) for steps in range(1, lax.axis_size("grp"))]


def block_partners(value):
    count = lax.axis_size("blk")
    if count & (count - 1):
        return [value] + [swap(value, "blk", steps) for steps in range(1, count)]
    far = [swap(value, "blk", steps) for steps in range(2, count, 2)]
    held = [value] + far
    return held + [swap(stack, "blk", 1) for stack in held]


def small(dims, kind):
    return math.prod(dims) * jnp.dtype(kind).itemsize <= KEPT_BYTES


def call(kernel, out_shapes, *operands, scratch=()):
    return pl.pallas_call(
        kernel,
        out_shape=tuple(out_shapes),
        scratch_shapes=scratch,
        compiler_params=pltpu.CompilerParams(vmem_limit_bytes=VMEM_LIMIT),
    )(*operands)


def hold(*operands):
    return [
        pltpu.with_memory_space_constraint(operand, pltpu.VMEM)
        if small(operand.shape, operand.dtype) else operand
        for operand in operands
    ]


def kept(dims, kind):
    return pltpu.VMEM(dims, kind) if small(dims, kind) else jax.ShapeDtypeStruct(dims, kind)


def shards(unary, member, features, compat):
    labels, own = unary.shape
    nears = lax.axis_size("grp")
    count = lax.axis_size("blk") * nears
    sent, held = call(
        prepare_kernel,
        [kept((labels + 8, own), jnp.float32), kept(compat.shape, jnp.float32)],
        features, member[None], unary, compat,
    )
    near = group_partners(sent)
    packed, rows = call(
        functools.partial(pack_kernel, labels),
        [kept((nears, labels + 8, own), jnp.bfloat16), kept((AUX, nears * own), jnp.bfloat16)],
        *hold(*near),
    )
    tile, q_near = call(
        functools.partial(first_kernel, labels, nears),
        [kept((count, own, own), jnp.bfloat16), kept((nears, labels, own), jnp.bfloat16)],
        *hold(rows, held, *near, *block_partners(packed)),
        scratch=[pltpu.VMEM((count, own, AUX), jnp.bfloat16)],
    )
    return call(
        second_kernel,
        [jax.ShapeDtypeStruct((labels, own), jnp.float32)] * 2,
        *hold(sent, held, tile, *block_partners(q_near)),
    )


def solution(mesh):
    in_specs = (P(None, ("scene", "blk", "grp")), P(("scene", "blk", "grp")), P(None, "scene"), P())
    out_specs = (P(None, ("scene", "blk", "grp")), P(None, ("scene", "blk", "grp")))
    return jax.shard_map(shards, mesh=mesh, in_specs=in_specs, out_specs=out_specs, check_vma=False)
```

```python
import functools
import math

import jax
import jax.numpy as jnp
from jax import lax
from jax.experimental import pallas as pl
from jax.experimental.pallas import tpu as pltpu
from jax.sharding import PartitionSpec as P

AUX = 16
LANES = 128
VMEM_LIMIT = 56 * 1024 * 1024
KEPT_BYTES = 4 * 1024 * 1024


def normalize(logits):
    raised = jnp.exp(logits)
    return raised / jnp.sum(raised, axis=0, keepdims=True)


def three_parts(value):
    high = value.astype(jnp.bfloat16).astype(jnp.float32)
    middle = (value - high).astype(jnp.bfloat16).astype(jnp.float32)
    return [high, middle, value - high - middle]


def pick_features(features_ref, member):
    feats, points = features_ref.shape
    own = member.shape[1]
    groups = points // LANES
    wide = features_ref[...].astype(jnp.float32)
    wide = jnp.concatenate([wide, jnp.zeros((8 - feats, points), jnp.float32)], axis=0)
    table = jnp.concatenate(
        [wide[:, group * LANES:(group + 1) * LANES] for group in range(groups)], axis=0
    ).astype(jnp.bfloat16)
    lane = lax.broadcasted_iota(jnp.int32, (LANES, own), 0)
    chosen = jnp.where(lane == member % LANES, 1.0, 0.0).astype(jnp.bfloat16)
    found = jnp.dot(table, chosen, preferred_element_type=jnp.float32)
    found = found.reshape(groups, 8, own)
    group = lax.broadcasted_iota(jnp.int32, (groups, 8, own), 0)
    return jnp.sum(jnp.where(group == (member // LANES)[None], found, 0.0), axis=0)


def prepare_kernel(features_ref, member_ref, unary_ref, compat_ref, sent_ref, held_ref):
    labels = unary_ref.shape[0]
    sent_ref[pl.ds(0, labels), :] = unary_ref[...]
    sent_ref[pl.ds(labels, 8), :] = pick_features(features_ref, member_ref[...])
    held_ref[...] = compat_ref[...]


def half_norms(feats):
    return three_parts(-0.5 * jnp.sum(feats * feats, axis=0, keepdims=True))


def product_sides(feats):
    own = feats.shape[1]
    norms = half_norms(feats)
    ones = jnp.ones((3, own), jnp.float32)
    spare = jnp.zeros((AUX - 8 - 6, own), jnp.float32)
    columns = jnp.concatenate([feats] + norms + [ones, spare], axis=0)
    rows = jnp.concatenate([feats, ones] + norms + [spare], axis=0)
    return columns.astype(jnp.bfloat16), rows.astype(jnp.bfloat16)


def pack_kernel(labels, *refs):
    near_refs, packed_ref, rows_ref = refs[:-2], refs[-2], refs[-1]
    for place, near_ref in enumerate(near_refs):
        own = near_ref.shape[1]
        feats = near_ref[pl.ds(labels, 8), :]
        probs = normalize(-near_ref[pl.ds(0, labels), :])
        packed_ref[place] = jnp.concatenate([probs, feats], axis=0).astype(jnp.bfloat16)
        rows_ref[:, pl.ds(place * own, own)] = product_sides(feats)[1]


def over_blocks(count, body, start):
    if count <= 4:
        for index in range(count):
            start = body(index, start)
        return start
    return lax.fori_loop(0, count, body, start)


def finish(message, qb, unary, compat_ref):
    message = message - qb.astype(jnp.float32)
    pairwise = jnp.dot(
        compat_ref[...], message, precision=lax.Precision.HIGHEST,
        preferred_element_type=jnp.float32,
    )
    return normalize(-unary - pairwise), pairwise


def first_part(labels, rows_ref, packed_ref, total, tile_ref):
    blocks, _, own = packed_ref.shape
    packed = jnp.concatenate([packed_ref[index] for index in range(blocks)], axis=1)
    columns = product_sides(packed[labels:].astype(jnp.float32))[0]
    exponent = lax.dot_general(
        columns, rows_ref[...], (((0,), (0,)), ((), ())), preferred_element_type=jnp.float32
    )
    tile = jnp.exp(exponent).astype(jnp.bfloat16)
    for index in range(blocks):
        tile_ref[index] = tile[index * own:(index + 1) * own, :own]
    return total + jnp.dot(packed[:labels], tile, preferred_element_type=jnp.float32)


def first_opening(labels, rows_ref, packed_ref, total_ref, tile_ref):
    start = jnp.zeros(total_ref.shape, jnp.float32)
    total_ref[...] = first_part(labels, rows_ref, packed_ref, start, tile_ref)


def first_middle(labels, rows_ref, packed_ref, sum_ref, total_ref, tile_ref):
    total_ref[...] = first_part(labels, rows_ref, packed_ref, sum_ref[...], tile_ref)


def first_closing(labels, nears, *refs):
    rows_ref, packed_ref, sum_ref, own_ref, compat_ref = refs[:5]
    near_refs, q_ref, tile_ref = refs[5:-2], refs[-2], refs[-1]
    own = own_ref.shape[2]
    total = first_part(labels, rows_ref, packed_ref, sum_ref[...], tile_ref)
    labels_now = [own_ref[near][:labels] for near in range(nears)]
    unary = [near_ref[pl.ds(0, labels), :] for near_ref in near_refs]
    probs, _ = finish(
        total, jnp.concatenate(labels_now, axis=1), jnp.concatenate(unary, axis=1), compat_ref
    )
    for near in range(nears):
        q_ref[near] = probs[:, near * own:(near + 1) * own].astype(jnp.bfloat16)


def second_part(pairs, total):
    for q_ref, tile_ref in pairs:
        body = lambda index, total, q_ref=q_ref, tile_ref=tile_ref: total + jnp.dot(
            q_ref[index], tile_ref[index], preferred_element_type=jnp.float32
        )
        total = over_blocks(q_ref.shape[0], body, total)
    return total


def second_opening(*refs):
    total_ref = refs[-1]
    stacks = len(refs) // 2
    pairs = zip(refs[:stacks], refs[stacks:-1])
    total_ref[...] = second_part(pairs, jnp.zeros(total_ref.shape, jnp.float32))


def second_closing(
    q_ref, tile_ref, sum_ref, own_ref, near_ref, compat_ref, probs_ref, pairwise_ref
):
    total = second_part([(q_ref, tile_ref)], sum_ref[...])
    unary = near_ref[pl.ds(0, total.shape[0]), :]
    probs, pairwise = finish(total, own_ref[0], unary, compat_ref)
    probs_ref[...] = probs
    pairwise_ref[...] = pairwise


def swap(value, axis, steps):
    count = lax.axis_size(axis)
    paired = count & (count - 1) == 0
    pairs = [
        (source, source ^ steps if paired else (source + steps) % count)
        for source in range(count)
    ]
    return lax.ppermute(value, axis, pairs)


def group_partners(value):
    count = lax.axis_size("grp")
    order = sorted(range(1, count), key=lambda steps: (steps != count // 2, -steps))
    return [value] + [swap(value, "grp", steps) for steps in reversed(order)]


def block_partners(value, use_early=None):
    count = lax.axis_size("blk")
    if count & (count - 1):
        stacks = [value] + [swap(value, "blk", steps) for steps in range(1, count)]
        if use_early:
            use_early(stacks[:2])
        return stacks
    far = [swap(value, "blk", steps) for steps in range(2, count, 2)]
    beside = swap(value, "blk", 1)
    if use_early:
        *far, _ = lax.optimization_barrier((*far, use_early([value, beside])))
    return [value, beside] + far + [swap(stack, "blk", 1) for stack in far]


def small(dims, kind):
    return math.prod(dims) * jnp.dtype(kind).itemsize <= KEPT_BYTES


def call(kernel, out_shapes, *operands):
    return pl.pallas_call(
        kernel,
        out_shape=tuple(out_shapes),
        compiler_params=pltpu.CompilerParams(vmem_limit_bytes=VMEM_LIMIT),
    )(*operands)


def hold(*operands):
    return [
        pltpu.with_memory_space_constraint(operand, pltpu.VMEM)
        if small(operand.shape, operand.dtype) else operand
        for operand in operands
    ]


def kept(dims, kind, copies=1):
    if small((copies,) + dims, kind):
        return pltpu.VMEM(dims, kind)
    return jax.ShapeDtypeStruct(dims, kind)


def shards(unary, member, features, compat):
    labels, own = unary.shape
    nears = lax.axis_size("grp")
    count = lax.axis_size("blk") * nears
    sent, held = call(
        prepare_kernel,
        [kept((labels + 8, own), jnp.float32), kept(compat.shape, jnp.float32)],
        features, member[None], unary, compat,
    )
    near = group_partners(sent)
    packed, rows = call(
        functools.partial(pack_kernel, labels),
        [kept((nears, labels + 8, own), jnp.bfloat16), kept((AUX, nears * own), jnp.bfloat16)],
        *hold(*near),
    )
    parts = lax.axis_size("blk")
    tile_kind = kept((nears, own, own), jnp.bfloat16, parts)
    tiles, totals = [], []

    def first(place, last, stack):
        if last:
            q_near, tile = call(
                functools.partial(first_closing, labels, nears),
                [kept((nears, labels, own), jnp.bfloat16), tile_kind],
                *hold(rows, stack, *totals[-1:], packed, held, *near),
            )
            tiles.append(tile)
            return q_near
        total, tile = call(
            functools.partial(first_middle if totals else first_opening, labels),
            [kept((labels, nears * own), jnp.float32), tile_kind],
            *hold(rows, stack, *totals[-1:]),
        )
        tiles.append(tile)
        totals.append(total)
        return total

    def first_early(stacks):
        for place, stack in enumerate(stacks):
            result = first(place, place + 1 == parts, stack)
        return result

    stacks = block_partners(packed, first_early)
    for place in range(2, parts):
        q_near = first(place, place + 1 == parts, stacks[place])

    if parts * math.prod(tile_kind.shape) * 2 <= KEPT_BYTES:
        tiles = hold(*tiles)
    *stacks, last = block_partners(q_near)
    (total,) = call(second_opening, [kept((labels, own), jnp.float32)], *hold(*stacks), *tiles[:-1])
    return call(
        second_closing,
        [jax.ShapeDtypeStruct((labels, own), jnp.float32)] * 2,
        *hold(last), tiles[-1], *hold(total, q_near, sent, held),
    )


def solution(mesh):
    in_specs = (P(None, ("scene", "blk", "grp")), P(("scene", "blk", "grp")), P(None, "scene"), P())
    out_specs = (P(None, ("scene", "blk", "grp")), P(None, ("scene", "blk", "grp")))
    return jax.shard_map(shards, mesh=mesh, in_specs=in_specs, out_specs=out_specs, check_vma=False)
```

```python
import functools
import math

import jax
import jax.numpy as jnp
from jax import lax
from jax.experimental import pallas as pl
from jax.experimental.pallas import tpu as pltpu
from jax.sharding import PartitionSpec as P

AUX = 16
LANES = 128
VMEM_LIMIT = 56 * 1024 * 1024
KEPT_BYTES = 4 * 1024 * 1024


def normalize(logits):
    raised = jnp.exp(logits)
    return raised / jnp.sum(raised, axis=0, keepdims=True)


def three_parts(value):
    high = value.astype(jnp.bfloat16).astype(jnp.float32)
    middle = (value - high).astype(jnp.bfloat16).astype(jnp.float32)
    return [high, middle, value - high - middle]


def pick_features(features_ref, member):
    feats, points = features_ref.shape
    own = member.shape[1]
    groups = points // LANES
    wide = features_ref[...].astype(jnp.float32)
    wide = jnp.concatenate([wide, jnp.zeros((8 - feats, points), jnp.float32)], axis=0)
    table = jnp.concatenate(
        [wide[:, group * LANES:(group + 1) * LANES] for group in range(groups)], axis=0
    ).astype(jnp.bfloat16)
    lane = lax.broadcasted_iota(jnp.int32, (LANES, own), 0)
    chosen = jnp.where(lane == member % LANES, 1.0, 0.0).astype(jnp.bfloat16)
    found = jnp.dot(table, chosen, preferred_element_type=jnp.float32)
    found = found.reshape(groups, 8, own)
    group = lax.broadcasted_iota(jnp.int32, (groups, 8, own), 0)
    return jnp.sum(jnp.where(group == (member // LANES)[None], found, 0.0), axis=0)


def prepare_kernel(features_ref, member_ref, unary_ref, compat_ref, sent_ref, held_ref):
    labels = unary_ref.shape[0]
    sent_ref[pl.ds(0, labels), :] = unary_ref[...]
    sent_ref[pl.ds(labels, 8), :] = pick_features(features_ref, member_ref[...])
    held_ref[...] = compat_ref[...]


def half_norms(feats):
    return three_parts(-0.5 * jnp.sum(feats * feats, axis=0, keepdims=True))


def product_sides(feats):
    own = feats.shape[1]
    norms = half_norms(feats)
    ones = jnp.ones((3, own), jnp.float32)
    spare = jnp.zeros((AUX - 8 - 6, own), jnp.float32)
    columns = jnp.concatenate([feats] + norms + [ones, spare], axis=0)
    rows = jnp.concatenate([feats, ones] + norms + [spare], axis=0)
    return columns.astype(jnp.bfloat16), rows.astype(jnp.bfloat16)


def pack_kernel(labels, *refs):
    near_refs, packed_ref, rows_ref = refs[:-2], refs[-2], refs[-1]
    for place, near_ref in enumerate(near_refs):
        own = near_ref.shape[1]
        feats = near_ref[pl.ds(labels, 8), :]
        probs = normalize(-near_ref[pl.ds(0, labels), :])
        packed_ref[place] = jnp.concatenate([probs, feats], axis=0).astype(jnp.bfloat16)
        rows_ref[:, pl.ds(place * own, own)] = product_sides(feats)[1]


def over_blocks(count, body, start):
    if count <= 4:
        for index in range(count):
            start = body(index, start)
        return start
    return lax.fori_loop(0, count, body, start)


def finish(message, qb, unary, compat_ref):
    message = message - qb.astype(jnp.float32)
    pairwise = jnp.dot(
        compat_ref[...], message, precision=lax.Precision.HIGHEST,
        preferred_element_type=jnp.float32,
    )
    return normalize(-unary - pairwise), pairwise


def first_part(labels, rows_ref, packed_ref, total, tile_ref):
    blocks, _, own = packed_ref.shape
    packed = jnp.concatenate([packed_ref[index] for index in range(blocks)], axis=1)
    columns = product_sides(packed[labels:].astype(jnp.float32))[0]
    exponent = lax.dot_general(
        columns, rows_ref[...], (((0,), (0,)), ((), ())), preferred_element_type=jnp.float32
    )
    tile = jnp.exp(exponent).astype(jnp.bfloat16)
    tile_ref[...] = tile[:own]
    return total + jnp.dot(packed[:labels], tile, preferred_element_type=jnp.float32)


def first_opening(labels, rows_ref, packed_ref, total_ref, tile_ref):
    start = jnp.zeros(total_ref.shape, jnp.float32)
    total_ref[...] = first_part(labels, rows_ref, packed_ref, start, tile_ref)


def first_middle(labels, rows_ref, packed_ref, sum_ref, total_ref, tile_ref):
    total_ref[...] = first_part(labels, rows_ref, packed_ref, sum_ref[...], tile_ref)


def first_closing(labels, nears, *refs):
    rows_ref, packed_ref, sum_ref, own_ref, compat_ref = refs[:5]
    near_refs, q_ref, tile_ref = refs[5:-2], refs[-2], refs[-1]
    own = own_ref.shape[2]
    total = first_part(labels, rows_ref, packed_ref, sum_ref[...], tile_ref)
    labels_now = [own_ref[near][:labels] for near in range(nears)]
    unary = [near_ref[pl.ds(0, labels), :] for near_ref in near_refs]
    probs, _ = finish(
        total, jnp.concatenate(labels_now, axis=1), jnp.concatenate(unary, axis=1), compat_ref
    )
    q_ref[...] = probs.astype(jnp.bfloat16)


def second_parts(q_ref, *refs):
    count = len(refs) // 2
    for tile_ref, part_ref in zip(refs[:count], refs[count:]):
        part_ref[...] = lax.dot_general(
            q_ref[...], tile_ref[...], (((1,), (1,)), ((), ())),
            preferred_element_type=jnp.float32,
        )


def second_closing(q_ref, near_ref, compat_ref, *refs):
    probs_ref, pairwise_ref = refs[-2:]
    labels, own = probs_ref.shape
    total = refs[0][...]
    for part_ref in refs[1:-2]:
        total = total + part_ref[...]
    unary = near_ref[pl.ds(0, labels), :]
    probs, pairwise = finish(total, q_ref[:, pl.ds(0, own)], unary, compat_ref)
    probs_ref[...] = probs
    pairwise_ref[...] = pairwise


def swap(value, axis, steps):
    count = lax.axis_size(axis)
    pairs = [
        (source, source ^ steps if paired(axis) else (source + steps) % count)
        for source in range(count)
    ]
    return lax.ppermute(value, axis, pairs)


def group_partners(value):
    count = lax.axis_size("grp")
    order = sorted(range(1, count), key=lambda steps: (steps != count // 2, -steps))
    return [value] + [swap(value, "grp", steps) for steps in reversed(order)]


def paired(axis):
    count = lax.axis_size(axis)
    return count & (count - 1) == 0


def block_partners(value, use_early):
    count = lax.axis_size("blk")
    if not paired("blk"):
        stacks = [value] + [swap(value, "blk", steps) for steps in range(1, count)]
        use_early(stacks[:2])
        return stacks, list(range(count))
    steps = list(range(2, count, 2))
    far = [swap(value, "blk", step) for step in steps]
    beside = swap(value, "blk", 1)
    *far, _ = lax.optimization_barrier((*far, use_early([value, beside])))
    stacks = [value, beside] + far + [swap(stack, "blk", 1) for stack in far]
    return stacks, [0, 1] + steps + [step + 1 for step in steps]


def send_back(value, steps):
    return swap(value, "blk", steps if paired("blk") else lax.axis_size("blk") - steps)


def small(dims, kind):
    return math.prod(dims) * jnp.dtype(kind).itemsize <= KEPT_BYTES


def call(kernel, out_shapes, *operands):
    return pl.pallas_call(
        kernel,
        out_shape=tuple(out_shapes),
        compiler_params=pltpu.CompilerParams(vmem_limit_bytes=VMEM_LIMIT),
    )(*operands)


def hold(*operands):
    return [
        pltpu.with_memory_space_constraint(operand, pltpu.VMEM)
        if small(operand.shape, operand.dtype) else operand
        for operand in operands
    ]


def kept(dims, kind, copies=1):
    if small((copies,) + dims, kind):
        return pltpu.VMEM(dims, kind)
    return jax.ShapeDtypeStruct(dims, kind)


def shards(unary, member, features, compat):
    labels, own = unary.shape
    nears = lax.axis_size("grp")
    count = lax.axis_size("blk") * nears
    sent, held = call(
        prepare_kernel,
        [kept((labels + 8, own), jnp.float32), kept(compat.shape, jnp.float32)],
        features, member[None], unary, compat,
    )
    near = group_partners(sent)
    packed, rows = call(
        functools.partial(pack_kernel, labels),
        [kept((nears, labels + 8, own), jnp.bfloat16), kept((AUX, nears * own), jnp.bfloat16)],
        *hold(*near),
    )
    parts = lax.axis_size("blk")
    tile_kind = kept((own, nears * own), jnp.bfloat16, parts)
    tiles, totals = [], []

    def first(place, last, stack):
        if last:
            q_near, tile = call(
                functools.partial(first_closing, labels, nears),
                [kept((labels, nears * own), jnp.bfloat16), tile_kind],
                *hold(rows, stack, *totals[-1:], packed, held, *near),
            )
            tiles.append(tile)
            return q_near
        total, tile = call(
            functools.partial(first_middle if totals else first_opening, labels),
            [kept((labels, nears * own), jnp.float32), tile_kind],
            *hold(rows, stack, *totals[-1:]),
        )
        tiles.append(tile)
        totals.append(total)
        return total

    def first_early(stacks):
        for place, stack in enumerate(stacks):
            result = first(place, place + 1 == parts, stack)
        return result

    stacks, steps = block_partners(packed, first_early)
    for place in range(2, parts):
        q_near = first(place, place + 1 == parts, stacks[place])

    if parts * math.prod(tile_kind.shape) * 2 <= KEPT_BYTES:
        tiles = hold(*tiles)
    part_kind = kept((labels, own), jnp.float32)
    far = call(second_parts, [part_kind] * (parts - 2), *hold(q_near), *tiles[2:])
    if far:
        q_near, *far = lax.optimization_barrier((q_near, *far))
    here, beside = call(second_parts, [part_kind] * 2, *hold(q_near), *tiles[:2])
    arrived = [send_back(part, step) for part, step in zip([beside, *far], steps[1:])]
    return call(
        second_closing,
        [jax.ShapeDtypeStruct((labels, own), jnp.float32)] * 2,
        *hold(q_near, sent, held, here, *arrived),
    )


def solution(mesh):
    in_specs = (P(None, ("scene", "blk", "grp")), P(("scene", "blk", "grp")), P(None, "scene"), P())
    out_specs = (P(None, ("scene", "blk", "grp")), P(None, ("scene", "blk", "grp")))
    return jax.shard_map(shards, mesh=mesh, in_specs=in_specs, out_specs=out_specs, check_vma=False)
```

```python
import functools
import math

import jax
import jax.numpy as jnp
from jax import lax
from jax.experimental import pallas as pl
from jax.experimental.pallas import tpu as pltpu
from jax.sharding import PartitionSpec as P

AUX = 16
LANES = 128
VMEM_LIMIT = 56 * 1024 * 1024
KEPT_BYTES = 4 * 1024 * 1024


def normalize(logits):
    raised = jnp.exp(logits)
    return raised / jnp.sum(raised, axis=0, keepdims=True)


def three_parts(value):
    high = value.astype(jnp.bfloat16).astype(jnp.float32)
    middle = (value - high).astype(jnp.bfloat16).astype(jnp.float32)
    return [high, middle, value - high - middle]


def pick_features(features_ref, member):
    feats, points = features_ref.shape
    own = member.shape[1]
    groups = points // LANES
    wide = features_ref[...].astype(jnp.float32)
    wide = jnp.concatenate([wide, jnp.zeros((8 - feats, points), jnp.float32)], axis=0)
    table = jnp.concatenate(
        [wide[:, group * LANES:(group + 1) * LANES] for group in range(groups)], axis=0
    ).astype(jnp.bfloat16)
    lane = lax.broadcasted_iota(jnp.int32, (LANES, own), 0)
    chosen = jnp.where(lane == member % LANES, 1.0, 0.0).astype(jnp.bfloat16)
    found = jnp.dot(table, chosen, preferred_element_type=jnp.float32)
    found = found.reshape(groups, 8, own)
    group = lax.broadcasted_iota(jnp.int32, (groups, 8, own), 0)
    return jnp.sum(jnp.where(group == (member // LANES)[None], found, 0.0), axis=0)


def prepare_kernel(features_ref, member_ref, unary_ref, compat_ref, sent_ref, held_ref):
    labels = unary_ref.shape[0]
    sent_ref[pl.ds(0, labels), :] = unary_ref[...]
    sent_ref[pl.ds(labels, 8), :] = pick_features(features_ref, member_ref[...])
    held_ref[...] = compat_ref[...]


def half_norms(feats):
    return three_parts(-0.5 * jnp.sum(feats * feats, axis=0, keepdims=True))


def product_sides(feats):
    own = feats.shape[1]
    norms = half_norms(feats)
    ones = jnp.ones((3, own), jnp.float32)
    spare = jnp.zeros((AUX - 8 - 6, own), jnp.float32)
    columns = jnp.concatenate([feats] + norms + [ones, spare], axis=0)
    rows = jnp.concatenate([feats, ones] + norms + [spare], axis=0)
    return columns.astype(jnp.bfloat16), rows.astype(jnp.bfloat16)


def pack_kernel(labels, *refs):
    near_refs, packed_ref, rows_ref = refs[:-2], refs[-2], refs[-1]
    for place, near_ref in enumerate(near_refs):
        own = near_ref.shape[1]
        feats = near_ref[pl.ds(labels, 8), :]
        probs = normalize(-near_ref[pl.ds(0, labels), :])
        packed_ref[place] = jnp.concatenate([probs, feats], axis=0).astype(jnp.bfloat16)
        rows_ref[:, pl.ds(place * own, own)] = product_sides(feats)[1]


def over_blocks(count, body, start):
    if count <= 4:
        for index in range(count):
            start = body(index, start)
        return start
    return lax.fori_loop(0, count, body, start)


def finish(message, qb, unary, compat_ref):
    message = message - qb.astype(jnp.float32)
    pairwise = jnp.dot(
        compat_ref[...], message, precision=lax.Precision.HIGHEST,
        preferred_element_type=jnp.float32,
    )
    return normalize(-unary - pairwise), pairwise


def first_part(labels, rows_ref, packed_ref, total, tile_ref):
    blocks, _, own = packed_ref.shape
    rows = rows_ref[...]

    def exponents(index):
        columns = product_sides(packed_ref[index][labels:].astype(jnp.float32))[0]
        return lax.dot_general(
            columns, rows, (((0,), (0,)), ((), ())), preferred_element_type=jnp.float32
        )

    ahead = exponents(0)
    for index in range(blocks):
        exponent = ahead
        if index + 1 < blocks:
            ahead = exponents(index + 1)
        tile = jnp.exp(exponent).astype(jnp.bfloat16)
        if index == 0:
            tile_ref[...] = tile
        total = total + jnp.dot(
            packed_ref[index][:labels], tile, preferred_element_type=jnp.float32
        )
    return total


def first_opening(labels, rows_ref, packed_ref, total_ref, tile_ref):
    start = jnp.zeros(total_ref.shape, jnp.float32)
    total_ref[...] = first_part(labels, rows_ref, packed_ref, start, tile_ref)


def first_middle(labels, rows_ref, packed_ref, sum_ref, total_ref, tile_ref):
    total_ref[...] = first_part(labels, rows_ref, packed_ref, sum_ref[...], tile_ref)


def first_closing(labels, nears, *refs):
    rows_ref, packed_ref, sum_ref, own_ref, compat_ref = refs[:5]
    near_refs, q_ref, tile_ref = refs[5:-2], refs[-2], refs[-1]
    own = own_ref.shape[2]
    total = first_part(labels, rows_ref, packed_ref, sum_ref[...], tile_ref)
    labels_now = [own_ref[near][:labels] for near in range(nears)]
    unary = [near_ref[pl.ds(0, labels), :] for near_ref in near_refs]
    probs, _ = finish(
        total, jnp.concatenate(labels_now, axis=1), jnp.concatenate(unary, axis=1), compat_ref
    )
    q_ref[...] = probs.astype(jnp.bfloat16)


def second_parts(q_ref, *refs):
    count = len(refs) // 2
    for tile_ref, part_ref in zip(refs[:count], refs[count:]):
        part_ref[...] = lax.dot_general(
            q_ref[...], tile_ref[...], (((1,), (1,)), ((), ())),
            preferred_element_type=jnp.float32,
        )


def second_closing(q_ref, near_ref, compat_ref, *refs):
    probs_ref, pairwise_ref = refs[-2:]
    labels, own = probs_ref.shape
    total = refs[0][...]
    for part_ref in refs[1:-2]:
        total = total + part_ref[...]
    unary = near_ref[pl.ds(0, labels), :]
    probs, pairwise = finish(total, q_ref[:, pl.ds(0, own)], unary, compat_ref)
    probs_ref[...] = probs
    pairwise_ref[...] = pairwise


def swap(value, axis, steps):
    count = lax.axis_size(axis)
    pairs = [
        (source, source ^ steps if paired(axis) else (source + steps) % count)
        for source in range(count)
    ]
    return lax.ppermute(value, axis, pairs)


def group_partners(value):
    count = lax.axis_size("grp")
    order = sorted(range(1, count), key=lambda steps: (steps != count // 2, -steps))
    return [value] + [swap(value, "grp", steps) for steps in reversed(order)]


def paired(axis):
    count = lax.axis_size(axis)
    return count & (count - 1) == 0


def block_partners(value, use_early):
    count = lax.axis_size("blk")
    if not paired("blk"):
        stacks = [value] + [swap(value, "blk", steps) for steps in range(1, count)]
        use_early(stacks[:2])
        return stacks, list(range(count))
    steps = list(range(2, count, 2))
    far = [swap(value, "blk", step) for step in steps]
    beside = swap(value, "blk", 1)
    *far, _ = lax.optimization_barrier((*far, use_early([value, beside])))
    stacks = [value, beside] + far + [swap(stack, "blk", 1) for stack in far]
    return stacks, [0, 1] + steps + [step + 1 for step in steps]


def send_back(value, steps):
    return swap(value, "blk", steps if paired("blk") else lax.axis_size("blk") - steps)


def small(dims, kind):
    return math.prod(dims) * jnp.dtype(kind).itemsize <= KEPT_BYTES


def call(kernel, out_shapes, *operands):
    return pl.pallas_call(
        kernel,
        out_shape=tuple(out_shapes),
        compiler_params=pltpu.CompilerParams(vmem_limit_bytes=VMEM_LIMIT),
    )(*operands)


def hold(*operands):
    return [
        pltpu.with_memory_space_constraint(operand, pltpu.VMEM)
        if small(operand.shape, operand.dtype) else operand
        for operand in operands
    ]


def kept(dims, kind, copies=1):
    if small((copies,) + dims, kind):
        return pltpu.VMEM(dims, kind)
    return jax.ShapeDtypeStruct(dims, kind)


def shards(unary, member, features, compat):
    labels, own = unary.shape
    nears = lax.axis_size("grp")
    count = lax.axis_size("blk") * nears
    sent, held = call(
        prepare_kernel,
        [kept((labels + 8, own), jnp.float32), kept(compat.shape, jnp.float32)],
        features, member[None], unary, compat,
    )
    near = group_partners(sent)
    packed, rows = call(
        functools.partial(pack_kernel, labels),
        [kept((nears, labels + 8, own), jnp.bfloat16), kept((AUX, nears * own), jnp.bfloat16)],
        *hold(*near),
    )
    parts = lax.axis_size("blk")
    tile_kind = kept((own, nears * own), jnp.bfloat16, parts)
    tiles, totals = [], []

    def first(place, last, stack):
        if last:
            q_near, tile = call(
                functools.partial(first_closing, labels, nears),
                [kept((labels, nears * own), jnp.bfloat16), tile_kind],
                *hold(rows, stack, *totals[-1:], packed, held, *near),
            )
            tiles.append(tile)
            return q_near
        total, tile = call(
            functools.partial(first_middle if totals else first_opening, labels),
            [kept((labels, nears * own), jnp.float32), tile_kind],
            *hold(rows, stack, *totals[-1:]),
        )
        tiles.append(tile)
        totals.append(total)
        return total

    def first_early(stacks):
        for place, stack in enumerate(stacks):
            result = first(place, place + 1 == parts, stack)
        return result

    stacks, steps = block_partners(packed, first_early)
    for place in range(2, parts):
        q_near = first(place, place + 1 == parts, stacks[place])

    if parts * math.prod(tile_kind.shape) * 2 <= KEPT_BYTES:
        tiles = hold(*tiles)
    part_kind = kept((labels, own), jnp.float32)
    far = call(second_parts, [part_kind] * (parts - 2), *hold(q_near), *tiles[2:])
    if far:
        q_near, *far = lax.optimization_barrier((q_near, *far))
    here, beside = call(second_parts, [part_kind] * 2, *hold(q_near), *tiles[:2])
    arrived = [send_back(part, step) for part, step in zip([beside, *far], steps[1:])]
    return call(
        second_closing,
        [jax.ShapeDtypeStruct((labels, own), jnp.float32)] * 2,
        *hold(q_near, sent, held, here, *arrived),
    )


def solution(mesh):
    in_specs = (P(None, ("scene", "blk", "grp")), P(("scene", "blk", "grp")), P(None, "scene"), P())
    out_specs = (P(None, ("scene", "blk", "grp")), P(None, ("scene", "blk", "grp")))
    return jax.shard_map(shards, mesh=mesh, in_specs=in_specs, out_specs=out_specs, check_vma=False)
```

```python
import functools
import math

import jax
import jax.numpy as jnp
from jax import lax
from jax.experimental import pallas as pl
from jax.experimental.pallas import tpu as pltpu
from jax.sharding import PartitionSpec as P

AUX = 16
LANES = 128
VMEM_LIMIT = 56 * 1024 * 1024
KEPT_BYTES = 4 * 1024 * 1024
SCHEDULE_COST = 10 ** 10


def normalize(logits):
    raised = jnp.exp(logits)
    return raised / jnp.sum(raised, axis=0, keepdims=True)


def three_parts(value):
    high = value.astype(jnp.bfloat16).astype(jnp.float32)
    middle = (value - high).astype(jnp.bfloat16).astype(jnp.float32)
    return [high, middle, value - high - middle]


def pick_features(features_ref, member):
    feats, points = features_ref.shape
    own = member.shape[1]
    groups = points // LANES
    wide = features_ref[...].astype(jnp.float32)
    wide = jnp.concatenate([wide, jnp.zeros((8 - feats, points), jnp.float32)], axis=0)
    table = jnp.concatenate(
        [wide[:, group * LANES:(group + 1) * LANES] for group in range(groups)], axis=0
    ).astype(jnp.bfloat16)
    lane = lax.broadcasted_iota(jnp.int32, (LANES, own), 0)
    chosen = jnp.where(lane == member % LANES, 1.0, 0.0).astype(jnp.bfloat16)
    found = jnp.dot(table, chosen, preferred_element_type=jnp.float32)
    found = found.reshape(groups, 8, own)
    group = lax.broadcasted_iota(jnp.int32, (groups, 8, own), 0)
    return jnp.sum(jnp.where(group == (member // LANES)[None], found, 0.0), axis=0)


def prepare_kernel(features_ref, member_ref, unary_ref, compat_ref, sent_ref, held_ref):
    labels = unary_ref.shape[0]
    sent_ref[pl.ds(0, labels), :] = unary_ref[...]
    sent_ref[pl.ds(labels, 8), :] = pick_features(features_ref, member_ref[...])
    held_ref[...] = compat_ref[...]


def half_norms(feats):
    return three_parts(-0.5 * jnp.sum(feats * feats, axis=0, keepdims=True))


def product_sides(feats):
    own = feats.shape[1]
    norms = half_norms(feats)
    ones = jnp.ones((3, own), jnp.float32)
    spare = jnp.zeros((AUX - 8 - 6, own), jnp.float32)
    columns = jnp.concatenate([feats] + norms + [ones, spare], axis=0)
    rows = jnp.concatenate([feats, ones] + norms + [spare], axis=0)
    return columns.astype(jnp.bfloat16), rows.astype(jnp.bfloat16)


def pack_kernel(labels, *refs):
    near_refs, packed_ref, rows_ref = refs[:-2], refs[-2], refs[-1]
    for place, near_ref in enumerate(near_refs):
        own = near_ref.shape[1]
        feats = near_ref[pl.ds(labels, 8), :]
        probs = normalize(-near_ref[pl.ds(0, labels), :])
        packed_ref[place] = jnp.concatenate([probs, feats], axis=0).astype(jnp.bfloat16)
        rows_ref[:, pl.ds(place * own, own)] = product_sides(feats)[1]


def over_blocks(count, body, start):
    if count <= 4:
        for index in range(count):
            start = body(index, start)
        return start
    return lax.fori_loop(0, count, body, start)


def finish(message, qb, unary, compat_ref):
    message = message - qb.astype(jnp.float32)
    pairwise = jnp.dot(
        compat_ref[...], message, precision=lax.Precision.HIGHEST,
        preferred_element_type=jnp.float32,
    )
    return normalize(-unary - pairwise), pairwise


def first_part(labels, rows_ref, packed_ref, total, tile_ref=None, begin=0, end=None):
    blocks = range(begin, packed_ref.shape[0] if end is None else end)
    rows = rows_ref[...]

    def exponents(index):
        columns = product_sides(packed_ref[index][labels:].astype(jnp.float32))[0]
        return lax.dot_general(
            columns, rows, (((0,), (0,)), ((), ())), preferred_element_type=jnp.float32
        )

    ahead = exponents(begin)
    for index in blocks:
        exponent = ahead
        if index + 1 < blocks.stop:
            ahead = exponents(index + 1)
        tile = jnp.exp(exponent).astype(jnp.bfloat16)
        if index == 0 and tile_ref is not None:
            tile_ref[...] = tile
        total = total + jnp.dot(
            packed_ref[index][:labels], tile, preferred_element_type=jnp.float32
        )
    return total


def first_opening(labels, rows_ref, packed_ref, total_ref, tile_ref):
    start = jnp.zeros(total_ref.shape, jnp.float32)
    total_ref[...] = first_part(labels, rows_ref, packed_ref, start, tile_ref, end=1)


def first_rest(labels, rows_ref, packed_ref, sum_ref, total_ref):
    total_ref[...] = first_part(labels, rows_ref, packed_ref, sum_ref[...], begin=1)


def first_middle(labels, rows_ref, packed_ref, sum_ref, total_ref, tile_ref):
    total_ref[...] = first_part(labels, rows_ref, packed_ref, sum_ref[...], tile_ref)


def first_closing(labels, nears, *refs):
    rows_ref, packed_ref, sum_ref, own_ref, compat_ref = refs[:5]
    near_refs, q_ref, tile_ref = refs[5:-2], refs[-2], refs[-1]
    own = own_ref.shape[2]
    total = first_part(labels, rows_ref, packed_ref, sum_ref[...], tile_ref)
    labels_now = [own_ref[near][:labels] for near in range(nears)]
    unary = [near_ref[pl.ds(0, labels), :] for near_ref in near_refs]
    probs, _ = finish(
        total, jnp.concatenate(labels_now, axis=1), jnp.concatenate(unary, axis=1), compat_ref
    )
    q_ref[...] = probs.astype(jnp.bfloat16)


def second_parts(q_ref, *refs):
    count = len(refs) // 2
    for tile_ref, part_ref in zip(refs[:count], refs[count:]):
        part_ref[...] = lax.dot_general(
            q_ref[...], tile_ref[...], (((1,), (1,)), ((), ())),
            preferred_element_type=jnp.float32,
        )


def second_closing(q_ref, near_ref, compat_ref, *refs):
    probs_ref, pairwise_ref = refs[-2:]
    labels, own = probs_ref.shape
    total = refs[0][...]
    for part_ref in refs[1:-2]:
        total = total + part_ref[...]
    unary = near_ref[pl.ds(0, labels), :]
    probs, pairwise = finish(total, q_ref[:, pl.ds(0, own)], unary, compat_ref)
    probs_ref[...] = probs
    pairwise_ref[...] = pairwise


def swap(value, axis, steps):
    count = lax.axis_size(axis)
    pairs = [
        (source, source ^ steps if paired(axis) else (source + steps) % count)
        for source in range(count)
    ]
    return lax.ppermute(value, axis, pairs)


def group_partners(value):
    count = lax.axis_size("grp")
    order = sorted(range(1, count), key=lambda steps: (steps != count // 2, -steps))
    return [value] + [swap(value, "grp", steps) for steps in reversed(order)]


def paired(axis):
    count = lax.axis_size(axis)
    return count & (count - 1) == 0


def block_partners(value, use_own, use_beside):
    count = lax.axis_size("blk")
    if not paired("blk"):
        stacks = [value] + [swap(value, "blk", steps) for steps in range(1, count)]
        use_own(value)
        use_beside(stacks[1])
        return stacks, list(range(count))
    steps = list(range(2, count, 2))
    far = [swap(value, "blk", step) for step in steps]
    sent, _ = lax.optimization_barrier((value, use_own(value)))
    beside = swap(sent, "blk", 1)
    *far, _ = lax.optimization_barrier((*far, use_beside(beside)))
    stacks = [value, beside] + far + [swap(stack, "blk", 1) for stack in far]
    return stacks, [0, 1] + steps + [step + 1 for step in steps]


def send_back(value, steps):
    return swap(value, "blk", steps if paired("blk") else lax.axis_size("blk") - steps)


def small(dims, kind):
    return math.prod(dims) * jnp.dtype(kind).itemsize <= KEPT_BYTES


def call(kernel, out_shapes, *operands):
    return pl.pallas_call(
        kernel,
        out_shape=tuple(out_shapes),
        cost_estimate=pl.CostEstimate(flops=SCHEDULE_COST, transcendentals=0, bytes_accessed=SCHEDULE_COST),
        compiler_params=pltpu.CompilerParams(vmem_limit_bytes=VMEM_LIMIT),
    )(*operands)


def hold(*operands):
    return [
        pltpu.with_memory_space_constraint(operand, pltpu.VMEM)
        if small(operand.shape, operand.dtype) else operand
        for operand in operands
    ]


def kept(dims, kind, copies=1):
    if small((copies,) + dims, kind):
        return pltpu.VMEM(dims, kind)
    return jax.ShapeDtypeStruct(dims, kind)


def shards(unary, member, features, compat):
    labels, own = unary.shape
    nears = lax.axis_size("grp")
    count = lax.axis_size("blk") * nears
    sent, held = call(
        prepare_kernel,
        [kept((labels + 8, own), jnp.float32), kept(compat.shape, jnp.float32)],
        features, member[None], unary, compat,
    )
    near = group_partners(sent)
    packed, rows = call(
        functools.partial(pack_kernel, labels),
        [kept((nears, labels + 8, own), jnp.bfloat16), kept((AUX, nears * own), jnp.bfloat16)],
        *hold(*near),
    )
    parts = lax.axis_size("blk")
    tile_kind = kept((own, nears * own), jnp.bfloat16, parts)
    tiles, totals = [], []

    total_kind = kept((labels, nears * own), jnp.float32)

    def first_own(stack):
        opened, tile = call(
            functools.partial(first_opening, labels), [total_kind, tile_kind], *hold(rows, stack)
        )
        (total,) = call(
            functools.partial(first_rest, labels), [total_kind], *hold(rows, stack, opened)
        )
        tiles.append(tile)
        totals.append(total)
        return opened

    def first(stack):
        total, tile = call(
            functools.partial(first_middle, labels), [total_kind, tile_kind],
            *hold(rows, stack, totals[-1]),
        )
        tiles.append(tile)
        totals.append(total)
        return total

    stacks, steps = block_partners(packed, first_own, first)
    for stack in stacks[2:-1]:
        first(stack)
    q_near, tile = call(
        functools.partial(first_closing, labels, nears),
        [kept((labels, nears * own), jnp.bfloat16), tile_kind],
        *hold(rows, stacks[-1], totals[-1], packed, held, *near),
    )
    tiles.append(tile)

    if parts * math.prod(tile_kind.shape) * 2 <= KEPT_BYTES:
        tiles = hold(*tiles)
    part_kind = kept((labels, own), jnp.float32)
    far = call(second_parts, [part_kind] * (parts - 2), *hold(q_near), *tiles[2:])
    if far:
        q_near, *far = lax.optimization_barrier((q_near, *far))
    here, beside = call(second_parts, [part_kind] * 2, *hold(q_near), *tiles[:2])
    arrived = [send_back(part, step) for part, step in zip([beside, *far], steps[1:])]
    return call(
        second_closing,
        [jax.ShapeDtypeStruct((labels, own), jnp.float32)] * 2,
        *hold(q_near, sent, held, here, *arrived),
    )


def solution(mesh):
    in_specs = (P(None, ("scene", "blk", "grp")), P(("scene", "blk", "grp")), P(None, "scene"), P())
    out_specs = (P(None, ("scene", "blk", "grp")), P(None, ("scene", "blk", "grp")))
    return jax.shard_map(shards, mesh=mesh, in_specs=in_specs, out_specs=out_specs, check_vma=False)
```

```python
import functools
import math

import jax
import jax.numpy as jnp
from jax import lax
from jax.experimental import pallas as pl
from jax.experimental.pallas import tpu as pltpu
from jax.sharding import PartitionSpec as P

AUX = 16
LANES = 128
VMEM_LIMIT = 56 * 1024 * 1024
KEPT_BYTES = 4 * 1024 * 1024
SCHEDULE_COST = 10 ** 10


def normalize(logits):
    raised = jnp.exp(logits)
    return raised / jnp.sum(raised, axis=0, keepdims=True)


def three_parts(value):
    high = value.astype(jnp.bfloat16).astype(jnp.float32)
    middle = (value - high).astype(jnp.bfloat16).astype(jnp.float32)
    return [high, middle, value - high - middle]


def pick_features(features_ref, member):
    feats, points = features_ref.shape
    own = member.shape[1]
    groups = points // LANES
    wide = features_ref[...].astype(jnp.float32)
    wide = jnp.concatenate([wide, jnp.zeros((8 - feats, points), jnp.float32)], axis=0)
    table = jnp.concatenate(
        [wide[:, group * LANES:(group + 1) * LANES] for group in range(groups)], axis=0
    ).astype(jnp.bfloat16)
    lane = lax.broadcasted_iota(jnp.int32, (LANES, own), 0)
    chosen = jnp.where(lane == member % LANES, 1.0, 0.0).astype(jnp.bfloat16)
    found = jnp.dot(table, chosen, preferred_element_type=jnp.float32)
    found = found.reshape(groups, 8, own)
    group = lax.broadcasted_iota(jnp.int32, (groups, 8, own), 0)
    return jnp.sum(jnp.where(group == (member // LANES)[None], found, 0.0), axis=0)


def prepare_kernel(
    features_ref, member_ref, unary_ref, compat_ref, sent_ref, held_unary_ref, held_compat_ref
):
    unary = unary_ref[...]
    high, low, _ = three_parts(unary)
    feats = pick_features(features_ref, member_ref[...])
    sent_ref[...] = jnp.concatenate([high, low, feats], axis=0).astype(jnp.bfloat16)
    held_unary_ref[...] = unary
    held_compat_ref[...] = compat_ref[...]


def half_norms(feats):
    return three_parts(-0.5 * jnp.sum(feats * feats, axis=0, keepdims=True))


def product_sides(feats):
    own = feats.shape[1]
    norms = half_norms(feats)
    ones = jnp.ones((3, own), jnp.float32)
    spare = jnp.zeros((AUX - 8 - 6, own), jnp.float32)
    columns = jnp.concatenate([feats] + norms + [ones, spare], axis=0)
    rows = jnp.concatenate([feats, ones] + norms + [spare], axis=0)
    return columns.astype(jnp.bfloat16), rows.astype(jnp.bfloat16)


def pack_kernel(labels, *refs):
    near_refs, packed_ref, rows_ref, unary_ref = refs[:-3], refs[-3], refs[-2], refs[-1]
    for place, near_ref in enumerate(near_refs):
        own = near_ref.shape[1]
        near = near_ref[...].astype(jnp.float32)
        unary = near[:labels] + near[labels:2 * labels]
        feats = near[2 * labels:]
        packed = jnp.concatenate([normalize(-unary), feats], axis=0)
        packed_ref[place] = packed.astype(jnp.bfloat16)
        rows_ref[:, pl.ds(place * own, own)] = product_sides(feats)[1]
        unary_ref[:, pl.ds(place * own, own)] = unary


def finish(message, qb, unary, compat_ref):
    message = message - qb.astype(jnp.float32)
    pairwise = jnp.dot(
        compat_ref[...], message, precision=lax.Precision.HIGHEST,
        preferred_element_type=jnp.float32,
    )
    return normalize(-unary - pairwise), pairwise


def first_part(labels, rows_ref, packed_ref, total, tile_ref=None, begin=0, end=None):
    blocks = range(begin, packed_ref.shape[0] if end is None else end)
    rows = rows_ref[...]

    def exponents(index):
        columns = product_sides(packed_ref[index][labels:].astype(jnp.float32))[0]
        return lax.dot_general(
            columns, rows, (((0,), (0,)), ((), ())), preferred_element_type=jnp.float32
        )

    ahead = exponents(begin)
    for index in blocks:
        exponent = ahead
        if index + 1 < blocks.stop:
            ahead = exponents(index + 1)
        tile = jnp.exp(exponent).astype(jnp.bfloat16)
        if index == 0 and tile_ref is not None:
            tile_ref[...] = tile
        total = total + jnp.dot(
            packed_ref[index][:labels], tile, preferred_element_type=jnp.float32
        )
    return total


def first_opening(labels, rows_ref, packed_ref, total_ref, tile_ref):
    start = jnp.zeros(total_ref.shape, jnp.float32)
    total_ref[...] = first_part(labels, rows_ref, packed_ref, start, tile_ref, end=1)


def first_rest(labels, rows_ref, packed_ref, sum_ref, total_ref):
    total_ref[...] = first_part(labels, rows_ref, packed_ref, sum_ref[...], begin=1)


def first_middle(labels, rows_ref, packed_ref, sum_ref, total_ref, tile_ref):
    total_ref[...] = first_part(labels, rows_ref, packed_ref, sum_ref[...], tile_ref)


def first_closing(
    labels, rows_ref, packed_ref, sum_ref, own_ref, compat_ref, unary_ref, q_ref, tile_ref
):
    total = first_part(labels, rows_ref, packed_ref, sum_ref[...], tile_ref)
    labels_now = [own_ref[near][:labels] for near in range(own_ref.shape[0])]
    probs, _ = finish(
        total, jnp.concatenate(labels_now, axis=1), unary_ref[...], compat_ref
    )
    q_ref[...] = probs.astype(jnp.bfloat16)


def second_parts(q_ref, *refs):
    count = len(refs) // 2
    for tile_ref, part_ref in zip(refs[:count], refs[count:]):
        part_ref[...] = lax.dot_general(
            q_ref[...], tile_ref[...], (((1,), (1,)), ((), ())),
            preferred_element_type=jnp.float32,
        )


def second_closing(q_ref, unary_ref, compat_ref, *refs):
    probs_ref, pairwise_ref = refs[-2:]
    labels, own = probs_ref.shape
    total = refs[0][...]
    for part_ref in refs[1:-2]:
        total = total + part_ref[...]
    probs, pairwise = finish(total, q_ref[:, pl.ds(0, own)], unary_ref[...], compat_ref)
    probs_ref[...] = probs
    pairwise_ref[...] = pairwise


def swap(value, axis, steps):
    count = lax.axis_size(axis)
    pairs = [
        (source, source ^ steps if paired(axis) else (source + steps) % count)
        for source in range(count)
    ]
    return lax.ppermute(value, axis, pairs)


def group_partners(value):
    count = lax.axis_size("grp")
    order = sorted(range(1, count), key=lambda steps: (steps != count // 2, -steps))
    return [value] + [swap(value, "grp", steps) for steps in reversed(order)]


def paired(axis):
    count = lax.axis_size(axis)
    return count & (count - 1) == 0


def block_partners(value, use_own, use_beside):
    count = lax.axis_size("blk")
    if not paired("blk"):
        stacks = [value] + [swap(value, "blk", steps) for steps in range(1, count)]
        use_own(value)
        use_beside(stacks[1])
        return stacks, list(range(count))
    steps = list(range(2, count, 2))
    far = [swap(value, "blk", step) for step in steps]
    sent, _ = lax.optimization_barrier((value, use_own(value)))
    beside = swap(sent, "blk", 1)
    *far, _ = lax.optimization_barrier((*far, use_beside(beside)))
    stacks = [value, beside] + far + [swap(stack, "blk", 1) for stack in far]
    return stacks, [0, 1] + steps + [step + 1 for step in steps]


def send_back(value, steps):
    return swap(value, "blk", steps if paired("blk") else lax.axis_size("blk") - steps)


def small(dims, kind):
    return math.prod(dims) * jnp.dtype(kind).itemsize <= KEPT_BYTES


def call(kernel, out_shapes, *operands):
    return pl.pallas_call(
        kernel,
        out_shape=tuple(out_shapes),
        cost_estimate=pl.CostEstimate(flops=SCHEDULE_COST, transcendentals=0, bytes_accessed=SCHEDULE_COST),
        compiler_params=pltpu.CompilerParams(vmem_limit_bytes=VMEM_LIMIT),
    )(*operands)


def hold(*operands):
    return [
        pltpu.with_memory_space_constraint(operand, pltpu.VMEM)
        if small(operand.shape, operand.dtype) else operand
        for operand in operands
    ]


def kept(dims, kind, copies=1):
    if small((copies,) + dims, kind):
        return pltpu.VMEM(dims, kind)
    return jax.ShapeDtypeStruct(dims, kind)


def shards(unary, member, features, compat):
    labels, own = unary.shape
    nears = lax.axis_size("grp")
    count = lax.axis_size("blk") * nears
    sent, held_unary, held_compat = call(
        prepare_kernel,
        [
            kept((2 * labels + 8, own), jnp.bfloat16),
            kept(unary.shape, jnp.float32),
            kept(compat.shape, jnp.float32),
        ],
        features, member[None], unary, compat,
    )
    packed, rows, near_unary = call(
        functools.partial(pack_kernel, labels),
        [
            kept((nears, labels + 8, own), jnp.bfloat16),
            kept((AUX, nears * own), jnp.bfloat16),
            kept((labels, nears * own), jnp.float32),
        ],
        *hold(*group_partners(sent)),
    )
    parts = lax.axis_size("blk")
    tile_kind = kept((own, nears * own), jnp.bfloat16, parts)
    tiles, totals = [], []

    total_kind = kept((labels, nears * own), jnp.float32)

    def first_own(stack):
        opened, tile = call(
            functools.partial(first_opening, labels), [total_kind, tile_kind], *hold(rows, stack)
        )
        (total,) = call(
            functools.partial(first_rest, labels), [total_kind], *hold(rows, stack, opened)
        )
        tiles.append(tile)
        totals.append(total)
        return opened

    def first(stack):
        total, tile = call(
            functools.partial(first_middle, labels), [total_kind, tile_kind],
            *hold(rows, stack, totals[-1]),
        )
        tiles.append(tile)
        totals.append(total)
        return total

    stacks, steps = block_partners(packed, first_own, first)
    for stack in stacks[2:-1]:
        first(stack)
    q_near, tile = call(
        functools.partial(first_closing, labels),
        [kept((labels, nears * own), jnp.bfloat16), tile_kind],
        *hold(rows, stacks[-1], totals[-1], packed, held_compat, near_unary),
    )
    tiles.append(tile)

    if parts * math.prod(tile_kind.shape) * 2 <= KEPT_BYTES:
        tiles = hold(*tiles)
    part_kind = kept((labels, own), jnp.float32)
    far = call(second_parts, [part_kind] * (parts - 2), *hold(q_near), *tiles[2:])
    if far:
        q_near, *far = lax.optimization_barrier((q_near, *far))
    here, beside = call(second_parts, [part_kind] * 2, *hold(q_near), *tiles[:2])
    arrived = [send_back(part, step) for part, step in zip([beside, *far], steps[1:])]
    return call(
        second_closing,
        [jax.ShapeDtypeStruct((labels, own), jnp.float32)] * 2,
        *hold(q_near, held_unary, held_compat, here, *arrived),
    )


def solution(mesh):
    in_specs = (P(None, ("scene", "blk", "grp")), P(("scene", "blk", "grp")), P(None, "scene"), P())
    out_specs = (P(None, ("scene", "blk", "grp")), P(None, ("scene", "blk", "grp")))
    return jax.shard_map(shards, mesh=mesh, in_specs=in_specs, out_specs=out_specs, check_vma=False)
```

```python
import functools
import math

import jax
import jax.numpy as jnp
from jax import lax
from jax.experimental import pallas as pl
from jax.experimental.pallas import tpu as pltpu
from jax.sharding import PartitionSpec as P

AUX = 16
LANES = 128
VMEM_LIMIT = 56 * 1024 * 1024
KEPT_BYTES = 4 * 1024 * 1024
HIDING_COST = 10 ** 10


def normalize(logits):
    raised = jnp.exp(logits)
    return raised / jnp.sum(raised, axis=0, keepdims=True)


def three_parts(value):
    high = value.astype(jnp.bfloat16).astype(jnp.float32)
    middle = (value - high).astype(jnp.bfloat16).astype(jnp.float32)
    return [high, middle, value - high - middle]


def pick_features(features_ref, member):
    feats, points = features_ref.shape
    own = member.shape[1]
    groups = points // LANES
    wide = features_ref[...].astype(jnp.float32)
    wide = jnp.concatenate([wide, jnp.zeros((8 - feats, points), jnp.float32)], axis=0)
    table = jnp.concatenate(
        [wide[:, group * LANES:(group + 1) * LANES] for group in range(groups)], axis=0
    ).astype(jnp.bfloat16)
    lane = lax.broadcasted_iota(jnp.int32, (LANES, own), 0)
    chosen = jnp.where(lane == member % LANES, 1.0, 0.0).astype(jnp.bfloat16)
    found = jnp.dot(table, chosen, preferred_element_type=jnp.float32)
    found = found.reshape(groups, 8, own)
    group = lax.broadcasted_iota(jnp.int32, (groups, 8, own), 0)
    return jnp.sum(jnp.where(group == (member // LANES)[None], found, 0.0), axis=0)


def prepare_kernel(features_ref, member_ref, unary_ref, compat_ref, sent_ref, held_ref):
    labels = unary_ref.shape[0]
    sent_ref[pl.ds(0, labels), :] = unary_ref[...]
    sent_ref[pl.ds(labels, 8), :] = pick_features(features_ref, member_ref[...])
    held_ref[...] = compat_ref[...]


def half_norms(feats):
    return three_parts(-0.5 * jnp.sum(feats * feats, axis=0, keepdims=True))


def product_sides(feats):
    own = feats.shape[1]
    norms = half_norms(feats)
    ones = jnp.ones((3, own), jnp.float32)
    spare = jnp.zeros((AUX - 8 - 6, own), jnp.float32)
    columns = jnp.concatenate([feats] + norms + [ones, spare], axis=0)
    rows = jnp.concatenate([feats, ones] + norms + [spare], axis=0)
    return columns.astype(jnp.bfloat16), rows


def pack_kernel(labels, *refs):
    near_refs, packed_ref, rows_ref = refs[:-2], refs[-2], refs[-1]
    for place, near_ref in enumerate(near_refs):
        own = near_ref.shape[1]
        feats = near_ref[pl.ds(labels, 8), :]
        probs = normalize(-near_ref[pl.ds(0, labels), :])
        packed_ref[place] = jnp.concatenate([probs, feats], axis=0).astype(jnp.bfloat16)
        rows_ref[pl.ds(place * own, own), :] = product_sides(feats)[1].T.astype(jnp.bfloat16)


def over_blocks(count, body, start):
    if count <= 4:
        for index in range(count):
            start = body(index, start)
        return start
    return lax.fori_loop(0, count, body, start)


def finish(message, qb, unary, compat_ref):
    message = message - qb.astype(jnp.float32)
    pairwise = jnp.dot(
        compat_ref[...], message, precision=lax.Precision.HIGHEST,
        preferred_element_type=jnp.float32,
    )
    return normalize(-unary - pairwise), pairwise


def first_part(labels, rows_ref, packed_ref, total, tile_ref=None, begin=0, end=None):
    blocks = range(begin, packed_ref.shape[0] if end is None else end)
    packed = jnp.concatenate([packed_ref[index] for index in blocks], axis=1)
    columns = product_sides(packed[labels:].astype(jnp.float32))[0]
    exponent = jnp.dot(rows_ref[...], columns, preferred_element_type=jnp.float32)
    tile = jnp.exp(exponent).astype(jnp.bfloat16)
    if tile_ref is not None:
        tile_ref[...] = tile[:, :packed_ref.shape[2]]
    return total + lax.dot_general(
        tile, packed[:labels], (((1,), (1,)), ((), ())), preferred_element_type=jnp.float32
    )


def first_opening(labels, rows_ref, packed_ref, total_ref, tile_ref):
    start = jnp.zeros(total_ref.shape, jnp.float32)
    total_ref[...] = first_part(labels, rows_ref, packed_ref, start, tile_ref, end=1)


def first_rest(labels, rows_ref, packed_ref, sum_ref, total_ref):
    total_ref[...] = first_part(labels, rows_ref, packed_ref, sum_ref[...], begin=1)


def first_middle(labels, rows_ref, packed_ref, sum_ref, total_ref, tile_ref):
    total_ref[...] = first_part(labels, rows_ref, packed_ref, sum_ref[...], tile_ref)


def first_closing(labels, nears, *refs):
    rows_ref, packed_ref, sum_ref, own_ref, compat_ref = refs[:5]
    near_refs, q_ref, tile_ref = refs[5:-2], refs[-2], refs[-1]
    own = own_ref.shape[2]
    total = first_part(labels, rows_ref, packed_ref, sum_ref[...], tile_ref).T
    labels_now = [own_ref[near][:labels] for near in range(nears)]
    unary = [near_ref[pl.ds(0, labels), :] for near_ref in near_refs]
    probs, _ = finish(
        total, jnp.concatenate(labels_now, axis=1), jnp.concatenate(unary, axis=1), compat_ref
    )
    q_ref[...] = probs.astype(jnp.bfloat16)


def second_parts(q_ref, *refs):
    count = len(refs) // 2
    for tile_ref, part_ref in zip(refs[:count], refs[count:]):
        part_ref[...] = jnp.dot(q_ref[...], tile_ref[...], preferred_element_type=jnp.float32)


def second_closing(q_ref, near_ref, compat_ref, *refs):
    probs_ref, pairwise_ref = refs[-2:]
    labels, own = probs_ref.shape
    total = refs[0][...]
    for part_ref in refs[1:-2]:
        total = total + part_ref[...]
    unary = near_ref[pl.ds(0, labels), :]
    probs, pairwise = finish(total, q_ref[:, pl.ds(0, own)], unary, compat_ref)
    probs_ref[...] = probs
    pairwise_ref[...] = pairwise


def swap(value, axis, steps):
    count = lax.axis_size(axis)
    pairs = [
        (source, source ^ steps if paired(axis) else (source + steps) % count)
        for source in range(count)
    ]
    return lax.ppermute(value, axis, pairs)


def group_partners(value):
    count = lax.axis_size("grp")
    order = sorted(range(1, count), key=lambda steps: (steps != count // 2, -steps))
    return [value] + [swap(value, "grp", steps) for steps in reversed(order)]


def paired(axis):
    count = lax.axis_size(axis)
    return count & (count - 1) == 0


def block_partners(value, use_own, use_beside):
    count = lax.axis_size("blk")
    if not paired("blk"):
        stacks = [value] + [swap(value, "blk", steps) for steps in range(1, count)]
        use_own(value)
        use_beside(stacks[1])
        return stacks, list(range(count))
    steps = list(range(2, count, 2))
    far = [swap(value, "blk", step) for step in steps]
    sent, _ = lax.optimization_barrier((value, use_own(value)))
    beside = swap(sent, "blk", 1)
    *far, _ = lax.optimization_barrier((*far, use_beside(beside)))
    stacks = [value, beside] + far + [swap(stack, "blk", 1) for stack in far]
    return stacks, [0, 1] + steps + [step + 1 for step in steps]


def send_back(value, steps):
    return swap(value, "blk", steps if paired("blk") else lax.axis_size("blk") - steps)


def small(dims, kind):
    return math.prod(dims) * jnp.dtype(kind).itemsize <= KEPT_BYTES


def call(kernel, out_shapes, *operands, cost=1):
    return pl.pallas_call(
        kernel,
        out_shape=tuple(out_shapes),
        cost_estimate=pl.CostEstimate(flops=cost, transcendentals=0, bytes_accessed=cost),
        compiler_params=pltpu.CompilerParams(vmem_limit_bytes=VMEM_LIMIT),
    )(*operands)


def hold(*operands):
    return [
        pltpu.with_memory_space_constraint(operand, pltpu.VMEM)
        if small(operand.shape, operand.dtype) else operand
        for operand in operands
    ]


def kept(dims, kind, copies=1):
    if small((copies,) + dims, kind):
        return pltpu.VMEM(dims, kind)
    return jax.ShapeDtypeStruct(dims, kind)


def shards(unary, member, features, compat):
    labels, own = unary.shape
    nears = lax.axis_size("grp")
    count = lax.axis_size("blk") * nears
    sent, held = call(
        prepare_kernel,
        [kept((labels + 8, own), jnp.float32), kept(compat.shape, jnp.float32)],
        features, member[None], unary, compat,
    )
    near = group_partners(sent)
    packed, rows = call(
        functools.partial(pack_kernel, labels),
        [kept((nears, labels + 8, own), jnp.bfloat16), kept((nears * own, AUX), jnp.bfloat16)],
        *hold(*near),
    )
    parts = lax.axis_size("blk")
    tile_kind = kept((nears * own, own), jnp.bfloat16, parts)
    tiles, totals = [], []

    total_kind = kept((nears * own, labels), jnp.float32)

    def first_own(stack):
        opened, tile = call(
            functools.partial(first_opening, labels), [total_kind, tile_kind], *hold(rows, stack),
        )
        (total,) = call(
            functools.partial(first_rest, labels), [total_kind], *hold(rows, stack, opened),
            cost=HIDING_COST,
        )
        tiles.append(tile)
        totals.append(total)
        return opened

    def first(stack):
        total, tile = call(
            functools.partial(first_middle, labels), [total_kind, tile_kind],
            *hold(rows, stack, totals[-1]),
        )
        tiles.append(tile)
        totals.append(total)
        return total

    stacks, steps = block_partners(packed, first_own, first)
    for stack in stacks[2:-1]:
        first(stack)
    q_near, tile = call(
        functools.partial(first_closing, labels, nears),
        [kept((labels, nears * own), jnp.bfloat16), tile_kind],
        *hold(rows, stacks[-1], totals[-1], packed, held, *near),
    )
    tiles.append(tile)

    if parts * math.prod(tile_kind.shape) * 2 <= KEPT_BYTES:
        tiles = hold(*tiles)
    part_kind = kept((labels, own), jnp.float32)
    far = call(second_parts, [part_kind] * (parts - 2), *hold(q_near), *tiles[2:])
    if far:
        q_near, *far = lax.optimization_barrier((q_near, *far))
    here, beside = call(second_parts, [part_kind] * 2, *hold(q_near), *tiles[:2])
    arrived = [send_back(part, step) for part, step in zip([beside, *far], steps[1:])]
    return call(
        second_closing,
        [jax.ShapeDtypeStruct((labels, own), jnp.float32)] * 2,
        *hold(q_near, sent, held, here, *arrived),
    )


def solution(mesh):
    in_specs = (P(None, ("scene", "blk", "grp")), P(("scene", "blk", "grp")), P(None, "scene"), P())
    out_specs = (P(None, ("scene", "blk", "grp")), P(None, ("scene", "blk", "grp")))
    return jax.shard_map(shards, mesh=mesh, in_specs=in_specs, out_specs=out_specs, check_vma=False)
```

```python
import functools
import math

import jax
import jax.numpy as jnp
from jax import lax
from jax.experimental import pallas as pl
from jax.experimental.pallas import tpu as pltpu
from jax.sharding import PartitionSpec as P

AUX = 16
LANES = 128
VMEM_LIMIT = 56 * 1024 * 1024
KEPT_BYTES = 4 * 1024 * 1024
SCHEDULE_COST = 10 ** 10
EXP_SQUARINGS = 5
EXP_TERMS = [
    term / 2.0 ** (EXP_SQUARINGS * power)
    for power, term in enumerate([
        1.0000000387843881, 0.9999854684180126, 0.499772553042558,
        0.16550051010162015, 0.03898878338548839, 0.005403287826230924,
    ])
]


def normalize(logits):
    raised = jnp.exp(logits)
    return raised / jnp.sum(raised, axis=0, keepdims=True)


def three_parts(value):
    high = value.astype(jnp.bfloat16).astype(jnp.float32)
    middle = (value - high).astype(jnp.bfloat16).astype(jnp.float32)
    return [high, middle, value - high - middle]


def pick_features(features_ref, member):
    feats, points = features_ref.shape
    own = member.shape[1]
    groups = points // LANES
    wide = features_ref[...].astype(jnp.float32)
    wide = jnp.concatenate([wide, jnp.zeros((8 - feats, points), jnp.float32)], axis=0)
    table = jnp.concatenate(
        [wide[:, group * LANES:(group + 1) * LANES] for group in range(groups)], axis=0
    ).astype(jnp.bfloat16)
    lane = lax.broadcasted_iota(jnp.int32, (LANES, own), 0)
    chosen = jnp.where(lane == member % LANES, 1.0, 0.0).astype(jnp.bfloat16)
    found = jnp.dot(table, chosen, preferred_element_type=jnp.float32)
    found = found.reshape(groups, 8, own)
    group = lax.broadcasted_iota(jnp.int32, (groups, 8, own), 0)
    return jnp.sum(jnp.where(group == (member // LANES)[None], found, 0.0), axis=0)


def prepare_kernel(features_ref, member_ref, unary_ref, compat_ref, sent_ref, held_ref):
    labels = unary_ref.shape[0]
    sent_ref[pl.ds(0, labels), :] = unary_ref[...]
    sent_ref[pl.ds(labels, 8), :] = pick_features(features_ref, member_ref[...])
    held_ref[...] = compat_ref[...]


def half_norms(feats):
    return three_parts(-0.5 * jnp.sum(feats * feats, axis=0, keepdims=True))


def product_sides(feats):
    own = feats.shape[1]
    norms = half_norms(feats)
    ones = jnp.ones((3, own), jnp.float32)
    spare = jnp.zeros((AUX - 8 - 6, own), jnp.float32)
    columns = jnp.concatenate([feats] + norms + [ones, spare], axis=0)
    rows = jnp.concatenate([feats, ones] + norms + [spare], axis=0)
    return columns.astype(jnp.bfloat16), rows.astype(jnp.bfloat16)


def pack_kernel(labels, *refs):
    near_refs, packed_ref, rows_ref = refs[:-2], refs[-2], refs[-1]
    for place, near_ref in enumerate(near_refs):
        own = near_ref.shape[1]
        feats = near_ref[pl.ds(labels, 8), :]
        probs = normalize(-near_ref[pl.ds(0, labels), :])
        packed_ref[place] = jnp.concatenate([probs, feats], axis=0).astype(jnp.bfloat16)
        rows_ref[:, pl.ds(place * own, own)] = product_sides(feats)[1]


def over_blocks(count, body, start):
    if count <= 4:
        for index in range(count):
            start = body(index, start)
        return start
    return lax.fori_loop(0, count, body, start)


def finish(message, qb, unary, compat_ref):
    message = message - qb.astype(jnp.float32)
    pairwise = jnp.dot(
        compat_ref[...], message, precision=lax.Precision.HIGHEST,
        preferred_element_type=jnp.float32,
    )
    return normalize(-unary - pairwise), pairwise


def exp_by_squaring(value):
    result = jnp.full_like(value, EXP_TERMS[-1])
    for term in EXP_TERMS[-2::-1]:
        result = result * value + term
    for _ in range(EXP_SQUARINGS):
        result = result * result
    return result


def exp_tile(exponent):
    count = exponent.shape[0] // 4
    parts = [jnp.exp(exponent[count:]), exp_by_squaring(exponent[:count])]
    return jnp.concatenate([parts[1], parts[0]], axis=0).astype(jnp.bfloat16)


def first_part(labels, rows_ref, packed_ref, total, tile_ref=None, begin=0, end=None):
    blocks = range(begin, packed_ref.shape[0] if end is None else end)
    rows = rows_ref[...]

    def exponents(index):
        columns = product_sides(packed_ref[index][labels:].astype(jnp.float32))[0]
        return lax.dot_general(
            columns, rows, (((0,), (0,)), ((), ())), preferred_element_type=jnp.float32
        )

    ahead = exponents(begin)
    for index in blocks:
        exponent = ahead
        if index + 1 < blocks.stop:
            ahead = exponents(index + 1)
        tile = exp_tile(exponent)
        if index == 0 and tile_ref is not None:
            tile_ref[...] = tile
        total = total + jnp.dot(
            packed_ref[index][:labels], tile, preferred_element_type=jnp.float32
        )
    return total


def first_opening(labels, rows_ref, packed_ref, total_ref, tile_ref):
    start = jnp.zeros(total_ref.shape, jnp.float32)
    total_ref[...] = first_part(labels, rows_ref, packed_ref, start, tile_ref, end=1)


def first_rest(labels, rows_ref, packed_ref, sum_ref, total_ref):
    total_ref[...] = first_part(labels, rows_ref, packed_ref, sum_ref[...], begin=1)


def first_middle(labels, rows_ref, packed_ref, sum_ref, total_ref, tile_ref):
    total_ref[...] = first_part(labels, rows_ref, packed_ref, sum_ref[...], tile_ref)


def first_closing(labels, nears, *refs):
    rows_ref, packed_ref, sum_ref, own_ref, compat_ref = refs[:5]
    near_refs, q_ref, tile_ref = refs[5:-2], refs[-2], refs[-1]
    own = own_ref.shape[2]
    total = first_part(labels, rows_ref, packed_ref, sum_ref[...], tile_ref)
    labels_now = [own_ref[near][:labels] for near in range(nears)]
    unary = [near_ref[pl.ds(0, labels), :] for near_ref in near_refs]
    probs, _ = finish(
        total, jnp.concatenate(labels_now, axis=1), jnp.concatenate(unary, axis=1), compat_ref
    )
    q_ref[...] = probs.astype(jnp.bfloat16)


def second_parts(q_ref, *refs):
    count = len(refs) // 2
    for tile_ref, part_ref in zip(refs[:count], refs[count:]):
        part_ref[...] = lax.dot_general(
            q_ref[...], tile_ref[...], (((1,), (1,)), ((), ())),
            preferred_element_type=jnp.float32,
        )


def second_closing(q_ref, near_ref, compat_ref, *refs):
    probs_ref, pairwise_ref = refs[-2:]
    labels, own = probs_ref.shape
    total = refs[0][...]
    for part_ref in refs[1:-2]:
        total = total + part_ref[...]
    unary = near_ref[pl.ds(0, labels), :]
    probs, pairwise = finish(total, q_ref[:, pl.ds(0, own)], unary, compat_ref)
    probs_ref[...] = probs
    pairwise_ref[...] = pairwise


def swap(value, axis, steps):
    count = lax.axis_size(axis)
    pairs = [
        (source, source ^ steps if paired(axis) else (source + steps) % count)
        for source in range(count)
    ]
    return lax.ppermute(value, axis, pairs)


def group_partners(value):
    count = lax.axis_size("grp")
    order = sorted(range(1, count), key=lambda steps: (steps != count // 2, -steps))
    return [value] + [swap(value, "grp", steps) for steps in reversed(order)]


def paired(axis):
    count = lax.axis_size(axis)
    return count & (count - 1) == 0


def block_partners(value, use_own, use_beside):
    count = lax.axis_size("blk")
    if not paired("blk"):
        stacks = [value] + [swap(value, "blk", steps) for steps in range(1, count)]
        use_own(value)
        use_beside(stacks[1])
        return stacks, list(range(count))
    steps = list(range(2, count, 2))
    far = [swap(value, "blk", step) for step in steps]
    sent, _ = lax.optimization_barrier((value, use_own(value)))
    beside = swap(sent, "blk", 1)
    *far, _ = lax.optimization_barrier((*far, use_beside(beside)))
    stacks = [value, beside] + far + [swap(stack, "blk", 1) for stack in far]
    return stacks, [0, 1] + steps + [step + 1 for step in steps]


def send_back(value, steps):
    return swap(value, "blk", steps if paired("blk") else lax.axis_size("blk") - steps)


def small(dims, kind):
    return math.prod(dims) * jnp.dtype(kind).itemsize <= KEPT_BYTES


def call(kernel, out_shapes, *operands):
    return pl.pallas_call(
        kernel,
        out_shape=tuple(out_shapes),
        cost_estimate=pl.CostEstimate(flops=SCHEDULE_COST, transcendentals=0, bytes_accessed=SCHEDULE_COST),
        compiler_params=pltpu.CompilerParams(vmem_limit_bytes=VMEM_LIMIT),
    )(*operands)


def hold(*operands):
    return [
        pltpu.with_memory_space_constraint(operand, pltpu.VMEM)
        if small(operand.shape, operand.dtype) else operand
        for operand in operands
    ]


def kept(dims, kind, copies=1):
    if small((copies,) + dims, kind):
        return pltpu.VMEM(dims, kind)
    return jax.ShapeDtypeStruct(dims, kind)


def shards(unary, member, features, compat):
    labels, own = unary.shape
    nears = lax.axis_size("grp")
    count = lax.axis_size("blk") * nears
    sent, held = call(
        prepare_kernel,
        [kept((labels + 8, own), jnp.float32), kept(compat.shape, jnp.float32)],
        features, member[None], unary, compat,
    )
    near = group_partners(sent)
    packed, rows = call(
        functools.partial(pack_kernel, labels),
        [kept((nears, labels + 8, own), jnp.bfloat16), kept((AUX, nears * own), jnp.bfloat16)],
        *hold(*near),
    )
    parts = lax.axis_size("blk")
    tile_kind = kept((own, nears * own), jnp.bfloat16, parts)
    tiles, totals = [], []

    total_kind = kept((labels, nears * own), jnp.float32)

    def first_own(stack):
        opened, tile = call(
            functools.partial(first_opening, labels), [total_kind, tile_kind], *hold(rows, stack)
        )
        (total,) = call(
            functools.partial(first_rest, labels), [total_kind], *hold(rows, stack, opened)
        )
        tiles.append(tile)
        totals.append(total)
        return opened

    def first(stack):
        total, tile = call(
            functools.partial(first_middle, labels), [total_kind, tile_kind],
            *hold(rows, stack, totals[-1]),
        )
        tiles.append(tile)
        totals.append(total)
        return total

    stacks, steps = block_partners(packed, first_own, first)
    for stack in stacks[2:-1]:
        first(stack)
    q_near, tile = call(
        functools.partial(first_closing, labels, nears),
        [kept((labels, nears * own), jnp.bfloat16), tile_kind],
        *hold(rows, stacks[-1], totals[-1], packed, held, *near),
    )
    tiles.append(tile)

    if parts * math.prod(tile_kind.shape) * 2 <= KEPT_BYTES:
        tiles = hold(*tiles)
    part_kind = kept((labels, own), jnp.float32)
    far = call(second_parts, [part_kind] * (parts - 2), *hold(q_near), *tiles[2:])
    if far:
        q_near, *far = lax.optimization_barrier((q_near, *far))
    here, beside = call(second_parts, [part_kind] * 2, *hold(q_near), *tiles[:2])
    arrived = [send_back(part, step) for part, step in zip([beside, *far], steps[1:])]
    return call(
        second_closing,
        [jax.ShapeDtypeStruct((labels, own), jnp.float32)] * 2,
        *hold(q_near, sent, held, here, *arrived),
    )


def solution(mesh):
    in_specs = (P(None, ("scene", "blk", "grp")), P(("scene", "blk", "grp")), P(None, "scene"), P())
    out_specs = (P(None, ("scene", "blk", "grp")), P(None, ("scene", "blk", "grp")))
    return jax.shard_map(shards, mesh=mesh, in_specs=in_specs, out_specs=out_specs, check_vma=False)
```

```python
import functools
import math

import jax
import jax.numpy as jnp
from jax import lax
from jax.experimental import pallas as pl
from jax.experimental.pallas import tpu as pltpu
from jax.sharding import PartitionSpec as P

AUX = 32
LOG2E = math.log2(math.e)
LANES = 128
VMEM_LIMIT = 56 * 1024 * 1024
KEPT_BYTES = 4 * 1024 * 1024
SCHEDULE_COST = 10 ** 10


def normalize(logits):
    raised = jnp.exp(logits)
    return raised / jnp.sum(raised, axis=0, keepdims=True)


def three_parts(value):
    high = value.astype(jnp.bfloat16).astype(jnp.float32)
    middle = (value - high).astype(jnp.bfloat16).astype(jnp.float32)
    return [high, middle, value - high - middle]


def pick_features(features_ref, member):
    feats, points = features_ref.shape
    own = member.shape[1]
    groups = points // LANES
    wide = features_ref[...].astype(jnp.float32)
    wide = jnp.concatenate([wide, jnp.zeros((8 - feats, points), jnp.float32)], axis=0)
    table = jnp.concatenate(
        [wide[:, group * LANES:(group + 1) * LANES] for group in range(groups)], axis=0
    ).astype(jnp.bfloat16)
    lane = lax.broadcasted_iota(jnp.int32, (LANES, own), 0)
    chosen = jnp.where(lane == member % LANES, 1.0, 0.0).astype(jnp.bfloat16)
    found = jnp.dot(table, chosen, preferred_element_type=jnp.float32)
    found = found.reshape(groups, 8, own)
    group = lax.broadcasted_iota(jnp.int32, (groups, 8, own), 0)
    return jnp.sum(jnp.where(group == (member // LANES)[None], found, 0.0), axis=0)


def prepare_kernel(features_ref, member_ref, unary_ref, compat_ref, sent_ref, held_ref):
    labels = unary_ref.shape[0]
    sent_ref[pl.ds(0, labels), :] = unary_ref[...]
    sent_ref[pl.ds(labels, 8), :] = pick_features(features_ref, member_ref[...])
    held_ref[...] = compat_ref[...]


def product_sides(feats):
    own = feats.shape[1]
    norms = three_parts(-0.5 * LOG2E * jnp.sum(feats * feats, axis=0, keepdims=True))
    ones = jnp.ones((3, own), jnp.float32)
    spare = jnp.zeros((AUX - 3 * 8 - 6, own), jnp.float32)
    columns = jnp.concatenate([feats] * 3 + norms + [ones, spare], axis=0)
    rows = jnp.concatenate(three_parts(LOG2E * feats) + [ones] + norms + [spare], axis=0)
    return columns.astype(jnp.bfloat16), rows.astype(jnp.bfloat16)


def pack_kernel(labels, *refs):
    near_refs, packed_ref, rows_ref = refs[:-2], refs[-2], refs[-1]
    for place, near_ref in enumerate(near_refs):
        own = near_ref.shape[1]
        feats = near_ref[pl.ds(labels, 8), :]
        probs = normalize(-near_ref[pl.ds(0, labels), :])
        packed_ref[place] = jnp.concatenate([probs, feats], axis=0).astype(jnp.bfloat16)
        rows_ref[:, pl.ds(place * own, own)] = product_sides(feats)[1]


def over_blocks(count, body, start):
    if count <= 4:
        for index in range(count):
            start = body(index, start)
        return start
    return lax.fori_loop(0, count, body, start)


def finish(message, qb, unary, compat_ref):
    message = message - qb.astype(jnp.float32)
    pairwise = jnp.dot(
        compat_ref[...], message, precision=lax.Precision.HIGHEST,
        preferred_element_type=jnp.float32,
    )
    return normalize(-unary - pairwise), pairwise


def first_part(labels, rows_ref, packed_ref, total, tile_ref=None, begin=0, end=None):
    blocks = range(begin, packed_ref.shape[0] if end is None else end)
    rows = rows_ref[...]

    def exponents(index):
        columns = product_sides(packed_ref[index][labels:].astype(jnp.float32))[0]
        return lax.dot_general(
            columns, rows, (((0,), (0,)), ((), ())), preferred_element_type=jnp.float32
        )

    ahead = exponents(begin)
    for index in blocks:
        exponent = ahead
        if index + 1 < blocks.stop:
            ahead = exponents(index + 1)
        tile = jnp.exp2(exponent).astype(jnp.bfloat16)
        if index == 0 and tile_ref is not None:
            tile_ref[...] = tile
        total = total + jnp.dot(
            packed_ref[index][:labels], tile, preferred_element_type=jnp.float32
        )
    return total


def first_opening(labels, rows_ref, packed_ref, total_ref, tile_ref):
    start = jnp.zeros(total_ref.shape, jnp.float32)
    total_ref[...] = first_part(labels, rows_ref, packed_ref, start, tile_ref, end=1)


def first_rest(labels, rows_ref, packed_ref, sum_ref, total_ref):
    total_ref[...] = first_part(labels, rows_ref, packed_ref, sum_ref[...], begin=1)


def first_middle(labels, rows_ref, packed_ref, sum_ref, total_ref, tile_ref):
    total_ref[...] = first_part(labels, rows_ref, packed_ref, sum_ref[...], tile_ref)


def first_closing(labels, nears, *refs):
    rows_ref, packed_ref, sum_ref, own_ref, compat_ref = refs[:5]
    near_refs, q_ref, tile_ref = refs[5:-2], refs[-2], refs[-1]
    own = own_ref.shape[2]
    total = first_part(labels, rows_ref, packed_ref, sum_ref[...], tile_ref)
    labels_now = [own_ref[near][:labels] for near in range(nears)]
    unary = [near_ref[pl.ds(0, labels), :] for near_ref in near_refs]
    probs, _ = finish(
        total, jnp.concatenate(labels_now, axis=1), jnp.concatenate(unary, axis=1), compat_ref
    )
    q_ref[...] = probs.astype(jnp.bfloat16)


def second_parts(q_ref, *refs):
    count = len(refs) // 2
    for tile_ref, part_ref in zip(refs[:count], refs[count:]):
        part_ref[...] = lax.dot_general(
            q_ref[...], tile_ref[...], (((1,), (1,)), ((), ())),
            preferred_element_type=jnp.float32,
        )


def second_closing(q_ref, near_ref, compat_ref, *refs):
    probs_ref, pairwise_ref = refs[-2:]
    labels, own = probs_ref.shape
    total = refs[0][...]
    for part_ref in refs[1:-2]:
        total = total + part_ref[...]
    unary = near_ref[pl.ds(0, labels), :]
    probs, pairwise = finish(total, q_ref[:, pl.ds(0, own)], unary, compat_ref)
    probs_ref[...] = probs
    pairwise_ref[...] = pairwise


def swap(value, axis, steps):
    count = lax.axis_size(axis)
    pairs = [
        (source, source ^ steps if paired(axis) else (source + steps) % count)
        for source in range(count)
    ]
    return lax.ppermute(value, axis, pairs)


def group_partners(value):
    count = lax.axis_size("grp")
    order = sorted(range(1, count), key=lambda steps: (steps != count // 2, -steps))
    return [value] + [swap(value, "grp", steps) for steps in reversed(order)]


def paired(axis):
    count = lax.axis_size(axis)
    return count & (count - 1) == 0


def block_partners(value, use_own, use_beside):
    count = lax.axis_size("blk")
    if not paired("blk"):
        stacks = [value] + [swap(value, "blk", steps) for steps in range(1, count)]
        use_own(value)
        use_beside(stacks[1])
        return stacks, list(range(count))
    steps = list(range(2, count, 2))
    far = [swap(value, "blk", step) for step in steps]
    sent, _ = lax.optimization_barrier((value, use_own(value)))
    beside = swap(sent, "blk", 1)
    *far, _ = lax.optimization_barrier((*far, use_beside(beside)))
    stacks = [value, beside] + far + [swap(stack, "blk", 1) for stack in far]
    return stacks, [0, 1] + steps + [step + 1 for step in steps]


def send_back(value, steps):
    return swap(value, "blk", steps if paired("blk") else lax.axis_size("blk") - steps)


def small(dims, kind):
    return math.prod(dims) * jnp.dtype(kind).itemsize <= KEPT_BYTES


def call(kernel, out_shapes, *operands):
    return pl.pallas_call(
        kernel,
        out_shape=tuple(out_shapes),
        cost_estimate=pl.CostEstimate(flops=SCHEDULE_COST, transcendentals=0, bytes_accessed=SCHEDULE_COST),
        compiler_params=pltpu.CompilerParams(vmem_limit_bytes=VMEM_LIMIT),
    )(*operands)


def hold(*operands):
    return [
        pltpu.with_memory_space_constraint(operand, pltpu.VMEM)
        if small(operand.shape, operand.dtype) else operand
        for operand in operands
    ]


def kept(dims, kind, copies=1):
    if small((copies,) + dims, kind):
        return pltpu.VMEM(dims, kind)
    return jax.ShapeDtypeStruct(dims, kind)


def shards(unary, member, features, compat):
    labels, own = unary.shape
    nears = lax.axis_size("grp")
    count = lax.axis_size("blk") * nears
    sent, held = call(
        prepare_kernel,
        [kept((labels + 8, own), jnp.float32), kept(compat.shape, jnp.float32)],
        features, member[None], unary, compat,
    )
    near = group_partners(sent)
    packed, rows = call(
        functools.partial(pack_kernel, labels),
        [kept((nears, labels + 8, own), jnp.bfloat16), kept((AUX, nears * own), jnp.bfloat16)],
        *hold(*near),
    )
    parts = lax.axis_size("blk")
    tile_kind = kept((own, nears * own), jnp.bfloat16, parts)
    tiles, totals = [], []

    total_kind = kept((labels, nears * own), jnp.float32)

    def first_own(stack):
        opened, tile = call(
            functools.partial(first_opening, labels), [total_kind, tile_kind], *hold(rows, stack)
        )
        (total,) = call(
            functools.partial(first_rest, labels), [total_kind], *hold(rows, stack, opened)
        )
        tiles.append(tile)
        totals.append(total)
        return opened

    def first(stack):
        total, tile = call(
            functools.partial(first_middle, labels), [total_kind, tile_kind],
            *hold(rows, stack, totals[-1]),
        )
        tiles.append(tile)
        totals.append(total)
        return total

    stacks, steps = block_partners(packed, first_own, first)
    for stack in stacks[2:-1]:
        first(stack)
    q_near, tile = call(
        functools.partial(first_closing, labels, nears),
        [kept((labels, nears * own), jnp.bfloat16), tile_kind],
        *hold(rows, stacks[-1], totals[-1], packed, held, *near),
    )
    tiles.append(tile)

    if parts * math.prod(tile_kind.shape) * 2 <= KEPT_BYTES:
        tiles = hold(*tiles)
    part_kind = kept((labels, own), jnp.float32)
    far = call(second_parts, [part_kind] * (parts - 2), *hold(q_near), *tiles[2:])
    if far:
        q_near, *far = lax.optimization_barrier((q_near, *far))
    here, beside = call(second_parts, [part_kind] * 2, *hold(q_near), *tiles[:2])
    arrived = [send_back(part, step) for part, step in zip([beside, *far], steps[1:])]
    return call(
        second_closing,
        [jax.ShapeDtypeStruct((labels, own), jnp.float32)] * 2,
        *hold(q_near, sent, held, here, *arrived),
    )


def solution(mesh):
    in_specs = (P(None, ("scene", "blk", "grp")), P(("scene", "blk", "grp")), P(None, "scene"), P())
    out_specs = (P(None, ("scene", "blk", "grp")), P(None, ("scene", "blk", "grp")))
    return jax.shard_map(shards, mesh=mesh, in_specs=in_specs, out_specs=out_specs, check_vma=False)
```

```python
import functools
import math

import jax
import jax.numpy as jnp
from jax import lax
from jax.experimental import pallas as pl
from jax.experimental.pallas import tpu as pltpu
from jax.sharding import PartitionSpec as P

AUX = 16
LANES = 128
VMEM_LIMIT = 56 * 1024 * 1024
KEPT_BYTES = 4 * 1024 * 1024
SCHEDULE_COST = 10 ** 10


def normalize(logits):
    raised = jnp.exp(logits)
    return raised / jnp.sum(raised, axis=0, keepdims=True)


def three_parts(value):
    high = value.astype(jnp.bfloat16).astype(jnp.float32)
    middle = (value - high).astype(jnp.bfloat16).astype(jnp.float32)
    return [high, middle, value - high - middle]


def pick_features(features_ref, member):
    feats, points = features_ref.shape
    own = member.shape[1]
    groups = points // LANES
    wide = features_ref[...].astype(jnp.float32)
    wide = jnp.concatenate([wide, jnp.zeros((8 - feats, points), jnp.float32)], axis=0)
    table = jnp.concatenate(
        [wide[:, group * LANES:(group + 1) * LANES] for group in range(groups)], axis=0
    ).astype(jnp.bfloat16)
    lane = lax.broadcasted_iota(jnp.int32, (LANES, own), 0)
    chosen = jnp.where(lane == member % LANES, 1.0, 0.0).astype(jnp.bfloat16)
    found = jnp.dot(table, chosen, preferred_element_type=jnp.float32)
    found = found.reshape(groups, 8, own)
    group = lax.broadcasted_iota(jnp.int32, (groups, 8, own), 0)
    return jnp.sum(jnp.where(group == (member // LANES)[None], found, 0.0), axis=0)


def prepare_kernel(features_ref, member_ref, unary_ref, compat_ref, sent_ref, held_ref):
    labels = unary_ref.shape[0]
    sent_ref[pl.ds(0, labels), :] = unary_ref[...]
    sent_ref[pl.ds(labels, 8), :] = pick_features(features_ref, member_ref[...])
    held_ref[...] = compat_ref[...]


def half_norms(feats):
    return three_parts(-0.5 * jnp.sum(feats * feats, axis=0, keepdims=True))


def product_sides(feats):
    own = feats.shape[1]
    norms = half_norms(feats)
    ones = jnp.ones((3, own), jnp.float32)
    spare = jnp.zeros((AUX - 8 - 6, own), jnp.float32)
    columns = jnp.concatenate([feats] + norms + [ones, spare], axis=0)
    rows = jnp.concatenate([feats, ones] + norms + [spare], axis=0)
    return columns.astype(jnp.bfloat16), rows.astype(jnp.bfloat16)


def pack_kernel(labels, *refs):
    near_refs, packed_ref, rows_ref = refs[:-2], refs[-2], refs[-1]
    for place, near_ref in enumerate(near_refs):
        own = near_ref.shape[1]
        feats = near_ref[pl.ds(labels, 8), :]
        probs = normalize(-near_ref[pl.ds(0, labels), :])
        packed_ref[place] = jnp.concatenate([probs, feats], axis=0).astype(jnp.bfloat16)
        rows_ref[:, pl.ds(place * own, own)] = product_sides(feats)[1]


def over_blocks(count, body, start):
    if count <= 4:
        for index in range(count):
            start = body(index, start)
        return start
    return lax.fori_loop(0, count, body, start)


def finish(message, qb, unary, compat_ref):
    message = message - qb.astype(jnp.float32)
    pairwise = jnp.dot(
        compat_ref[...], message, precision=lax.Precision.HIGHEST,
        preferred_element_type=jnp.float32,
    )
    return normalize(-unary - pairwise), pairwise


def first_part(labels, rows_ref, packed_ref, total, tile_ref):
    blocks, _, own = packed_ref.shape
    rows = rows_ref[...]

    def exponents(index):
        columns = product_sides(packed_ref[index][labels:].astype(jnp.float32))[0]
        return lax.dot_general(
            columns, rows, (((0,), (0,)), ((), ())), preferred_element_type=jnp.float32
        )

    ahead = exponents(0)
    for index in range(blocks):
        exponent = ahead
        if index + 1 < blocks:
            ahead = exponents(index + 1)
        tile = jnp.exp(exponent).astype(jnp.bfloat16)
        if index == 0:
            tile_ref[...] = tile
        total = total + jnp.dot(
            packed_ref[index][:labels], tile, preferred_element_type=jnp.float32
        )
    return total


def first_opening(labels, rows_ref, packed_ref, total_ref, tile_ref):
    start = jnp.zeros(total_ref.shape, jnp.float32)
    total_ref[...] = first_part(labels, rows_ref, packed_ref, start, tile_ref)


def first_middle(labels, rows_ref, packed_ref, sum_ref, total_ref, tile_ref):
    total_ref[...] = first_part(labels, rows_ref, packed_ref, sum_ref[...], tile_ref)


def copy_kernel(stack_ref, copy_ref):
    copy_ref[...] = stack_ref[...]


def first_closing(labels, nears, *refs):
    rows_ref, packed_ref, sum_ref, own_ref, compat_ref = refs[:5]
    near_refs, refs = refs[5:5 + nears], refs[5 + nears:]
    count = len(refs) // 2
    far_refs, (q_ref, tile_ref, *part_refs) = refs[:count - 1], refs[count - 1:]
    total = first_part(labels, rows_ref, packed_ref, sum_ref[...], tile_ref)
    labels_now = [own_ref[near][:labels] for near in range(nears)]
    unary = [near_ref[pl.ds(0, labels), :] for near_ref in near_refs]
    probs, _ = finish(
        total, jnp.concatenate(labels_now, axis=1), jnp.concatenate(unary, axis=1), compat_ref
    )
    q_ref[...] = probs.astype(jnp.bfloat16)
    second_parts(q_ref, *far_refs, tile_ref, *part_refs)


def second_parts(q_ref, *refs):
    count = len(refs) // 2
    for tile_ref, part_ref in zip(refs[:count], refs[count:]):
        part_ref[...] = lax.dot_general(
            q_ref[...], tile_ref[...], (((1,), (1,)), ((), ())),
            preferred_element_type=jnp.float32,
        )


def second_closing(q_ref, near_ref, compat_ref, *refs):
    probs_ref, pairwise_ref = refs[-2:]
    labels, own = probs_ref.shape
    total = refs[0][...]
    for part_ref in refs[1:-2]:
        total = total + part_ref[...]
    unary = near_ref[pl.ds(0, labels), :]
    probs, pairwise = finish(total, q_ref[:, pl.ds(0, own)], unary, compat_ref)
    probs_ref[...] = probs
    pairwise_ref[...] = pairwise


def swap(value, axis, steps):
    count = lax.axis_size(axis)
    pairs = [
        (source, source ^ steps if paired(axis) else (source + steps) % count)
        for source in range(count)
    ]
    return lax.ppermute(value, axis, pairs)


def group_partners(value):
    count = lax.axis_size("grp")
    order = sorted(range(1, count), key=lambda steps: (steps != count // 2, -steps))
    return [value] + [swap(value, "grp", steps) for steps in reversed(order)]


def paired(axis):
    count = lax.axis_size(axis)
    return count & (count - 1) == 0


def block_partners(value, copied, use):
    count = lax.axis_size("blk")
    if not paired("blk"):
        stacks = [value] + [swap(value, "blk", steps) for steps in range(1, count)]
        use(value)
        use(stacks[1])
        return stacks, list(range(count))
    steps = list(range(2, count, 2))
    far = [swap(value, "blk", step) for step in steps]
    beside = swap(copied, "blk", 1)
    use(value)
    *far, _ = lax.optimization_barrier((*far, use(beside)))
    stacks = [value, beside] + far + [swap(stack, "blk", 1) for stack in far]
    return stacks, [0, 1] + steps + [step + 1 for step in steps]


def send_back(value, steps):
    return swap(value, "blk", steps if paired("blk") else lax.axis_size("blk") - steps)


def small(dims, kind):
    return math.prod(dims) * jnp.dtype(kind).itemsize <= KEPT_BYTES


def call(kernel, out_shapes, *operands):
    return pl.pallas_call(
        kernel,
        out_shape=tuple(out_shapes),
        cost_estimate=pl.CostEstimate(flops=SCHEDULE_COST, transcendentals=0, bytes_accessed=SCHEDULE_COST),
        compiler_params=pltpu.CompilerParams(vmem_limit_bytes=VMEM_LIMIT),
    )(*operands)


def hold(*operands):
    return [
        pltpu.with_memory_space_constraint(operand, pltpu.VMEM)
        if small(operand.shape, operand.dtype) else operand
        for operand in operands
    ]


def kept(dims, kind, copies=1):
    if small((copies,) + dims, kind):
        return pltpu.VMEM(dims, kind)
    return jax.ShapeDtypeStruct(dims, kind)


def shards(unary, member, features, compat):
    labels, own = unary.shape
    nears = lax.axis_size("grp")
    count = lax.axis_size("blk") * nears
    sent, held = call(
        prepare_kernel,
        [kept((labels + 8, own), jnp.float32), kept(compat.shape, jnp.float32)],
        features, member[None], unary, compat,
    )
    near = group_partners(sent)
    packed, rows = call(
        functools.partial(pack_kernel, labels),
        [kept((nears, labels + 8, own), jnp.bfloat16), kept((AUX, nears * own), jnp.bfloat16)],
        *hold(*near),
    )
    parts = lax.axis_size("blk")
    tile_kind = kept((own, nears * own), jnp.bfloat16, parts)
    tiles, totals = [], []

    total_kind = kept((labels, nears * own), jnp.float32)

    def first(stack):
        kernel = first_middle if totals else first_opening
        total, tile = call(
            functools.partial(kernel, labels), [total_kind, tile_kind],
            *hold(rows, stack, *totals[-1:]),
        )
        tiles.append(tile)
        totals.append(total)
        return total

    (copied,) = call(copy_kernel, [kept(packed.shape, jnp.bfloat16)], *hold(packed))
    stacks, steps = block_partners(packed, copied, first)
    for stack in stacks[2:-1]:
        first(stack)
    far_tiles = tiles[2:]
    if parts * math.prod(tile_kind.shape) * 2 <= KEPT_BYTES:
        tiles, far_tiles = hold(*tiles), hold(*far_tiles)
    part_kind = kept((labels, own), jnp.float32)
    q_near, _, *far = call(
        functools.partial(first_closing, labels, nears),
        [kept((labels, nears * own), jnp.bfloat16), tile_kind] + [part_kind] * (parts - 2),
        *hold(rows, stacks[-1], totals[-1], packed, held, *near), *far_tiles,
    )
    if far:
        q_near, *far = lax.optimization_barrier((q_near, *far))
    here, beside = call(second_parts, [part_kind] * 2, *hold(q_near), *tiles[:2])
    arrived = [send_back(part, step) for part, step in zip([beside, *far], steps[1:])]
    return call(
        second_closing,
        [jax.ShapeDtypeStruct((labels, own), jnp.float32)] * 2,
        *hold(q_near, sent, held, here, *arrived),
    )


def solution(mesh):
    in_specs = (P(None, ("scene", "blk", "grp")), P(("scene", "blk", "grp")), P(None, "scene"), P())
    out_specs = (P(None, ("scene", "blk", "grp")), P(None, ("scene", "blk", "grp")))
    return jax.shard_map(shards, mesh=mesh, in_specs=in_specs, out_specs=out_specs, check_vma=False)
```

```python
import functools
import math

import jax
import jax.numpy as jnp
from jax import lax
from jax.experimental import pallas as pl
from jax.experimental.pallas import tpu as pltpu
from jax.sharding import PartitionSpec as P

AUX = 16
LANES = 128
VMEM_LIMIT = 56 * 1024 * 1024
KEPT_BYTES = 4 * 1024 * 1024
SCHEDULE_COST = 10 ** 10


def normalize(logits):
    raised = jnp.exp(logits)
    return raised / jnp.sum(raised, axis=0, keepdims=True)


def three_parts(value):
    high = value.astype(jnp.bfloat16).astype(jnp.float32)
    middle = (value - high).astype(jnp.bfloat16).astype(jnp.float32)
    return [high, middle, value - high - middle]


def pick_features(features_ref, member):
    feats, points = features_ref.shape
    own = member.shape[1]
    groups = points // LANES
    wide = features_ref[...].astype(jnp.float32)
    wide = jnp.concatenate([wide, jnp.zeros((8 - feats, points), jnp.float32)], axis=0)
    table = jnp.concatenate(
        [wide[:, group * LANES:(group + 1) * LANES] for group in range(groups)], axis=0
    ).astype(jnp.bfloat16)
    lane = lax.broadcasted_iota(jnp.int32, (LANES, own), 0)
    chosen = jnp.where(lane == member % LANES, 1.0, 0.0).astype(jnp.bfloat16)
    found = jnp.dot(table, chosen, preferred_element_type=jnp.float32)
    found = found.reshape(groups, 8, own)
    group = lax.broadcasted_iota(jnp.int32, (groups, 8, own), 0)
    return jnp.sum(jnp.where(group == (member // LANES)[None], found, 0.0), axis=0)


def prepare_kernel(features_ref, member_ref, unary_ref, compat_ref, sent_ref, held_ref):
    labels = unary_ref.shape[0]
    sent_ref[pl.ds(0, labels), :] = unary_ref[...]
    sent_ref[pl.ds(labels, 8), :] = pick_features(features_ref, member_ref[...])
    held_ref[...] = compat_ref[...]


def half_norms(feats):
    return three_parts(-0.5 * jnp.sum(feats * feats, axis=0, keepdims=True))


def product_sides(feats):
    own = feats.shape[1]
    norms = half_norms(feats)
    ones = jnp.ones((3, own), jnp.float32)
    spare = jnp.zeros((AUX - 8 - 6, own), jnp.float32)
    columns = jnp.concatenate([feats] + norms + [ones, spare], axis=0)
    rows = jnp.concatenate([feats, ones] + norms + [spare], axis=0)
    return columns.astype(jnp.bfloat16), rows.astype(jnp.bfloat16)


def pack_kernel(labels, *refs):
    near_refs, packed_ref, rows_ref = refs[:-2], refs[-2], refs[-1]
    for place, near_ref in enumerate(near_refs):
        own = near_ref.shape[1]
        feats = near_ref[pl.ds(labels, 8), :]
        probs = normalize(-near_ref[pl.ds(0, labels), :])
        packed_ref[place] = jnp.concatenate([probs, feats], axis=0).astype(jnp.bfloat16)
        rows_ref[:, pl.ds(place * own, own)] = product_sides(feats)[1]


def over_blocks(count, body, start):
    if count <= 4:
        for index in range(count):
            start = body(index, start)
        return start
    return lax.fori_loop(0, count, body, start)


def finish(message, qb, unary, compat_ref):
    message = message - qb.astype(jnp.float32)
    pairwise = jnp.dot(
        compat_ref[...], message, precision=lax.Precision.HIGHEST,
        preferred_element_type=jnp.float32,
    )
    return normalize(-unary - pairwise), pairwise


def first_part(labels, rows_ref, packed_ref, total, tile_ref):
    blocks, _, own = packed_ref.shape
    rows = rows_ref[...]

    def exponents(index):
        columns = product_sides(packed_ref[index][labels:].astype(jnp.float32))[0]
        return lax.dot_general(
            columns, rows, (((0,), (0,)), ((), ())), preferred_element_type=jnp.float32
        )

    ahead = exponents(0)
    for index in range(blocks):
        exponent = ahead
        if index + 1 < blocks:
            ahead = exponents(index + 1)
        tile = jnp.exp(exponent).astype(jnp.bfloat16)
        if index == 0:
            tile_ref[...] = tile
        total = total + jnp.dot(
            packed_ref[index][:labels], tile, preferred_element_type=jnp.float32
        )
    return total


def first_opening(labels, rows_ref, packed_ref, total_ref, tile_ref):
    start = jnp.zeros(total_ref.shape, jnp.float32)
    total_ref[...] = first_part(labels, rows_ref, packed_ref, start, tile_ref)


def first_middle(labels, rows_ref, packed_ref, sum_ref, total_ref, tile_ref):
    total_ref[...] = first_part(labels, rows_ref, packed_ref, sum_ref[...], tile_ref)


def copy_kernel(stack_ref, copy_ref):
    copy_ref[...] = stack_ref[...]


def first_closing(labels, nears, *refs):
    rows_ref, packed_ref, sum_ref, own_ref, compat_ref = refs[:5]
    near_refs, refs = refs[5:5 + nears], refs[5 + nears:]
    count = len(refs) // 2
    far_refs, (q_ref, *part_refs, tile_ref) = refs[:count - 1], refs[count - 1:]
    total = first_part(labels, rows_ref, packed_ref, sum_ref[...], tile_ref)
    labels_now = [own_ref[near][:labels] for near in range(nears)]
    unary = [near_ref[pl.ds(0, labels), :] for near_ref in near_refs]
    probs, _ = finish(
        total, jnp.concatenate(labels_now, axis=1), jnp.concatenate(unary, axis=1), compat_ref
    )
    q_ref[...] = probs.astype(jnp.bfloat16)
    second_parts(q_ref, *far_refs, tile_ref, *part_refs)


def second_parts(q_ref, *refs):
    count = len(refs) // 2
    for tile_ref, part_ref in zip(refs[:count], refs[count:]):
        part_ref[...] = lax.dot_general(
            q_ref[...], tile_ref[...], (((1,), (1,)), ((), ())),
            preferred_element_type=jnp.float32,
        )


def second_closing(q_ref, near_ref, compat_ref, *refs):
    probs_ref, pairwise_ref = refs[-2:]
    labels, own = probs_ref.shape
    total = refs[0][...]
    for part_ref in refs[1:-2]:
        total = total + part_ref[...]
    unary = near_ref[pl.ds(0, labels), :]
    probs, pairwise = finish(total, q_ref[:, pl.ds(0, own)], unary, compat_ref)
    probs_ref[...] = probs
    pairwise_ref[...] = pairwise


def swap(value, axis, steps):
    count = lax.axis_size(axis)
    pairs = [
        (source, source ^ steps if paired(axis) else (source + steps) % count)
        for source in range(count)
    ]
    return lax.ppermute(value, axis, pairs)


def group_partners(value):
    count = lax.axis_size("grp")
    order = sorted(range(1, count), key=lambda steps: (steps != count // 2, -steps))
    return [value] + [swap(value, "grp", steps) for steps in reversed(order)]


def paired(axis):
    count = lax.axis_size(axis)
    return count & (count - 1) == 0


def block_partners(value, copied, use):
    count = lax.axis_size("blk")
    if not paired("blk"):
        stacks = [value] + [swap(value, "blk", steps) for steps in range(1, count)]
        use(value)
        use(stacks[1])
        return stacks, list(range(count))
    steps = list(range(2, count, 2))
    far = [swap(value, "blk", step) for step in steps]
    beside = swap(copied, "blk", 1)
    use(value)
    *far, _ = lax.optimization_barrier((*far, use(beside)))
    stacks = [value, beside] + far + [swap(stack, "blk", 1) for stack in far]
    return stacks, [0, 1] + steps + [step + 1 for step in steps]


def send_back(value, steps):
    return swap(value, "blk", steps if paired("blk") else lax.axis_size("blk") - steps)


def small(dims, kind):
    return math.prod(dims) * jnp.dtype(kind).itemsize <= KEPT_BYTES


def call(kernel, out_shapes, *operands, scratch=()):
    return pl.pallas_call(
        kernel,
        out_shape=tuple(out_shapes),
        scratch_shapes=scratch,
        cost_estimate=pl.CostEstimate(flops=SCHEDULE_COST, transcendentals=0, bytes_accessed=SCHEDULE_COST),
        compiler_params=pltpu.CompilerParams(vmem_limit_bytes=VMEM_LIMIT),
    )(*operands)


def hold(*operands):
    return [
        pltpu.with_memory_space_constraint(operand, pltpu.VMEM)
        if small(operand.shape, operand.dtype) else operand
        for operand in operands
    ]


def kept(dims, kind, copies=1):
    if small((copies,) + dims, kind):
        return pltpu.VMEM(dims, kind)
    return jax.ShapeDtypeStruct(dims, kind)


def shards(unary, member, features, compat):
    labels, own = unary.shape
    nears = lax.axis_size("grp")
    count = lax.axis_size("blk") * nears
    sent, held = call(
        prepare_kernel,
        [kept((labels + 8, own), jnp.float32), kept(compat.shape, jnp.float32)],
        features, member[None], unary, compat,
    )
    near = group_partners(sent)
    packed, rows = call(
        functools.partial(pack_kernel, labels),
        [kept((nears, labels + 8, own), jnp.bfloat16), kept((AUX, nears * own), jnp.bfloat16)],
        *hold(*near),
    )
    parts = lax.axis_size("blk")
    tile_kind = kept((own, nears * own), jnp.bfloat16, parts)
    tiles, totals = [], []

    total_kind = kept((labels, nears * own), jnp.float32)

    def first(stack):
        kernel = first_middle if totals else first_opening
        total, tile = call(
            functools.partial(kernel, labels), [total_kind, tile_kind],
            *hold(rows, stack, *totals[-1:]),
        )
        tiles.append(tile)
        totals.append(total)
        return total

    (copied,) = call(copy_kernel, [kept(packed.shape, jnp.bfloat16)], *hold(packed))
    stacks, steps = block_partners(packed, copied, first)
    for stack in stacks[2:-1]:
        first(stack)
    far_tiles = tiles[2:]
    if parts * math.prod(tile_kind.shape) * 2 <= KEPT_BYTES:
        tiles, far_tiles = hold(*tiles), hold(*far_tiles)
    part_kind = kept((labels, own), jnp.float32)
    q_near, *far = call(
        functools.partial(first_closing, labels, nears),
        [kept((labels, nears * own), jnp.bfloat16)] + [part_kind] * (parts - 2),
        *hold(rows, stacks[-1], totals[-1], packed, held, *near), *far_tiles,
        scratch=[pltpu.VMEM((own, nears * own), jnp.bfloat16)],
    )
    if far:
        q_near, *far = lax.optimization_barrier((q_near, *far))
    here, beside = call(second_parts, [part_kind] * 2, *hold(q_near), *tiles[:2])
    arrived = [send_back(part, step) for part, step in zip([beside, *far], steps[1:])]
    return call(
        second_closing,
        [jax.ShapeDtypeStruct((labels, own), jnp.float32)] * 2,
        *hold(q_near, sent, held, here, *arrived),
    )


def solution(mesh):
    in_specs = (P(None, ("scene", "blk", "grp")), P(("scene", "blk", "grp")), P(None, "scene"), P())
    out_specs = (P(None, ("scene", "blk", "grp")), P(None, ("scene", "blk", "grp")))
    return jax.shard_map(shards, mesh=mesh, in_specs=in_specs, out_specs=out_specs, check_vma=False)
```

```python
import functools
import math

import jax
import jax.numpy as jnp
from jax import lax
from jax.experimental import pallas as pl
from jax.experimental.pallas import tpu as pltpu
from jax.sharding import PartitionSpec as P

AUX = 16
LANES = 128
VMEM_LIMIT = 56 * 1024 * 1024
KEPT_BYTES = 4 * 1024 * 1024
SCHEDULE_COST = 10 ** 10


def normalize(logits):
    raised = jnp.exp(logits)
    return raised / jnp.sum(raised, axis=0, keepdims=True)


def three_parts(value):
    high = value.astype(jnp.bfloat16).astype(jnp.float32)
    middle = (value - high).astype(jnp.bfloat16).astype(jnp.float32)
    return [high, middle, value - high - middle]


def pick_features(features_ref, member):
    feats, points = features_ref.shape
    own = member.shape[1]
    groups = points // LANES
    wide = features_ref[...].astype(jnp.float32)
    wide = jnp.concatenate([wide, jnp.zeros((8 - feats, points), jnp.float32)], axis=0)
    table = jnp.concatenate(
        [wide[:, group * LANES:(group + 1) * LANES] for group in range(groups)], axis=0
    ).astype(jnp.bfloat16)
    lane = lax.broadcasted_iota(jnp.int32, (LANES, own), 0)
    chosen = jnp.where(lane == member % LANES, 1.0, 0.0).astype(jnp.bfloat16)
    found = jnp.dot(table, chosen, preferred_element_type=jnp.float32)
    found = found.reshape(groups, 8, own)
    group = lax.broadcasted_iota(jnp.int32, (groups, 8, own), 0)
    return jnp.sum(jnp.where(group == (member // LANES)[None], found, 0.0), axis=0)


def prepare_kernel(features_ref, member_ref, unary_ref, compat_ref, sent_ref, held_ref):
    labels = unary_ref.shape[0]
    sent_ref[pl.ds(0, labels), :] = unary_ref[...]
    sent_ref[pl.ds(labels, 8), :] = pick_features(features_ref, member_ref[...])
    held_ref[...] = compat_ref[...]


def half_norms(feats):
    return three_parts(-0.5 * jnp.sum(feats * feats, axis=0, keepdims=True))


def product_sides(feats):
    own = feats.shape[1]
    norms = half_norms(feats)
    ones = jnp.ones((3, own), jnp.float32)
    spare = jnp.zeros((AUX - 8 - 6, own), jnp.float32)
    columns = jnp.concatenate([feats] + norms + [ones, spare], axis=0)
    rows = jnp.concatenate([feats, ones] + norms + [spare], axis=0)
    return columns.astype(jnp.bfloat16), rows.astype(jnp.bfloat16)


def pack_kernel(labels, *refs):
    near_refs, packed_ref, rows_ref = refs[:-2], refs[-2], refs[-1]
    for place, near_ref in enumerate(near_refs):
        own = near_ref.shape[1]
        feats = near_ref[pl.ds(labels, 8), :]
        probs = normalize(-near_ref[pl.ds(0, labels), :])
        packed_ref[place] = jnp.concatenate([probs, feats], axis=0).astype(jnp.bfloat16)
        rows_ref[:, pl.ds(place * own, own)] = product_sides(feats)[1]


def join_kernel(*refs):
    joined_ref = refs[-1]
    base = 0
    for ref in refs[:-1]:
        joined_ref[pl.ds(base, ref.shape[0])] = ref[...]
        base += ref.shape[0]


def finish(message, qb, unary, compat_ref):
    message = message - qb.astype(jnp.float32)
    pairwise = jnp.dot(
        compat_ref[...], message, precision=lax.Precision.HIGHEST,
        preferred_element_type=jnp.float32,
    )
    return normalize(-unary - pairwise), pairwise


def first_part(labels, row_refs, stack_refs, total, tile_ref):
    blocks = [(ref, index) for ref in stack_refs for index in range(ref.shape[0])]
    rows = jnp.concatenate([ref[...] for ref in row_refs], axis=1)

    def exponents(place):
        ref, index = blocks[place]
        columns = product_sides(ref[index][labels:].astype(jnp.float32))[0]
        return lax.dot_general(
            columns, rows, (((0,), (0,)), ((), ())), preferred_element_type=jnp.float32
        )

    ahead = exponents(0)
    for place, (ref, index) in enumerate(blocks):
        exponent = ahead
        if place + 1 < len(blocks):
            ahead = exponents(place + 1)
        tile = jnp.exp(exponent).astype(jnp.bfloat16)
        if place == 0:
            tile_ref[...] = tile
        total = total + jnp.dot(ref[index][:labels], tile, preferred_element_type=jnp.float32)
    return total


def first_opening(labels, *refs):
    total_ref, tile_ref = refs[-2:]
    start = jnp.zeros(total_ref.shape, jnp.float32)
    total_ref[...] = first_part(labels, refs[:2], refs[2:-2], start, tile_ref)


def first_middle(labels, *refs):
    sum_ref, total_ref, tile_ref = refs[-3:]
    total_ref[...] = first_part(labels, refs[:2], refs[2:-3], sum_ref[...], tile_ref)


def first_closing(labels, nears, stacks, *refs):
    row_refs, refs = refs[:2], refs[2:]
    stack_refs, (sum_ref, compat_ref, *refs) = refs[:stacks], refs[stacks:]
    near_refs, refs = refs[:nears], refs[nears:]
    own_refs, (q_ref, tile_ref) = refs[:-2], refs[-2:]
    total = first_part(labels, row_refs, stack_refs, sum_ref[...], tile_ref)
    labels_now = [ref[index][:labels] for ref in own_refs for index in range(ref.shape[0])]
    unary = [near_ref[pl.ds(0, labels), :] for near_ref in near_refs]
    probs, _ = finish(
        total, jnp.concatenate(labels_now, axis=1), jnp.concatenate(unary, axis=1), compat_ref
    )
    q_ref[...] = probs.astype(jnp.bfloat16)


def second_parts(q_ref, *refs):
    count = len(refs) // 2
    for tile_ref, part_ref in zip(refs[:count], refs[count:]):
        part_ref[...] = lax.dot_general(
            q_ref[...], tile_ref[...], (((1,), (1,)), ((), ())),
            preferred_element_type=jnp.float32,
        )


def second_closing(q_ref, near_ref, compat_ref, *refs):
    probs_ref, pairwise_ref = refs[-2:]
    labels, own = probs_ref.shape
    total = refs[0][...]
    for part_ref in refs[1:-2]:
        total = total + part_ref[...]
    unary = near_ref[pl.ds(0, labels), :]
    probs, pairwise = finish(total, q_ref[:, pl.ds(0, own)], unary, compat_ref)
    probs_ref[...] = probs
    pairwise_ref[...] = pairwise


def swap(value, axis, steps):
    count = lax.axis_size(axis)
    pairs = [
        (source, source ^ steps if paired(axis) else (source + steps) % count)
        for source in range(count)
    ]
    return lax.ppermute(value, axis, pairs)


def group_partners(value):
    count = lax.axis_size("grp")
    order = sorted(range(1, count), key=lambda steps: (steps != count // 2, steps))
    return [value] + [swap(value, "grp", steps) for steps in order]


def paired(axis):
    count = lax.axis_size(axis)
    return count & (count - 1) == 0


def send_back(value, steps):
    return swap(value, "blk", steps if paired("blk") else lax.axis_size("blk") - steps)


def small(dims, kind):
    return math.prod(dims) * jnp.dtype(kind).itemsize <= KEPT_BYTES


def call(kernel, out_shapes, *operands):
    return pl.pallas_call(
        kernel,
        out_shape=tuple(out_shapes),
        cost_estimate=pl.CostEstimate(flops=SCHEDULE_COST, transcendentals=0, bytes_accessed=SCHEDULE_COST),
        compiler_params=pltpu.CompilerParams(vmem_limit_bytes=VMEM_LIMIT),
    )(*operands)


def hold(*operands):
    return [
        pltpu.with_memory_space_constraint(operand, pltpu.VMEM)
        if small(operand.shape, operand.dtype) else operand
        for operand in operands
    ]


def kept(dims, kind, copies=1):
    if small((copies,) + dims, kind):
        return pltpu.VMEM(dims, kind)
    return jax.ShapeDtypeStruct(dims, kind)


def shards(unary, member, features, compat):
    labels, own = unary.shape
    nears = lax.axis_size("grp")
    count = lax.axis_size("blk") * nears
    sent, held = call(
        prepare_kernel,
        [kept((labels + 8, own), jnp.float32), kept(compat.shape, jnp.float32)],
        features, member[None], unary, compat,
    )
    near = group_partners(sent)
    half = max(1, nears // 2)
    halves = [
        call(
            functools.partial(pack_kernel, labels),
            [
                kept((len(some), labels + 8, own), jnp.bfloat16),
                kept((AUX, len(some) * own), jnp.bfloat16),
            ],
            *hold(*some),
        )
        for some in (near[:half], near[half:])
    ]
    packed, rows = zip(*halves)
    parts = lax.axis_size("blk")
    tile_kind = kept((own, nears * own), jnp.bfloat16, parts)
    total_kind = kept((labels, nears * own), jnp.float32)
    tiles, totals = [], []

    def first(*stack):
        total, tile = call(
            functools.partial(first_middle if totals else first_opening, labels),
            [total_kind, tile_kind], *hold(*rows, *stack, *totals[-1:]),
        )
        tiles.append(tile)
        totals.append(total)
        return total

    (joined,) = call(
        join_kernel, [kept((nears, labels + 8, own), jnp.bfloat16)], *hold(*packed)
    )
    if paired("blk"):
        steps = list(range(2, parts, 2))
        far = [[swap(some, "blk", step) for step in steps] for some in packed]
        beside = swap(joined, "blk", 1)
        opened = first(*packed)
        early, late = far
        *early, _ = lax.optimization_barrier((*early, opened))
        relayed = [swap(some, "blk", 1) for some in early]
        *late, _ = lax.optimization_barrier((*late, first(beside)))
        stacks = list(zip(early, late))
        stacks += list(zip(relayed, [swap(some, "blk", 1) for some in late]))
        steps = [0, 1] + steps + [step + 1 for step in steps]
    else:
        steps = list(range(parts))
        stacks = [[swap(joined, "blk", step)] for step in steps[1:]]
        first(*packed)
        first(*stacks.pop(0))
    *middle, last = stacks
    for stack in middle:
        first(*stack)
    q_near, tile = call(
        functools.partial(first_closing, labels, nears, len(last)),
        [kept((labels, nears * own), jnp.bfloat16), tile_kind],
        *hold(*rows, *last, totals[-1], held, *near, *packed),
    )
    tiles.append(tile)

    if parts * math.prod(tile_kind.shape) * 2 <= KEPT_BYTES:
        tiles = hold(*tiles)
    part_kind = kept((labels, own), jnp.float32)
    far = call(second_parts, [part_kind] * (parts - 2), *hold(q_near), *tiles[2:])
    if far:
        q_near, *far = lax.optimization_barrier((q_near, *far))
    here, beside = call(second_parts, [part_kind] * 2, *hold(q_near), *tiles[:2])
    arrived = [send_back(part, step) for part, step in zip([beside, *far], steps[1:])]
    return call(
        second_closing,
        [jax.ShapeDtypeStruct((labels, own), jnp.float32)] * 2,
        *hold(q_near, sent, held, here, *arrived),
    )


def solution(mesh):
    in_specs = (P(None, ("scene", "blk", "grp")), P(("scene", "blk", "grp")), P(None, "scene"), P())
    out_specs = (P(None, ("scene", "blk", "grp")), P(None, ("scene", "blk", "grp")))
    return jax.shard_map(shards, mesh=mesh, in_specs=in_specs, out_specs=out_specs, check_vma=False)
```

```python
import functools
import math

import jax
import jax.numpy as jnp
from jax import lax
from jax.experimental import pallas as pl
from jax.experimental.pallas import tpu as pltpu
from jax.sharding import PartitionSpec as P

AUX = 16
LANES = 128
VMEM_LIMIT = 56 * 1024 * 1024
KEPT_BYTES = 4 * 1024 * 1024
SCHEDULE_COST = 10 ** 10


def normalize(logits):
    raised = jnp.exp(logits)
    return raised / jnp.sum(raised, axis=0, keepdims=True)


def three_parts(value):
    high = value.astype(jnp.bfloat16).astype(jnp.float32)
    middle = (value - high).astype(jnp.bfloat16).astype(jnp.float32)
    return [high, middle, value - high - middle]


def pick_features(features_ref, member):
    feats, points = features_ref.shape
    own = member.shape[1]
    groups = points // LANES
    wide = features_ref[...].astype(jnp.float32)
    wide = jnp.concatenate([wide, jnp.zeros((8 - feats, points), jnp.float32)], axis=0)
    table = jnp.concatenate(
        [wide[:, group * LANES:(group + 1) * LANES] for group in range(groups)], axis=0
    ).astype(jnp.bfloat16)
    lane = lax.broadcasted_iota(jnp.int32, (LANES, own), 0)
    chosen = jnp.where(lane == member % LANES, 1.0, 0.0).astype(jnp.bfloat16)
    found = jnp.dot(table, chosen, preferred_element_type=jnp.float32)
    found = found.reshape(groups, 8, own)
    group = lax.broadcasted_iota(jnp.int32, (groups, 8, own), 0)
    return jnp.sum(jnp.where(group == (member // LANES)[None], found, 0.0), axis=0)


def prepare_kernel(features_ref, member_ref, unary_ref, compat_ref, sent_ref, held_ref):
    labels = unary_ref.shape[0]
    sent_ref[pl.ds(0, labels), :] = unary_ref[...]
    sent_ref[pl.ds(labels, 8), :] = pick_features(features_ref, member_ref[...])
    held_ref[...] = compat_ref[...]


def half_norms(feats):
    return three_parts(-0.5 * jnp.sum(feats * feats, axis=0, keepdims=True))


def product_sides(feats):
    own = feats.shape[1]
    norms = half_norms(feats)
    ones = jnp.ones((3, own), jnp.float32)
    spare = jnp.zeros((AUX - 8 - 6, own), jnp.float32)
    columns = jnp.concatenate([feats] + norms + [ones, spare], axis=0)
    rows = jnp.concatenate([feats, ones] + norms + [spare], axis=0)
    return columns.astype(jnp.bfloat16), rows.astype(jnp.bfloat16)


def pack_kernel(labels, *refs):
    near_refs, packed_ref, rows_ref = refs[:-2], refs[-2], refs[-1]
    for place, near_ref in enumerate(near_refs):
        own = near_ref.shape[1]
        feats = near_ref[pl.ds(labels, 8), :]
        probs = normalize(-near_ref[pl.ds(0, labels), :])
        packed_ref[place] = jnp.concatenate([probs, feats], axis=0).astype(jnp.bfloat16)
        rows_ref[:, pl.ds(place * own, own)] = product_sides(feats)[1]


def join_kernel(*refs):
    joined_ref = refs[-1]
    base = 0
    for ref in refs[:-1]:
        joined_ref[pl.ds(base, ref.shape[0])] = ref[...]
        base += ref.shape[0]


def finish(message, qb, unary, compat_ref):
    message = message - qb.astype(jnp.float32)
    pairwise = jnp.dot(
        compat_ref[...], message, precision=lax.Precision.HIGHEST,
        preferred_element_type=jnp.float32,
    )
    return normalize(-unary - pairwise), pairwise


def first_part(labels, row_refs, stack_refs, total, tile_ref):
    blocks = [(ref, index) for ref in stack_refs for index in range(ref.shape[0])]
    rows = jnp.concatenate([ref[...] for ref in row_refs], axis=1)

    def exponents(place):
        ref, index = blocks[place]
        columns = product_sides(ref[index][labels:].astype(jnp.float32))[0]
        return lax.dot_general(
            columns, rows, (((0,), (0,)), ((), ())), preferred_element_type=jnp.float32
        )

    ahead = exponents(0)
    for place, (ref, index) in enumerate(blocks):
        exponent = ahead
        if place + 1 < len(blocks):
            ahead = exponents(place + 1)
        tile = jnp.exp(exponent).astype(jnp.bfloat16)
        if place == 0:
            tile_ref[...] = tile
        total = total + jnp.dot(ref[index][:labels], tile, preferred_element_type=jnp.float32)
    return total


def first_opening(labels, *refs):
    total_ref, tile_ref = refs[-2:]
    start = jnp.zeros(total_ref.shape, jnp.float32)
    total_ref[...] = first_part(labels, refs[:2], refs[2:-2], start, tile_ref)


def first_middle(labels, *refs):
    sum_ref, total_ref, tile_ref = refs[-3:]
    total_ref[...] = first_part(labels, refs[:2], refs[2:-3], sum_ref[...], tile_ref)


def first_closing(labels, nears, stacks, *refs):
    row_refs, refs = refs[:2], refs[2:]
    stack_refs, (sum_ref, compat_ref, *refs) = refs[:stacks], refs[stacks:]
    near_refs, refs = refs[:nears], refs[nears:]
    own_refs, (q_ref, tile_ref) = refs[:-2], refs[-2:]
    total = first_part(labels, row_refs, stack_refs, sum_ref[...], tile_ref)
    labels_now = [ref[index][:labels] for ref in own_refs for index in range(ref.shape[0])]
    unary = [near_ref[pl.ds(0, labels), :] for near_ref in near_refs]
    probs, _ = finish(
        total, jnp.concatenate(labels_now, axis=1), jnp.concatenate(unary, axis=1), compat_ref
    )
    q_ref[...] = probs.astype(jnp.bfloat16)


def second_parts(q_ref, *refs):
    count = len(refs) // 2
    for tile_ref, part_ref in zip(refs[:count], refs[count:]):
        part_ref[...] = lax.dot_general(
            q_ref[...], tile_ref[...], (((1,), (1,)), ((), ())),
            preferred_element_type=jnp.float32,
        )


def second_closing(q_ref, near_ref, compat_ref, *refs):
    probs_ref, pairwise_ref = refs[-2:]
    labels, own = probs_ref.shape
    total = refs[0][...]
    for part_ref in refs[1:-2]:
        total = total + part_ref[...]
    unary = near_ref[pl.ds(0, labels), :]
    probs, pairwise = finish(total, q_ref[:, pl.ds(0, own)], unary, compat_ref)
    probs_ref[...] = probs
    pairwise_ref[...] = pairwise


def swap(value, blk_steps, grp_steps=0):
    blks, grps = lax.axis_size("blk"), lax.axis_size("grp")
    pairs = [
        (
            blk * grps + grp,
            (blk ^ blk_steps if paired("blk") else (blk + blk_steps) % blks) * grps
            + (grp ^ grp_steps if paired("grp") else (grp + grp_steps) % grps),
        )
        for blk in range(blks)
        for grp in range(grps)
    ]
    return lax.ppermute(value, ("blk", "grp"), pairs)


def group_partners(value):
    count = lax.axis_size("grp")
    order = sorted(range(1, count), key=lambda steps: (steps != count // 2, steps))
    crossed = paired("blk") and paired("grp") and lax.axis_size("blk") > 1
    return [value] + [swap(value, steps % 2 if crossed else 0, steps) for steps in order]


def paired(axis):
    count = lax.axis_size(axis)
    return count & (count - 1) == 0


def send_back(value, steps):
    return swap(value, steps if paired("blk") else lax.axis_size("blk") - steps)


def small(dims, kind):
    return math.prod(dims) * jnp.dtype(kind).itemsize <= KEPT_BYTES


def call(kernel, out_shapes, *operands):
    return pl.pallas_call(
        kernel,
        out_shape=tuple(out_shapes),
        cost_estimate=pl.CostEstimate(flops=SCHEDULE_COST, transcendentals=0, bytes_accessed=SCHEDULE_COST),
        compiler_params=pltpu.CompilerParams(vmem_limit_bytes=VMEM_LIMIT),
    )(*operands)


def hold(*operands):
    return [
        pltpu.with_memory_space_constraint(operand, pltpu.VMEM)
        if small(operand.shape, operand.dtype) else operand
        for operand in operands
    ]


def kept(dims, kind, copies=1):
    if small((copies,) + dims, kind):
        return pltpu.VMEM(dims, kind)
    return jax.ShapeDtypeStruct(dims, kind)


def shards(unary, member, features, compat):
    labels, own = unary.shape
    nears = lax.axis_size("grp")
    count = lax.axis_size("blk") * nears
    sent, held = call(
        prepare_kernel,
        [kept((labels + 8, own), jnp.float32), kept(compat.shape, jnp.float32)],
        features, member[None], unary, compat,
    )
    near = group_partners(sent)
    half = max(1, nears // 2)
    halves = [
        call(
            functools.partial(pack_kernel, labels),
            [
                kept((len(some), labels + 8, own), jnp.bfloat16),
                kept((AUX, len(some) * own), jnp.bfloat16),
            ],
            *hold(*some),
        )
        for some in (near[:half], near[half:])
    ]
    packed, rows = zip(*halves)
    parts = lax.axis_size("blk")
    tile_kind = kept((own, nears * own), jnp.bfloat16, parts)
    total_kind = kept((labels, nears * own), jnp.float32)
    tiles, totals = [], []

    def first(*stack):
        total, tile = call(
            functools.partial(first_middle if totals else first_opening, labels),
            [total_kind, tile_kind], *hold(*rows, *stack, *totals[-1:]),
        )
        tiles.append(tile)
        totals.append(total)
        return total

    (joined,) = call(
        join_kernel, [kept((nears, labels + 8, own), jnp.bfloat16)], *hold(*packed)
    )
    if paired("blk"):
        steps = list(range(3, parts, 2))
        far = [[swap(some, step) for step in steps] for some in packed]
        beside = swap(joined, 1)
        opened = first(*packed)
        early, late = far
        *early, _ = lax.optimization_barrier((*early, opened))
        relayed = [swap(some, 1) for some in early]
        *late, _ = lax.optimization_barrier((*late, first(beside)))
        stacks = list(zip(early, late))
        stacks += list(zip(relayed, [swap(some, 1) for some in late]))
        steps = [0, 1] + steps + [step - 1 for step in steps]
    else:
        steps = list(range(parts))
        stacks = [[swap(joined, step)] for step in steps[1:]]
        first(*packed)
        first(*stacks.pop(0))
    *middle, last = stacks
    for stack in middle:
        first(*stack)
    q_near, tile = call(
        functools.partial(first_closing, labels, nears, len(last)),
        [kept((labels, nears * own), jnp.bfloat16), tile_kind],
        *hold(*rows, *last, totals[-1], held, *near, *packed),
    )
    tiles.append(tile)

    if parts * math.prod(tile_kind.shape) * 2 <= KEPT_BYTES:
        tiles = hold(*tiles)
    part_kind = kept((labels, own), jnp.float32)
    far = call(second_parts, [part_kind] * (parts - 2), *hold(q_near), *tiles[2:])
    if far:
        q_near, *far = lax.optimization_barrier((q_near, *far))
    here, beside = call(second_parts, [part_kind] * 2, *hold(q_near), *tiles[:2])
    sent_parts = dict(zip(steps[1:], [beside, *far]))
    arrived = [send_back(sent_parts[step], step) for step in range(1, parts)]
    return call(
        second_closing,
        [jax.ShapeDtypeStruct((labels, own), jnp.float32)] * 2,
        *hold(q_near, sent, held, here, *arrived),
    )


def solution(mesh):
    in_specs = (P(None, ("scene", "blk", "grp")), P(("scene", "blk", "grp")), P(None, "scene"), P())
    out_specs = (P(None, ("scene", "blk", "grp")), P(None, ("scene", "blk", "grp")))
    return jax.shard_map(shards, mesh=mesh, in_specs=in_specs, out_specs=out_specs, check_vma=False)
```

```python
import functools
import math

import jax
import jax.numpy as jnp
from jax import lax
from jax.experimental import pallas as pl
from jax.experimental.pallas import tpu as pltpu
from jax.sharding import PartitionSpec as P

AUX = 16
LANES = 128
VMEM_LIMIT = 56 * 1024 * 1024
KEPT_BYTES = 4 * 1024 * 1024
SCHEDULE_COST = 10 ** 10


def normalize(logits):
    raised = jnp.exp(logits)
    return raised / jnp.sum(raised, axis=0, keepdims=True)


def three_parts(value):
    high = value.astype(jnp.bfloat16).astype(jnp.float32)
    middle = (value - high).astype(jnp.bfloat16).astype(jnp.float32)
    return [high, middle, value - high - middle]


def pick_features(features_ref, member):
    feats, points = features_ref.shape
    own = member.shape[1]
    groups = points // LANES
    wide = features_ref[...].astype(jnp.float32)
    wide = jnp.concatenate([wide, jnp.zeros((8 - feats, points), jnp.float32)], axis=0)
    table = jnp.concatenate(
        [wide[:, group * LANES:(group + 1) * LANES] for group in range(groups)], axis=0
    ).astype(jnp.bfloat16)
    lane = lax.broadcasted_iota(jnp.int32, (LANES, own), 0)
    chosen = jnp.where(lane == member % LANES, 1.0, 0.0).astype(jnp.bfloat16)
    found = jnp.dot(table, chosen, preferred_element_type=jnp.float32)
    found = found.reshape(groups, 8, own)
    group = lax.broadcasted_iota(jnp.int32, (groups, 8, own), 0)
    return jnp.sum(jnp.where(group == (member // LANES)[None], found, 0.0), axis=0)


def prepare_kernel(features_ref, member_ref, unary_ref, compat_ref, sent_ref, held_ref):
    labels = unary_ref.shape[0]
    sent_ref[pl.ds(0, labels), :] = unary_ref[...]
    sent_ref[pl.ds(labels, 8), :] = pick_features(features_ref, member_ref[...])
    held_ref[...] = compat_ref[...]


def half_norms(feats):
    return three_parts(-0.5 * jnp.sum(feats * feats, axis=0, keepdims=True))


def product_sides(feats):
    own = feats.shape[1]
    norms = half_norms(feats)
    ones = jnp.ones((3, own), jnp.float32)
    spare = jnp.zeros((AUX - 8 - 6, own), jnp.float32)
    columns = jnp.concatenate([feats] + norms + [ones, spare], axis=0)
    rows = jnp.concatenate([feats, ones] + norms + [spare], axis=0)
    return columns.astype(jnp.bfloat16), rows.astype(jnp.bfloat16)


def pack_kernel(labels, *refs):
    near_refs, packed_ref, rows_ref = refs[:-2], refs[-2], refs[-1]
    for place, near_ref in enumerate(near_refs):
        own = near_ref.shape[1]
        feats = near_ref[pl.ds(labels, 8), :]
        probs = normalize(-near_ref[pl.ds(0, labels), :])
        packed_ref[place] = jnp.concatenate([probs, feats], axis=0).astype(jnp.bfloat16)
        rows_ref[:, pl.ds(place * own, own)] = product_sides(feats)[1]


def join_kernel(*refs):
    joined_ref = refs[-1]
    base = 0
    for ref in refs[:-1]:
        joined_ref[pl.ds(base, ref.shape[0])] = ref[...]
        base += ref.shape[0]


def finish(message, qb, unary, compat_ref):
    message = message - qb.astype(jnp.float32)
    pairwise = jnp.dot(
        compat_ref[...], message, precision=lax.Precision.HIGHEST,
        preferred_element_type=jnp.float32,
    )
    return normalize(-unary - pairwise), pairwise


def first_part(labels, row_refs, stack_refs, total, tile_ref):
    blocks = [(ref, index) for ref in stack_refs for index in range(ref.shape[0])]
    rows = jnp.concatenate([ref[...] for ref in row_refs], axis=1)

    def exponents(place):
        ref, index = blocks[place]
        columns = product_sides(ref[index][labels:].astype(jnp.float32))[0]
        return lax.dot_general(
            columns, rows, (((0,), (0,)), ((), ())), preferred_element_type=jnp.float32
        )

    ahead = exponents(0)
    for place, (ref, index) in enumerate(blocks):
        exponent = ahead
        if place + 1 < len(blocks):
            ahead = exponents(place + 1)
        tile = jnp.exp(exponent).astype(jnp.bfloat16)
        if place == 0:
            tile_ref[...] = tile
        total = total + jnp.dot(ref[index][:labels], tile, preferred_element_type=jnp.float32)
    return total


def first_opening(labels, *refs):
    total_ref, tile_ref = refs[-2:]
    start = jnp.zeros(total_ref.shape, jnp.float32)
    total_ref[...] = first_part(labels, refs[:2], refs[2:-2], start, tile_ref)


def first_middle(labels, *refs):
    sum_ref, total_ref, tile_ref = refs[-3:]
    total_ref[...] = first_part(labels, refs[:2], refs[2:-3], sum_ref[...], tile_ref)


def first_closing(labels, nears, stacks, *refs):
    row_refs, refs = refs[:2], refs[2:]
    stack_refs, (sum_ref, compat_ref, *refs) = refs[:stacks], refs[stacks:]
    near_refs, refs = refs[:nears], refs[nears:]
    own_refs, (q_ref, tile_ref) = refs[:-2], refs[-2:]
    total = first_part(labels, row_refs, stack_refs, sum_ref[...], tile_ref)
    labels_now = [ref[index][:labels] for ref in own_refs for index in range(ref.shape[0])]
    unary = [near_ref[pl.ds(0, labels), :] for near_ref in near_refs]
    probs, _ = finish(
        total, jnp.concatenate(labels_now, axis=1), jnp.concatenate(unary, axis=1), compat_ref
    )
    q_ref[...] = probs.astype(jnp.bfloat16)


def second_parts(q_ref, *refs):
    count = len(refs) // 2
    for tile_ref, part_ref in zip(refs[:count], refs[count:]):
        part_ref[...] = lax.dot_general(
            q_ref[...], tile_ref[...], (((1,), (1,)), ((), ())),
            preferred_element_type=jnp.float32,
        )


def second_closing(q_ref, near_ref, compat_ref, *refs):
    probs_ref, pairwise_ref = refs[-2:]
    labels, own = probs_ref.shape
    total = refs[0][...]
    for part_ref in refs[1:-2]:
        total = total + part_ref[...]
    unary = near_ref[pl.ds(0, labels), :]
    probs, pairwise = finish(total, q_ref[:, pl.ds(0, own)], unary, compat_ref)
    probs_ref[...] = probs
    pairwise_ref[...] = pairwise


def swap(value, blk_steps, grp_steps=0):
    blks, grps = lax.axis_size("blk"), lax.axis_size("grp")
    pairs = [
        (
            blk * grps + grp,
            (blk ^ blk_steps if paired("blk") else (blk + blk_steps) % blks) * grps
            + (grp ^ grp_steps if paired("grp") else (grp + grp_steps) % grps),
        )
        for blk in range(blks)
        for grp in range(grps)
    ]
    return lax.ppermute(value, ("blk", "grp"), pairs)


def group_partners(value):
    count = lax.axis_size("grp")
    order = sorted(range(1, count), key=lambda steps: (steps != count // 2, steps))
    crossed = paired("blk") and paired("grp") and lax.axis_size("blk") > 1
    return [value] + [swap(value, steps % 2 if crossed else 0, steps) for steps in order]


def paired(axis):
    count = lax.axis_size(axis)
    return count & (count - 1) == 0


def send_back(value, steps):
    return swap(value, steps if paired("blk") else lax.axis_size("blk") - steps)


def small(dims, kind):
    return math.prod(dims) * jnp.dtype(kind).itemsize <= KEPT_BYTES


def call(kernel, out_shapes, *operands):
    return pl.pallas_call(
        kernel,
        out_shape=tuple(out_shapes),
        cost_estimate=pl.CostEstimate(flops=SCHEDULE_COST, transcendentals=0, bytes_accessed=SCHEDULE_COST),
        compiler_params=pltpu.CompilerParams(vmem_limit_bytes=VMEM_LIMIT),
    )(*operands)


def hold(*operands):
    return [
        pltpu.with_memory_space_constraint(operand, pltpu.VMEM)
        if small(operand.shape, operand.dtype) else operand
        for operand in operands
    ]


def kept(dims, kind, copies=1):
    if small((copies,) + dims, kind):
        return pltpu.VMEM(dims, kind)
    return jax.ShapeDtypeStruct(dims, kind)


def shards(unary, member, features, compat):
    labels, own = unary.shape
    nears = lax.axis_size("grp")
    count = lax.axis_size("blk") * nears
    sent, held = call(
        prepare_kernel,
        [kept((labels + 8, own), jnp.float32), kept(compat.shape, jnp.float32)],
        features, member[None], unary, compat,
    )
    near = group_partners(sent)
    half = max(1, nears // 2)
    halves = [
        call(
            functools.partial(pack_kernel, labels),
            [
                kept((len(some), labels + 8, own), jnp.bfloat16),
                kept((AUX, len(some) * own), jnp.bfloat16),
            ],
            *hold(*some),
        )
        for some in (near[:half], near[half:])
    ]
    packed, rows = zip(*halves)
    parts = lax.axis_size("blk")
    tile_kind = kept((own, nears * own), jnp.bfloat16, parts)
    total_kind = kept((labels, nears * own), jnp.float32)
    tiles, totals = [], []

    def first(*stack):
        total, tile = call(
            functools.partial(first_middle if totals else first_opening, labels),
            [total_kind, tile_kind], *hold(*rows, *stack, *totals[-1:]),
        )
        tiles.append(tile)
        totals.append(total)
        return total

    def join(some):
        kind = kept((nears, labels + 8, own), jnp.bfloat16)
        return call(join_kernel, [kind], *hold(*some))[0]

    joined = join(packed)
    if paired("blk"):
        steps = list(range(3, parts, 2))
        far = [[swap(some, step) for step in steps] for some in packed]
        beside = swap(joined, 1)
        first(*packed)
        early, late = far
        *late, _ = lax.optimization_barrier((*late, first(beside)))
        stacks = list(zip(early, late))
        stacks += [(swap(join(some), 1),) for some in stacks]
        steps = [0, 1] + steps + [step - 1 for step in steps]
    else:
        steps = list(range(parts))
        stacks = [[swap(joined, step)] for step in steps[1:]]
        first(*packed)
        first(*stacks.pop(0))
    *middle, last = stacks
    for stack in middle:
        first(*stack)
    q_near, tile = call(
        functools.partial(first_closing, labels, nears, len(last)),
        [kept((labels, nears * own), jnp.bfloat16), tile_kind],
        *hold(*rows, *last, totals[-1], held, *near, *packed),
    )
    tiles.append(tile)

    if parts * math.prod(tile_kind.shape) * 2 <= KEPT_BYTES:
        tiles = hold(*tiles)
    part_kind = kept((labels, own), jnp.float32)
    far = call(second_parts, [part_kind] * (parts - 2), *hold(q_near), *tiles[2:])
    if far:
        q_near, *far = lax.optimization_barrier((q_near, *far))
    here, beside = call(second_parts, [part_kind] * 2, *hold(q_near), *tiles[:2])
    sent_parts = dict(zip(steps[1:], [beside, *far]))
    arrived = [send_back(sent_parts[step], step) for step in range(1, parts)]
    return call(
        second_closing,
        [jax.ShapeDtypeStruct((labels, own), jnp.float32)] * 2,
        *hold(q_near, sent, held, here, *arrived),
    )


def solution(mesh):
    in_specs = (P(None, ("scene", "blk", "grp")), P(("scene", "blk", "grp")), P(None, "scene"), P())
    out_specs = (P(None, ("scene", "blk", "grp")), P(None, ("scene", "blk", "grp")))
    return jax.shard_map(shards, mesh=mesh, in_specs=in_specs, out_specs=out_specs, check_vma=False)
```

```python
import functools
import math

import jax
import jax.numpy as jnp
from jax import lax
from jax.experimental import pallas as pl
from jax.experimental.pallas import tpu as pltpu
from jax.sharding import PartitionSpec as P

AUX = 16
LANES = 128
VMEM_LIMIT = 56 * 1024 * 1024
KEPT_BYTES = 4 * 1024 * 1024
SCHEDULE_COST = 10 ** 10


def normalize(logits):
    raised = jnp.exp(logits)
    return raised / jnp.sum(raised, axis=0, keepdims=True)


def three_parts(value):
    high = value.astype(jnp.bfloat16).astype(jnp.float32)
    middle = (value - high).astype(jnp.bfloat16).astype(jnp.float32)
    return [high, middle, value - high - middle]


def pick_features(features_ref, member):
    feats, points = features_ref.shape
    own = member.shape[1]
    groups = points // LANES
    wide = features_ref[...].astype(jnp.float32)
    wide = jnp.concatenate([wide, jnp.zeros((8 - feats, points), jnp.float32)], axis=0)
    table = jnp.concatenate(
        [wide[:, group * LANES:(group + 1) * LANES] for group in range(groups)], axis=0
    ).astype(jnp.bfloat16)
    lane = lax.broadcasted_iota(jnp.int32, (LANES, own), 0)
    chosen = jnp.where(lane == member % LANES, 1.0, 0.0).astype(jnp.bfloat16)
    found = jnp.dot(table, chosen, preferred_element_type=jnp.float32)
    found = found.reshape(groups, 8, own)
    group = lax.broadcasted_iota(jnp.int32, (groups, 8, own), 0)
    return jnp.sum(jnp.where(group == (member // LANES)[None], found, 0.0), axis=0)


def prepare_kernel(features_ref, member_ref, unary_ref, compat_ref, sent_ref, held_ref):
    labels = unary_ref.shape[0]
    sent_ref[pl.ds(0, labels), :] = unary_ref[...]
    sent_ref[pl.ds(labels, 8), :] = pick_features(features_ref, member_ref[...])
    held_ref[...] = compat_ref[...]


def half_norms(feats):
    return three_parts(-0.5 * jnp.sum(feats * feats, axis=0, keepdims=True))


def product_sides(feats):
    own = feats.shape[1]
    norms = half_norms(feats)
    ones = jnp.ones((3, own), jnp.float32)
    spare = jnp.zeros((AUX - 8 - 6, own), jnp.float32)
    columns = jnp.concatenate([feats] + norms + [ones, spare], axis=0)
    rows = jnp.concatenate([feats, ones] + norms + [spare], axis=0)
    return columns.astype(jnp.bfloat16), rows.astype(jnp.bfloat16)


def pack_kernel(labels, *refs):
    near_refs, packed_ref, rows_ref = refs[:-2], refs[-2], refs[-1]
    for place, near_ref in enumerate(near_refs):
        own = near_ref.shape[1]
        feats = near_ref[pl.ds(labels, 8), :]
        probs = normalize(-near_ref[pl.ds(0, labels), :])
        packed_ref[place] = jnp.concatenate([probs, feats], axis=0).astype(jnp.bfloat16)
        rows_ref[:, pl.ds(place * own, own)] = product_sides(feats)[1]


def join_kernel(*refs):
    joined_ref = refs[-1]
    base = 0
    for ref in refs[:-1]:
        joined_ref[pl.ds(base, ref.shape[0])] = ref[...]
        base += ref.shape[0]


def finish(message, qb, unary, compat_ref):
    message = message - qb.astype(jnp.float32)
    pairwise = jnp.dot(
        compat_ref[...], message, precision=lax.Precision.HIGHEST,
        preferred_element_type=jnp.float32,
    )
    return normalize(-unary - pairwise), pairwise


def first_part(labels, row_refs, stack_refs, total, tile_ref):
    blocks = [(ref, index) for ref in stack_refs for index in range(ref.shape[0])]
    rows = jnp.concatenate([ref[...] for ref in row_refs], axis=1)

    def exponents(place):
        ref, index = blocks[place]
        columns = product_sides(ref[index][labels:].astype(jnp.float32))[0]
        return lax.dot_general(
            columns, rows, (((0,), (0,)), ((), ())), preferred_element_type=jnp.float32
        )

    ahead = exponents(0)
    for place, (ref, index) in enumerate(blocks):
        exponent = ahead
        if place + 1 < len(blocks):
            ahead = exponents(place + 1)
        tile = jnp.exp(exponent).astype(jnp.bfloat16)
        if place == 0:
            tile_ref[...] = tile
        total = total + jnp.dot(ref[index][:labels], tile, preferred_element_type=jnp.float32)
    return total


def first_opening(labels, *refs):
    total_ref, tile_ref = refs[-2:]
    start = jnp.zeros(total_ref.shape, jnp.float32)
    total_ref[...] = first_part(labels, refs[:2], refs[2:-2], start, tile_ref)


def first_middle(labels, *refs):
    sum_ref, total_ref, tile_ref = refs[-3:]
    total_ref[...] = first_part(labels, refs[:2], refs[2:-3], sum_ref[...], tile_ref)


def first_closing(labels, nears, stacks, *refs):
    row_refs, refs = refs[:2], refs[2:]
    stack_refs, (sum_ref, compat_ref, *refs) = refs[:stacks], refs[stacks:]
    near_refs, refs = refs[:nears], refs[nears:]
    own_refs, (q_ref, tile_ref) = refs[:-2], refs[-2:]
    total = first_part(labels, row_refs, stack_refs, sum_ref[...], tile_ref)
    labels_now = [ref[index][:labels] for ref in own_refs for index in range(ref.shape[0])]
    unary = [near_ref[pl.ds(0, labels), :] for near_ref in near_refs]
    probs, _ = finish(
        total, jnp.concatenate(labels_now, axis=1), jnp.concatenate(unary, axis=1), compat_ref
    )
    q_ref[...] = probs.astype(jnp.bfloat16)


def second_parts(q_ref, *refs):
    count = len(refs) // 2
    for tile_ref, part_ref in zip(refs[:count], refs[count:]):
        part_ref[...] = lax.dot_general(
            tile_ref[...], q_ref[...], (((1,), (1,)), ((), ())),
            preferred_element_type=jnp.float32,
        ).T


def second_closing(q_ref, near_ref, compat_ref, *refs):
    probs_ref, pairwise_ref = refs[-2:]
    labels, own = probs_ref.shape
    total = refs[0][...]
    for part_ref in refs[1:-2]:
        total = total + part_ref[...]
    unary = near_ref[pl.ds(0, labels), :]
    probs, pairwise = finish(total, q_ref[:, pl.ds(0, own)], unary, compat_ref)
    probs_ref[...] = probs
    pairwise_ref[...] = pairwise


def swap(value, blk_steps, grp_steps=0):
    blks, grps = lax.axis_size("blk"), lax.axis_size("grp")
    pairs = [
        (
            blk * grps + grp,
            (blk ^ blk_steps if paired("blk") else (blk + blk_steps) % blks) * grps
            + (grp ^ grp_steps if paired("grp") else (grp + grp_steps) % grps),
        )
        for blk in range(blks)
        for grp in range(grps)
    ]
    return lax.ppermute(value, ("blk", "grp"), pairs)


def group_partners(value):
    count = lax.axis_size("grp")
    order = sorted(range(1, count), key=lambda steps: (steps != count // 2, steps))
    crossed = paired("blk") and paired("grp") and lax.axis_size("blk") > 1
    return [value] + [swap(value, steps % 2 if crossed else 0, steps) for steps in order]


def paired(axis):
    count = lax.axis_size(axis)
    return count & (count - 1) == 0


def send_back(value, steps):
    return swap(value, steps if paired("blk") else lax.axis_size("blk") - steps)


def small(dims, kind):
    return math.prod(dims) * jnp.dtype(kind).itemsize <= KEPT_BYTES


def call(kernel, out_shapes, *operands):
    return pl.pallas_call(
        kernel,
        out_shape=tuple(out_shapes),
        cost_estimate=pl.CostEstimate(flops=SCHEDULE_COST, transcendentals=0, bytes_accessed=SCHEDULE_COST),
        compiler_params=pltpu.CompilerParams(vmem_limit_bytes=VMEM_LIMIT),
    )(*operands)


def hold(*operands):
    return [
        pltpu.with_memory_space_constraint(operand, pltpu.VMEM)
        if small(operand.shape, operand.dtype) else operand
        for operand in operands
    ]


def kept(dims, kind, copies=1):
    if small((copies,) + dims, kind):
        return pltpu.VMEM(dims, kind)
    return jax.ShapeDtypeStruct(dims, kind)


def shards(unary, member, features, compat):
    labels, own = unary.shape
    nears = lax.axis_size("grp")
    count = lax.axis_size("blk") * nears
    sent, held = call(
        prepare_kernel,
        [kept((labels + 8, own), jnp.float32), kept(compat.shape, jnp.float32)],
        features, member[None], unary, compat,
    )
    near = group_partners(sent)
    half = max(1, nears // 2)
    halves = [
        call(
            functools.partial(pack_kernel, labels),
            [
                kept((len(some), labels + 8, own), jnp.bfloat16),
                kept((AUX, len(some) * own), jnp.bfloat16),
            ],
            *hold(*some),
        )
        for some in (near[:half], near[half:])
    ]
    packed, rows = zip(*halves)
    parts = lax.axis_size("blk")
    tile_kind = kept((own, nears * own), jnp.bfloat16, parts)
    total_kind = kept((labels, nears * own), jnp.float32)
    tiles, totals = [], []

    def first(*stack):
        total, tile = call(
            functools.partial(first_middle if totals else first_opening, labels),
            [total_kind, tile_kind], *hold(*rows, *stack, *totals[-1:]),
        )
        tiles.append(tile)
        totals.append(total)
        return total

    def join(some):
        kind = kept((nears, labels + 8, own), jnp.bfloat16)
        return call(join_kernel, [kind], *hold(*some))[0]

    joined = join(packed)
    if paired("blk"):
        steps = list(range(3, parts, 2))
        far = [[swap(some, step) for step in steps] for some in packed]
        beside = swap(joined, 1)
        first(*packed)
        early, late = far
        *late, _ = lax.optimization_barrier((*late, first(beside)))
        stacks = list(zip(early, late))
        stacks += [(swap(join(some), 1),) for some in stacks]
        steps = [0, 1] + steps + [step - 1 for step in steps]
    else:
        steps = list(range(parts))
        stacks = [[swap(joined, step)] for step in steps[1:]]
        first(*packed)
        first(*stacks.pop(0))
    *middle, last = stacks
    for stack in middle:
        first(*stack)
    q_near, tile = call(
        functools.partial(first_closing, labels, nears, len(last)),
        [kept((labels, nears * own), jnp.bfloat16), tile_kind],
        *hold(*rows, *last, totals[-1], held, *near, *packed),
    )
    tiles.append(tile)

    if parts * math.prod(tile_kind.shape) * 2 <= KEPT_BYTES:
        tiles = hold(*tiles)
    part_kind = kept((labels, own), jnp.float32)
    far = call(second_parts, [part_kind] * (parts - 2), *hold(q_near), *tiles[2:])
    if far:
        q_near, *far = lax.optimization_barrier((q_near, *far))
    here, beside = call(second_parts, [part_kind] * 2, *hold(q_near), *tiles[:2])
    sent_parts = dict(zip(steps[1:], [beside, *far]))
    arrived = [send_back(sent_parts[step], step) for step in range(1, parts)]
    return call(
        second_closing,
        [jax.ShapeDtypeStruct((labels, own), jnp.float32)] * 2,
        *hold(q_near, sent, held, here, *arrived),
    )


def solution(mesh):
    in_specs = (P(None, ("scene", "blk", "grp")), P(("scene", "blk", "grp")), P(None, "scene"), P())
    out_specs = (P(None, ("scene", "blk", "grp")), P(None, ("scene", "blk", "grp")))
    return jax.shard_map(shards, mesh=mesh, in_specs=in_specs, out_specs=out_specs, check_vma=False)
```

```python
import functools
import math

import jax
import jax.numpy as jnp
from jax import lax
from jax.experimental import pallas as pl
from jax.experimental.pallas import tpu as pltpu
from jax.sharding import PartitionSpec as P

AUX = 16
LANES = 128
VMEM_LIMIT = 56 * 1024 * 1024
KEPT_BYTES = 4 * 1024 * 1024
SCHEDULE_COST = 10 ** 10


def normalize(logits):
    raised = jnp.exp(logits)
    return raised / jnp.sum(raised, axis=0, keepdims=True)


def three_parts(value):
    high = value.astype(jnp.bfloat16).astype(jnp.float32)
    middle = (value - high).astype(jnp.bfloat16).astype(jnp.float32)
    return [high, middle, value - high - middle]


def pick_features(features_ref, member):
    feats, points = features_ref.shape
    own = member.shape[1]
    groups = points // LANES
    wide = features_ref[...].astype(jnp.float32)
    wide = jnp.concatenate([wide, jnp.zeros((8 - feats, points), jnp.float32)], axis=0)
    table = jnp.concatenate(
        [wide[:, group * LANES:(group + 1) * LANES] for group in range(groups)], axis=0
    ).astype(jnp.bfloat16)
    lane = lax.broadcasted_iota(jnp.int32, (LANES, own), 0)
    chosen = jnp.where(lane == member % LANES, 1.0, 0.0).astype(jnp.bfloat16)
    found = jnp.dot(table, chosen, preferred_element_type=jnp.float32)
    found = found.reshape(groups, 8, own)
    group = lax.broadcasted_iota(jnp.int32, (groups, 8, own), 0)
    return jnp.sum(jnp.where(group == (member // LANES)[None], found, 0.0), axis=0)


def prepare_kernel(features_ref, member_ref, unary_ref, compat_ref, sent_ref, held_ref):
    labels = unary_ref.shape[0]
    sent_ref[pl.ds(0, labels), :] = unary_ref[...]
    sent_ref[pl.ds(labels, 8), :] = pick_features(features_ref, member_ref[...])
    held_ref[...] = compat_ref[...]


def half_norms(feats):
    return three_parts(-0.5 * jnp.sum(feats * feats, axis=0, keepdims=True))


def product_sides(feats):
    own = feats.shape[1]
    norms = half_norms(feats)
    ones = jnp.ones((3, own), jnp.float32)
    spare = jnp.zeros((AUX - 8 - 6, own), jnp.float32)
    columns = jnp.concatenate([feats] + norms + [ones, spare], axis=0)
    rows = jnp.concatenate([feats, ones] + norms + [spare], axis=0)
    return columns.astype(jnp.bfloat16), rows.astype(jnp.bfloat16)


def pack_kernel(labels, *refs):
    near_refs, packed_ref, rows_ref = refs[:-2], refs[-2], refs[-1]
    for place, near_ref in enumerate(near_refs):
        own = near_ref.shape[1]
        feats = near_ref[pl.ds(labels, 8), :]
        probs = normalize(-near_ref[pl.ds(0, labels), :])
        packed_ref[place] = jnp.concatenate([probs, feats], axis=0).astype(jnp.bfloat16)
        rows_ref[:, pl.ds(place * own, own)] = product_sides(feats)[1]


def join_kernel(*refs):
    joined_ref = refs[-1]
    base = 0
    for ref in refs[:-1]:
        joined_ref[pl.ds(base, ref.shape[0])] = ref[...]
        base += ref.shape[0]


def finish(message, qb, unary, compat_ref):
    message = message - qb.astype(jnp.float32)
    pairwise = jnp.dot(
        compat_ref[...], message, precision=lax.Precision.HIGHEST,
        preferred_element_type=jnp.float32,
    )
    return normalize(-unary - pairwise), pairwise


def first_part(labels, row_refs, stack_refs, total, tile_ref):
    blocks = [(ref, index) for ref in stack_refs for index in range(ref.shape[0])]
    rows = jnp.concatenate([ref[...] for ref in row_refs], axis=1)

    def exponents(place):
        ref, index = blocks[place]
        columns = product_sides(ref[index][labels:].astype(jnp.float32))[0]
        return lax.dot_general(
            columns, rows, (((0,), (0,)), ((), ())), preferred_element_type=jnp.float32
        )

    ahead = exponents(0)
    for place, (ref, index) in enumerate(blocks):
        exponent = ahead
        if place + 1 < len(blocks):
            ahead = exponents(place + 1)
        tile = jnp.exp(exponent).astype(jnp.bfloat16)
        if place == 0:
            tile_ref[...] = tile
        total = total + jnp.dot(ref[index][:labels], tile, preferred_element_type=jnp.float32)
    return total


def first_opening(labels, *refs):
    total_ref, tile_ref = refs[-2:]
    start = jnp.zeros(total_ref.shape, jnp.float32)
    total_ref[...] = first_part(labels, refs[:2], refs[2:-2], start, tile_ref)


def first_middle(labels, *refs):
    sum_ref, total_ref, tile_ref = refs[-3:]
    total_ref[...] = first_part(labels, refs[:2], refs[2:-3], sum_ref[...], tile_ref)


def first_closing(labels, nears, stacks, *refs):
    row_refs, refs = refs[:2], refs[2:]
    stack_refs, (sum_ref, compat_ref, *refs) = refs[:stacks], refs[stacks:]
    near_refs, refs = refs[:nears], refs[nears:]
    own_refs, (q_ref, tile_ref) = refs[:-2], refs[-2:]
    total = first_part(labels, row_refs, stack_refs, sum_ref[...], tile_ref)
    labels_now = [ref[index][:labels] for ref in own_refs for index in range(ref.shape[0])]
    unary = [near_ref[pl.ds(0, labels), :] for near_ref in near_refs]
    probs, _ = finish(
        total, jnp.concatenate(labels_now, axis=1), jnp.concatenate(unary, axis=1), compat_ref
    )
    q_ref[...] = probs.astype(jnp.bfloat16)


def partial_message(q_ref, tile_ref):
    return lax.dot_general(
        q_ref[...], tile_ref[...], (((1,), (1,)), ((), ())), preferred_element_type=jnp.float32
    )


def second_parts(q_ref, *refs):
    count = len(refs) // 2
    for tile_ref, part_ref in zip(refs[:count], refs[count:]):
        part_ref[...] = partial_message(q_ref, tile_ref)


def second_stacked(q_ref, *refs):
    for index, tile_ref in enumerate(refs[:-1]):
        refs[-1][index] = partial_message(q_ref, tile_ref)


def second_sums(given_ref, *refs):
    count = len(refs) // 2
    for index in range(count):
        refs[count + index][...] = refs[index][...] + given_ref[index + 1]


def second_closing(q_ref, near_ref, compat_ref, *refs):
    probs_ref, pairwise_ref = refs[-2:]
    labels, own = probs_ref.shape
    total = refs[0][...]
    for part_ref in refs[1:-2]:
        total = total + (part_ref[0] if len(part_ref.shape) == 3 else part_ref[...])
    unary = near_ref[pl.ds(0, labels), :]
    probs, pairwise = finish(total, q_ref[:, pl.ds(0, own)], unary, compat_ref)
    probs_ref[...] = probs
    pairwise_ref[...] = pairwise


def swap(value, blk_steps, grp_steps=0):
    blks, grps = lax.axis_size("blk"), lax.axis_size("grp")
    pairs = [
        (
            blk * grps + grp,
            (blk ^ blk_steps if paired("blk") else (blk + blk_steps) % blks) * grps
            + (grp ^ grp_steps if paired("grp") else (grp + grp_steps) % grps),
        )
        for blk in range(blks)
        for grp in range(grps)
    ]
    return lax.ppermute(value, ("blk", "grp"), pairs)


def group_partners(value):
    count = lax.axis_size("grp")
    order = sorted(range(1, count), key=lambda steps: (steps != count // 2, steps))
    crossed = paired("blk") and paired("grp") and lax.axis_size("blk") > 1
    return [value] + [swap(value, steps % 2 if crossed else 0, steps) for steps in order]


def paired(axis):
    count = lax.axis_size(axis)
    return count & (count - 1) == 0


def small(dims, kind):
    return math.prod(dims) * jnp.dtype(kind).itemsize <= KEPT_BYTES


def call(kernel, out_shapes, *operands):
    return pl.pallas_call(
        kernel,
        out_shape=tuple(out_shapes),
        cost_estimate=pl.CostEstimate(flops=SCHEDULE_COST, transcendentals=0, bytes_accessed=SCHEDULE_COST),
        compiler_params=pltpu.CompilerParams(vmem_limit_bytes=VMEM_LIMIT),
    )(*operands)


def hold(*operands):
    return [
        pltpu.with_memory_space_constraint(operand, pltpu.VMEM)
        if small(operand.shape, operand.dtype) else operand
        for operand in operands
    ]


def kept(dims, kind, copies=1):
    if small((copies,) + dims, kind):
        return pltpu.VMEM(dims, kind)
    return jax.ShapeDtypeStruct(dims, kind)


def shards(unary, member, features, compat):
    labels, own = unary.shape
    nears = lax.axis_size("grp")
    count = lax.axis_size("blk") * nears
    sent, held = call(
        prepare_kernel,
        [kept((labels + 8, own), jnp.float32), kept(compat.shape, jnp.float32)],
        features, member[None], unary, compat,
    )
    near = group_partners(sent)
    half = max(1, nears // 2)
    halves = [
        call(
            functools.partial(pack_kernel, labels),
            [
                kept((len(some), labels + 8, own), jnp.bfloat16),
                kept((AUX, len(some) * own), jnp.bfloat16),
            ],
            *hold(*some),
        )
        for some in (near[:half], near[half:])
    ]
    packed, rows = zip(*halves)
    parts = lax.axis_size("blk")
    tile_kind = kept((own, nears * own), jnp.bfloat16, parts)
    total_kind = kept((labels, nears * own), jnp.float32)
    tiles, totals = [], []

    def first(*stack):
        total, tile = call(
            functools.partial(first_middle if totals else first_opening, labels),
            [total_kind, tile_kind], *hold(*rows, *stack, *totals[-1:]),
        )
        tiles.append(tile)
        totals.append(total)
        return total

    def join(some):
        kind = kept((nears, labels + 8, own), jnp.bfloat16)
        return call(join_kernel, [kind], *hold(*some))[0]

    joined = join(packed)
    if paired("blk"):
        steps = list(range(3, parts, 2))
        far = [[swap(some, step) for step in steps] for some in packed]
        beside = swap(joined, 1)
        first(*packed)
        early, late = far
        *late, _ = lax.optimization_barrier((*late, first(beside)))
        stacks = list(zip(early, late))
        stacks += [(swap(join(some), 1),) for some in stacks]
        steps = [0, 1] + steps + [step - 1 for step in steps]
    else:
        steps = list(range(parts))
        stacks = [[swap(joined, step)] for step in steps[1:]]
        first(*packed)
        first(*stacks.pop(0))
    *middle, last = stacks
    for stack in middle:
        first(*stack)
    q_near, tile = call(
        functools.partial(first_closing, labels, nears, len(last)),
        [kept((labels, nears * own), jnp.bfloat16), tile_kind],
        *hold(*rows, *last, totals[-1], held, *near, *packed),
    )
    tiles.append(tile)

    if parts * math.prod(tile_kind.shape) * 2 <= KEPT_BYTES:
        tiles = hold(*tiles)
    part_kind = kept((labels, own), jnp.float32)
    tile_of = dict(zip(steps, tiles))
    if paired("blk"):
        even = [1] + list(range(2, parts, 2))
        odd = list(range(3, parts, 2))
        (stacked,) = call(
            second_stacked, [kept((len(even), labels, own), jnp.float32)],
            *hold(q_near), *[tile_of[step] for step in even],
        )
        q_near, stacked = lax.optimization_barrier((q_near, stacked))
        here, *mine = call(
            second_parts, [part_kind] * (1 + len(odd)),
            *hold(q_near), *[tile_of[step] for step in [0] + odd],
        )
        given = swap(stacked, 1)
        sums = call(second_sums, [part_kind] * len(odd), *hold(given, *mine))
        arrived = [given] + [swap(part, step) for part, step in zip(sums, odd)]
    else:
        here, *away = call(
            second_parts, [part_kind] * parts, *hold(q_near), *[tile_of[step] for step in steps]
        )
        arrived = [swap(part, parts - step) for part, step in zip(away, steps[1:])]
    return call(
        second_closing,
        [jax.ShapeDtypeStruct((labels, own), jnp.float32)] * 2,
        *hold(q_near, sent, held, here, *arrived),
    )


def solution(mesh):
    in_specs = (P(None, ("scene", "blk", "grp")), P(("scene", "blk", "grp")), P(None, "scene"), P())
    out_specs = (P(None, ("scene", "blk", "grp")), P(None, ("scene", "blk", "grp")))
    return jax.shard_map(shards, mesh=mesh, in_specs=in_specs, out_specs=out_specs, check_vma=False)
```

```python
import functools
import math

import jax
import jax.numpy as jnp
from jax import lax
from jax.experimental import pallas as pl
from jax.experimental.pallas import tpu as pltpu
from jax.sharding import PartitionSpec as P

AUX = 16
LANES = 128
VMEM_LIMIT = 56 * 1024 * 1024
KEPT_BYTES = 4 * 1024 * 1024
SCHEDULE_COST = 10 ** 10


def normalize(logits):
    raised = jnp.exp(logits)
    return raised / jnp.sum(raised, axis=0, keepdims=True)


def three_parts(value):
    high = value.astype(jnp.bfloat16).astype(jnp.float32)
    middle = (value - high).astype(jnp.bfloat16).astype(jnp.float32)
    return [high, middle, value - high - middle]


def pick_features(features_ref, member):
    feats, points = features_ref.shape
    own = member.shape[1]
    groups = points // LANES
    wide = features_ref[...].astype(jnp.float32)
    wide = jnp.concatenate([wide, jnp.zeros((8 - feats, points), jnp.float32)], axis=0)
    table = jnp.concatenate(
        [wide[:, group * LANES:(group + 1) * LANES] for group in range(groups)], axis=0
    ).astype(jnp.bfloat16)
    lane = lax.broadcasted_iota(jnp.int32, (LANES, own), 0)
    chosen = jnp.where(lane == member % LANES, 1.0, 0.0).astype(jnp.bfloat16)
    found = jnp.dot(table, chosen, preferred_element_type=jnp.float32)
    found = found.reshape(groups, 8, own)
    group = lax.broadcasted_iota(jnp.int32, (groups, 8, own), 0)
    return jnp.sum(jnp.where(group == (member // LANES)[None], found, 0.0), axis=0)


def prepare_kernel(features_ref, member_ref, unary_ref, compat_ref, sent_ref, held_ref):
    labels = unary_ref.shape[0]
    sent_ref[pl.ds(0, labels), :] = unary_ref[...]
    sent_ref[pl.ds(labels, 8), :] = pick_features(features_ref, member_ref[...])
    held_ref[...] = compat_ref[...]


def half_norms(feats):
    return three_parts(-0.5 * jnp.sum(feats * feats, axis=0, keepdims=True))


def product_sides(feats):
    own = feats.shape[1]
    norms = half_norms(feats)
    ones = jnp.ones((3, own), jnp.float32)
    spare = jnp.zeros((AUX - 8 - 6, own), jnp.float32)
    columns = jnp.concatenate([feats] + norms + [ones, spare], axis=0)
    rows = jnp.concatenate([feats, ones] + norms + [spare], axis=0)
    return columns.astype(jnp.bfloat16), rows.astype(jnp.bfloat16)


def pack_kernel(labels, *refs):
    near_refs, packed_ref, rows_ref = refs[:-2], refs[-2], refs[-1]
    for place, near_ref in enumerate(near_refs):
        own = near_ref.shape[1]
        feats = near_ref[pl.ds(labels, 8), :]
        probs = normalize(-near_ref[pl.ds(0, labels), :])
        packed_ref[place] = jnp.concatenate([probs, feats], axis=0).astype(jnp.bfloat16)
        rows_ref[:, pl.ds(place * own, own)] = product_sides(feats)[1]


def join_kernel(*refs):
    joined_ref = refs[-1]
    base = 0
    for ref in refs[:-1]:
        joined_ref[pl.ds(base, ref.shape[0])] = ref[...]
        base += ref.shape[0]


def finish(message, qb, unary, compat_ref):
    message = message - qb.astype(jnp.float32)
    pairwise = jnp.dot(
        compat_ref[...], message, precision=lax.Precision.HIGHEST,
        preferred_element_type=jnp.float32,
    )
    return normalize(-unary - pairwise), pairwise


def first_part(labels, row_refs, stack_refs, total, tile_ref):
    blocks = [(ref, index) for ref in stack_refs for index in range(ref.shape[0])]
    rows = jnp.concatenate([ref[...] for ref in row_refs], axis=1)

    def exponents(place):
        ref, index = blocks[place]
        columns = product_sides(ref[index][labels:].astype(jnp.float32))[0]
        return lax.dot_general(
            columns, rows, (((0,), (0,)), ((), ())), preferred_element_type=jnp.float32
        )

    ahead = exponents(0)
    for place, (ref, index) in enumerate(blocks):
        exponent = ahead
        if place + 1 < len(blocks):
            ahead = exponents(place + 1)
        tile = jnp.exp(exponent).astype(jnp.bfloat16)
        if place == 0:
            tile_ref[...] = tile
        total = total + jnp.dot(ref[index][:labels], tile, preferred_element_type=jnp.float32)
    return total


def first_opening(labels, *refs):
    total_ref, tile_ref = refs[-2:]
    start = jnp.zeros(total_ref.shape, jnp.float32)
    total_ref[...] = first_part(labels, refs[:2], refs[2:-2], start, tile_ref)


def first_middle(labels, *refs):
    sum_ref, total_ref, tile_ref = refs[-3:]
    total_ref[...] = first_part(labels, refs[:2], refs[2:-3], sum_ref[...], tile_ref)


def first_closing(labels, nears, stacks, *refs):
    row_refs, refs = refs[:2], refs[2:]
    stack_refs, (sum_ref, compat_ref, *refs) = refs[:stacks], refs[stacks:]
    near_refs, refs = refs[:nears], refs[nears:]
    own_refs, (q_ref, tile_ref) = refs[:-2], refs[-2:]
    total = first_part(labels, row_refs, stack_refs, sum_ref[...], tile_ref)
    labels_now = [ref[index][:labels] for ref in own_refs for index in range(ref.shape[0])]
    unary = [near_ref[pl.ds(0, labels), :] for near_ref in near_refs]
    probs, _ = finish(
        total, jnp.concatenate(labels_now, axis=1), jnp.concatenate(unary, axis=1), compat_ref
    )
    q_ref[...] = probs.astype(jnp.bfloat16)


def second_parts(q_ref, *refs):
    count = len(refs) // 2
    for tile_ref, part_ref in zip(refs[:count], refs[count:]):
        part_ref[...] = lax.dot_general(
            q_ref[...], tile_ref[...], (((1,), (1,)), ((), ())),
            preferred_element_type=jnp.float32,
        )


def second_closing(q_ref, near_ref, compat_ref, *refs):
    probs_ref, pairwise_ref = refs[-2:]
    labels, own = probs_ref.shape
    total = refs[0][...]
    for part_ref in refs[1:-2]:
        total = total + part_ref[...]
    unary = near_ref[pl.ds(0, labels), :]
    probs, pairwise = finish(total, q_ref[:, pl.ds(0, own)], unary, compat_ref)
    probs_ref[...] = probs
    pairwise_ref[...] = pairwise


def swap(value, blk_steps, grp_steps=0):
    blks, grps = lax.axis_size("blk"), lax.axis_size("grp")
    pairs = [
        (
            blk * grps + grp,
            (blk ^ blk_steps if paired("blk") else (blk + blk_steps) % blks) * grps
            + (grp ^ grp_steps if paired("grp") else (grp + grp_steps) % grps),
        )
        for blk in range(blks)
        for grp in range(grps)
    ]
    return lax.ppermute(value, ("blk", "grp"), pairs)


def group_partners(value):
    count = lax.axis_size("grp")
    order = sorted(range(1, count), key=lambda steps: (steps != count // 2, steps))
    crossed = paired("blk") and paired("grp") and lax.axis_size("blk") > 1
    return [value] + [
        swap(value, 2 * steps // count if crossed else 0, steps) for steps in order
    ]


def paired(axis):
    count = lax.axis_size(axis)
    return count & (count - 1) == 0


def send_back(value, steps):
    return swap(value, steps if paired("blk") else lax.axis_size("blk") - steps)


def small(dims, kind):
    return math.prod(dims) * jnp.dtype(kind).itemsize <= KEPT_BYTES


def call(kernel, out_shapes, *operands):
    return pl.pallas_call(
        kernel,
        out_shape=tuple(out_shapes),
        cost_estimate=pl.CostEstimate(flops=SCHEDULE_COST, transcendentals=0, bytes_accessed=SCHEDULE_COST),
        compiler_params=pltpu.CompilerParams(vmem_limit_bytes=VMEM_LIMIT),
    )(*operands)


def hold(*operands):
    return [
        pltpu.with_memory_space_constraint(operand, pltpu.VMEM)
        if small(operand.shape, operand.dtype) else operand
        for operand in operands
    ]


def kept(dims, kind, copies=1):
    if small((copies,) + dims, kind):
        return pltpu.VMEM(dims, kind)
    return jax.ShapeDtypeStruct(dims, kind)


def shards(unary, member, features, compat):
    labels, own = unary.shape
    nears = lax.axis_size("grp")
    count = lax.axis_size("blk") * nears
    sent, held = call(
        prepare_kernel,
        [kept((labels + 8, own), jnp.float32), kept(compat.shape, jnp.float32)],
        features, member[None], unary, compat,
    )
    near = group_partners(sent)
    half = max(1, nears // 2)
    halves = [
        call(
            functools.partial(pack_kernel, labels),
            [
                kept((len(some), labels + 8, own), jnp.bfloat16),
                kept((AUX, len(some) * own), jnp.bfloat16),
            ],
            *hold(*some),
        )
        for some in (near[:half], near[half:])
    ]
    packed, rows = zip(*halves)
    parts = lax.axis_size("blk")
    tile_kind = kept((own, nears * own), jnp.bfloat16, parts)
    total_kind = kept((labels, nears * own), jnp.float32)
    tiles, totals = [], []

    def first(*stack):
        total, tile = call(
            functools.partial(first_middle if totals else first_opening, labels),
            [total_kind, tile_kind], *hold(*rows, *stack, *totals[-1:]),
        )
        tiles.append(tile)
        totals.append(total)
        return total

    def join(some):
        kind = kept((nears, labels + 8, own), jnp.bfloat16)
        return call(join_kernel, [kind], *hold(*some))[0]

    joined = join(packed)
    if paired("blk"):
        steps = list(range(3, parts, 2))
        far = [[swap(some, step) for step in steps] for some in packed]
        beside = swap(joined, 1)
        first(*packed)
        early, late = far
        *late, _ = lax.optimization_barrier((*late, first(beside)))
        stacks = list(zip(early, late))
        stacks += [(swap(join(some), 1),) for some in stacks]
        steps = [0, 1] + steps + [step - 1 for step in steps]
    else:
        steps = list(range(parts))
        stacks = [[swap(joined, step)] for step in steps[1:]]
        first(*packed)
        first(*stacks.pop(0))
    *middle, last = stacks
    for stack in middle:
        first(*stack)
    q_near, tile = call(
        functools.partial(first_closing, labels, nears, len(last)),
        [kept((labels, nears * own), jnp.bfloat16), tile_kind],
        *hold(*rows, *last, totals[-1], held, *near, *packed),
    )
    tiles.append(tile)

    if parts * math.prod(tile_kind.shape) * 2 <= KEPT_BYTES:
        tiles = hold(*tiles)
    part_kind = kept((labels, own), jnp.float32)
    far = call(second_parts, [part_kind] * (parts - 2), *hold(q_near), *tiles[2:])
    if far:
        q_near, *far = lax.optimization_barrier((q_near, *far))
    here, beside = call(second_parts, [part_kind] * 2, *hold(q_near), *tiles[:2])
    sent_parts = dict(zip(steps[1:], [beside, *far]))
    arrived = [send_back(sent_parts[step], step) for step in range(1, parts)]
    return call(
        second_closing,
        [jax.ShapeDtypeStruct((labels, own), jnp.float32)] * 2,
        *hold(q_near, sent, held, here, *arrived),
    )


def solution(mesh):
    in_specs = (P(None, ("scene", "blk", "grp")), P(("scene", "blk", "grp")), P(None, "scene"), P())
    out_specs = (P(None, ("scene", "blk", "grp")), P(None, ("scene", "blk", "grp")))
    return jax.shard_map(shards, mesh=mesh, in_specs=in_specs, out_specs=out_specs, check_vma=False)
```

```python
import functools
import math

import jax
import jax.numpy as jnp
from jax import lax
from jax.experimental import pallas as pl
from jax.experimental.pallas import tpu as pltpu
from jax.sharding import PartitionSpec as P

AUX = 16
LANES = 128
VMEM_LIMIT = 56 * 1024 * 1024
KEPT_BYTES = 4 * 1024 * 1024
SCHEDULE_COST = 10 ** 10


def normalize(logits):
    raised = jnp.exp(logits)
    return raised / jnp.sum(raised, axis=0, keepdims=True)


def three_parts(value):
    high = value.astype(jnp.bfloat16).astype(jnp.float32)
    middle = (value - high).astype(jnp.bfloat16).astype(jnp.float32)
    return [high, middle, value - high - middle]


def pick_features(features_ref, member):
    feats, points = features_ref.shape
    own = member.shape[1]
    groups = points // LANES
    wide = features_ref[...].astype(jnp.float32)
    wide = jnp.concatenate([wide, jnp.zeros((8 - feats, points), jnp.float32)], axis=0)
    table = jnp.concatenate(
        [wide[:, group * LANES:(group + 1) * LANES] for group in range(groups)], axis=0
    ).astype(jnp.bfloat16)
    lane = lax.broadcasted_iota(jnp.int32, (LANES, own), 0)
    chosen = jnp.where(lane == member % LANES, 1.0, 0.0).astype(jnp.bfloat16)
    found = jnp.dot(table, chosen, preferred_element_type=jnp.float32)
    found = found.reshape(groups, 8, own)
    group = lax.broadcasted_iota(jnp.int32, (groups, 8, own), 0)
    return jnp.sum(jnp.where(group == (member // LANES)[None], found, 0.0), axis=0)


def prepare_kernel(features_ref, member_ref, unary_ref, compat_ref, sent_ref, held_ref):
    labels = unary_ref.shape[0]
    sent_ref[pl.ds(0, labels), :] = unary_ref[...]
    sent_ref[pl.ds(labels, 8), :] = pick_features(features_ref, member_ref[...])
    held_ref[...] = compat_ref[...]


def half_norms(feats):
    return three_parts(-0.5 * jnp.sum(feats * feats, axis=0, keepdims=True))


def product_sides(feats):
    own = feats.shape[1]
    norms = half_norms(feats)
    ones = jnp.ones((3, own), jnp.float32)
    spare = jnp.zeros((AUX - 8 - 6, own), jnp.float32)
    columns = jnp.concatenate([feats] + norms + [ones, spare], axis=0)
    rows = jnp.concatenate([feats, ones] + norms + [spare], axis=0)
    return columns.astype(jnp.bfloat16), rows.astype(jnp.bfloat16)


def pack_kernel(labels, *refs):
    near_refs, packed_ref, rows_ref = refs[:-2], refs[-2], refs[-1]
    for place, near_ref in enumerate(near_refs):
        own = near_ref.shape[1]
        feats = near_ref[pl.ds(labels, 8), :]
        probs = normalize(-near_ref[pl.ds(0, labels), :])
        packed_ref[place] = jnp.concatenate([probs, feats], axis=0).astype(jnp.bfloat16)
        rows_ref[:, pl.ds(place * own, own)] = product_sides(feats)[1]


def join_kernel(*refs):
    joined_ref = refs[-1]
    base = 0
    for ref in refs[:-1]:
        joined_ref[pl.ds(base, ref.shape[0])] = ref[...]
        base += ref.shape[0]


def finish(message, qb, unary, compat_ref):
    message = message - qb.astype(jnp.float32)
    pairwise = jnp.dot(
        compat_ref[...], message, precision=lax.Precision.HIGHEST,
        preferred_element_type=jnp.float32,
    )
    return normalize(-unary - pairwise), pairwise


def first_part(labels, row_refs, stack_refs, total, tile_ref):
    blocks = [(ref, index) for ref in stack_refs for index in range(ref.shape[0])]
    rows = jnp.concatenate([ref[...] for ref in row_refs], axis=1)

    def exponents(place):
        ref, index = blocks[place]
        columns = product_sides(ref[index][labels:].astype(jnp.float32))[0]
        return lax.dot_general(
            columns, rows, (((0,), (0,)), ((), ())), preferred_element_type=jnp.float32
        )

    ahead = exponents(0)
    for place, (ref, index) in enumerate(blocks):
        exponent = ahead
        if place + 1 < len(blocks):
            ahead = exponents(place + 1)
        tile = jnp.exp(exponent).astype(jnp.bfloat16)
        if place == 0:
            tile_ref[...] = tile
        total = total + jnp.dot(ref[index][:labels], tile, preferred_element_type=jnp.float32)
    return total


def first_opening(labels, *refs):
    total_ref, tile_ref = refs[-2:]
    start = jnp.zeros(total_ref.shape, jnp.float32)
    total_ref[...] = first_part(labels, refs[:2], refs[2:-2], start, tile_ref)


def first_middle(labels, *refs):
    sum_ref, total_ref, tile_ref = refs[-3:]
    total_ref[...] = first_part(labels, refs[:2], refs[2:-3], sum_ref[...], tile_ref)


def first_closing(labels, nears, stacks, *refs):
    row_refs, refs = refs[:2], refs[2:]
    stack_refs, (sum_ref, compat_ref, *refs) = refs[:stacks], refs[stacks:]
    near_refs, refs = refs[:nears], refs[nears:]
    own_refs, (q_ref, tile_ref) = refs[:-2], refs[-2:]
    total = first_part(labels, row_refs, stack_refs, sum_ref[...], tile_ref)
    labels_now = [ref[index][:labels] for ref in own_refs for index in range(ref.shape[0])]
    unary = [near_ref[pl.ds(0, labels), :] for near_ref in near_refs]
    probs, _ = finish(
        total, jnp.concatenate(labels_now, axis=1), jnp.concatenate(unary, axis=1), compat_ref
    )
    q_ref[...] = probs.astype(jnp.bfloat16)


def partial_message(q_ref, tile_ref):
    return lax.dot_general(
        q_ref[...], tile_ref[...], (((1,), (1,)), ((), ())), preferred_element_type=jnp.float32
    )


def second_parts(q_ref, *refs):
    count = len(refs) // 2
    for tile_ref, part_ref in zip(refs[:count], refs[count:]):
        part_ref[...] = partial_message(q_ref, tile_ref)


def second_stacked(q_ref, *refs):
    for index, tile_ref in enumerate(refs[:-1]):
        refs[-1][index] = partial_message(q_ref, tile_ref)


def second_sums(given_ref, *refs):
    count = len(refs) // 2
    for index in range(count):
        refs[count + index][...] = refs[index][...] + given_ref[index]


def second_closing(q_ref, near_ref, compat_ref, *refs):
    probs_ref, pairwise_ref = refs[-2:]
    labels, own = probs_ref.shape
    total = refs[0][...]
    for part_ref in refs[1:-2]:
        total = total + part_ref[...]
    unary = near_ref[pl.ds(0, labels), :]
    probs, pairwise = finish(total, q_ref[:, pl.ds(0, own)], unary, compat_ref)
    probs_ref[...] = probs
    pairwise_ref[...] = pairwise


def swap(value, blk_steps, grp_steps=0):
    blks, grps = lax.axis_size("blk"), lax.axis_size("grp")
    pairs = [
        (
            blk * grps + grp,
            (blk ^ blk_steps if paired("blk") else (blk + blk_steps) % blks) * grps
            + (grp ^ grp_steps if paired("grp") else (grp + grp_steps) % grps),
        )
        for blk in range(blks)
        for grp in range(grps)
    ]
    return lax.ppermute(value, ("blk", "grp"), pairs)


def group_partners(value):
    count = lax.axis_size("grp")
    order = sorted(range(1, count), key=lambda steps: (steps != count // 2, steps))
    crossed = paired("blk") and paired("grp") and lax.axis_size("blk") > 1
    return [value] + [
        swap(value, 2 * steps // count if crossed else 0, steps) for steps in order
    ]


def paired(axis):
    count = lax.axis_size(axis)
    return count & (count - 1) == 0


def small(dims, kind):
    return math.prod(dims) * jnp.dtype(kind).itemsize <= KEPT_BYTES


def call(kernel, out_shapes, *operands):
    return pl.pallas_call(
        kernel,
        out_shape=tuple(out_shapes),
        cost_estimate=pl.CostEstimate(flops=SCHEDULE_COST, transcendentals=0, bytes_accessed=SCHEDULE_COST),
        compiler_params=pltpu.CompilerParams(vmem_limit_bytes=VMEM_LIMIT),
    )(*operands)


def hold(*operands):
    return [
        pltpu.with_memory_space_constraint(operand, pltpu.VMEM)
        if small(operand.shape, operand.dtype) else operand
        for operand in operands
    ]


def kept(dims, kind, copies=1):
    if small((copies,) + dims, kind):
        return pltpu.VMEM(dims, kind)
    return jax.ShapeDtypeStruct(dims, kind)


def shards(unary, member, features, compat):
    labels, own = unary.shape
    nears = lax.axis_size("grp")
    count = lax.axis_size("blk") * nears
    sent, held = call(
        prepare_kernel,
        [kept((labels + 8, own), jnp.float32), kept(compat.shape, jnp.float32)],
        features, member[None], unary, compat,
    )
    near = group_partners(sent)
    half = max(1, nears // 2)
    halves = [
        call(
            functools.partial(pack_kernel, labels),
            [
                kept((len(some), labels + 8, own), jnp.bfloat16),
                kept((AUX, len(some) * own), jnp.bfloat16),
            ],
            *hold(*some),
        )
        for some in (near[:half], near[half:])
    ]
    packed, rows = zip(*halves)
    parts = lax.axis_size("blk")
    tile_kind = kept((own, nears * own), jnp.bfloat16, parts)
    total_kind = kept((labels, nears * own), jnp.float32)
    tiles, totals = [], []

    def first(*stack):
        total, tile = call(
            functools.partial(first_middle if totals else first_opening, labels),
            [total_kind, tile_kind], *hold(*rows, *stack, *totals[-1:]),
        )
        tiles.append(tile)
        totals.append(total)
        return total

    def join(some):
        kind = kept((nears, labels + 8, own), jnp.bfloat16)
        return call(join_kernel, [kind], *hold(*some))[0]

    joined = join(packed)
    if paired("blk"):
        steps = list(range(3, parts, 2))
        far = [[swap(some, step) for step in steps] for some in packed]
        beside = swap(joined, 1)
        first(*packed)
        early, late = far
        *late, _ = lax.optimization_barrier((*late, first(beside)))
        stacks = list(zip(early, late))
        stacks += [(swap(join(some), 1),) for some in stacks]
        steps = [0, 1] + steps + [step - 1 for step in steps]
    else:
        steps = list(range(parts))
        stacks = [[swap(joined, step)] for step in steps[1:]]
        first(*packed)
        first(*stacks.pop(0))
    *middle, last = stacks
    for stack in middle:
        first(*stack)
    q_near, tile = call(
        functools.partial(first_closing, labels, nears, len(last)),
        [kept((labels, nears * own), jnp.bfloat16), tile_kind],
        *hold(*rows, *last, totals[-1], held, *near, *packed),
    )
    tiles.append(tile)

    if parts * math.prod(tile_kind.shape) * 2 <= KEPT_BYTES:
        tiles = hold(*tiles)
    part_kind = kept((labels, own), jnp.float32)
    tile_of = dict(zip(steps, tiles))
    if paired("blk"):
        even, odd = list(range(2, parts, 2)), list(range(3, parts, 2))
        (stacked,) = call(
            second_stacked, [kept((len(even), labels, own), jnp.float32)],
            *hold(q_near), *[tile_of[step] for step in even],
        )
        q_near, stacked = lax.optimization_barrier((q_near, stacked))
        here, beside, *mine = call(
            second_parts, [part_kind] * (2 + len(odd)),
            *hold(q_near), *[tile_of[step] for step in [0, 1] + odd],
        )
        sums = call(second_sums, [part_kind] * len(odd), *hold(swap(stacked, 1), *mine))
        beside, *sums = lax.optimization_barrier((beside, *sums))
        arrived = [swap(part, step) for part, step in zip(sums, odd)]
        arrived.append(swap(beside, 1))
    else:
        here, *away = call(
            second_parts, [part_kind] * parts, *hold(q_near), *[tile_of[step] for step in steps]
        )
        arrived = [swap(part, parts - step) for part, step in zip(away, steps[1:])]
    return call(
        second_closing,
        [jax.ShapeDtypeStruct((labels, own), jnp.float32)] * 2,
        *hold(q_near, sent, held, here, *arrived),
    )


def solution(mesh):
    in_specs = (P(None, ("scene", "blk", "grp")), P(("scene", "blk", "grp")), P(None, "scene"), P())
    out_specs = (P(None, ("scene", "blk", "grp")), P(None, ("scene", "blk", "grp")))
    return jax.shard_map(shards, mesh=mesh, in_specs=in_specs, out_specs=out_specs, check_vma=False)
```

```python
import functools
import math

import jax
import jax.numpy as jnp
from jax import lax
from jax.experimental import pallas as pl
from jax.experimental.pallas import tpu as pltpu
from jax.sharding import PartitionSpec as P

AUX = 16
LANES = 128
VMEM_LIMIT = 56 * 1024 * 1024
KEPT_BYTES = 4 * 1024 * 1024
SCHEDULE_COST = 10 ** 10


def normalize(logits):
    raised = jnp.exp(logits)
    return raised / jnp.sum(raised, axis=0, keepdims=True)


def three_parts(value):
    high = value.astype(jnp.bfloat16).astype(jnp.float32)
    middle = (value - high).astype(jnp.bfloat16).astype(jnp.float32)
    return [high, middle, value - high - middle]


def pick_features(features_ref, member):
    feats, points = features_ref.shape
    own = member.shape[1]
    groups = points // LANES
    wide = features_ref[...].astype(jnp.float32)
    wide = jnp.concatenate([wide, jnp.zeros((8 - feats, points), jnp.float32)], axis=0)
    table = jnp.concatenate(
        [wide[:, group * LANES:(group + 1) * LANES] for group in range(groups)], axis=0
    ).astype(jnp.bfloat16)
    lane = lax.broadcasted_iota(jnp.int32, (LANES, own), 0)
    chosen = jnp.where(lane == member % LANES, 1.0, 0.0).astype(jnp.bfloat16)
    found = jnp.dot(table, chosen, preferred_element_type=jnp.float32)
    found = found.reshape(groups, 8, own)
    group = lax.broadcasted_iota(jnp.int32, (groups, 8, own), 0)
    return jnp.sum(jnp.where(group == (member // LANES)[None], found, 0.0), axis=0)


def prepare_kernel(features_ref, member_ref, unary_ref, compat_ref, sent_ref, held_ref):
    labels = unary_ref.shape[0]
    sent_ref[pl.ds(0, labels), :] = unary_ref[...]
    sent_ref[pl.ds(labels, 8), :] = pick_features(features_ref, member_ref[...])
    held_ref[...] = compat_ref[...]


def half_norms(feats):
    return three_parts(-0.5 * jnp.sum(feats * feats, axis=0, keepdims=True))


def product_sides(feats):
    own = feats.shape[1]
    norms = half_norms(feats)
    ones = jnp.ones((3, own), jnp.float32)
    spare = jnp.zeros((AUX - 8 - 6, own), jnp.float32)
    columns = jnp.concatenate([feats] + norms + [ones, spare], axis=0)
    rows = jnp.concatenate([feats, ones] + norms + [spare], axis=0)
    return columns.astype(jnp.bfloat16), rows.astype(jnp.bfloat16)


def pack_kernel(labels, *refs):
    near_refs, packed_ref, rows_ref = refs[:-2], refs[-2], refs[-1]
    for place, near_ref in enumerate(near_refs):
        own = near_ref.shape[1]
        feats = near_ref[pl.ds(labels, 8), :]
        probs = normalize(-near_ref[pl.ds(0, labels), :])
        packed_ref[place] = jnp.concatenate([probs, feats], axis=0).astype(jnp.bfloat16)
        rows_ref[:, pl.ds(place * own, own)] = product_sides(feats)[1]


def join_kernel(*refs):
    joined_ref = refs[-1]
    base = 0
    for ref in refs[:-1]:
        joined_ref[pl.ds(base, ref.shape[0])] = ref[...]
        base += ref.shape[0]


def finish(message, qb, unary, compat_ref):
    message = message - qb.astype(jnp.float32)
    pairwise = jnp.dot(
        compat_ref[...], message, precision=lax.Precision.HIGHEST,
        preferred_element_type=jnp.float32,
    )
    return normalize(-unary - pairwise), pairwise


def first_part(labels, row_refs, stack_refs, total, tile_ref):
    blocks = [(ref, index) for ref in stack_refs for index in range(ref.shape[0])]
    rows = jnp.concatenate([ref[...] for ref in row_refs], axis=1)

    def exponents(place):
        ref, index = blocks[place]
        columns = product_sides(ref[index][labels:].astype(jnp.float32))[0]
        return lax.dot_general(
            columns, rows, (((0,), (0,)), ((), ())), preferred_element_type=jnp.float32
        )

    ahead = exponents(0)
    for place, (ref, index) in enumerate(blocks):
        exponent = ahead
        if place + 1 < len(blocks):
            ahead = exponents(place + 1)
        tile = jnp.exp(exponent).astype(jnp.bfloat16)
        if place == 0:
            tile_ref[...] = tile
        total = total + jnp.dot(ref[index][:labels], tile, preferred_element_type=jnp.float32)
    return total


def first_opening(labels, *refs):
    total_ref, tile_ref = refs[-2:]
    start = jnp.zeros(total_ref.shape, jnp.float32)
    total_ref[...] = first_part(labels, refs[:2], refs[2:-2], start, tile_ref)


def first_middle(labels, *refs):
    sum_ref, total_ref, tile_ref = refs[-3:]
    total_ref[...] = first_part(labels, refs[:2], refs[2:-3], sum_ref[...], tile_ref)


def first_closing(labels, nears, stacks, *refs):
    row_refs, refs = refs[:2], refs[2:]
    stack_refs, (sum_ref, compat_ref, *refs) = refs[:stacks], refs[stacks:]
    near_refs, refs = refs[:nears], refs[nears:]
    own_refs, (q_ref, tile_ref) = refs[:-2], refs[-2:]
    total = first_part(labels, row_refs, stack_refs, sum_ref[...], tile_ref)
    labels_now = [ref[index][:labels] for ref in own_refs for index in range(ref.shape[0])]
    unary = [near_ref[pl.ds(0, labels), :] for near_ref in near_refs]
    probs, _ = finish(
        total, jnp.concatenate(labels_now, axis=1), jnp.concatenate(unary, axis=1), compat_ref
    )
    q_ref[...] = probs.astype(jnp.bfloat16)


def partial_message(q_ref, tile_ref):
    return lax.dot_general(
        q_ref[...], tile_ref[...], (((1,), (1,)), ((), ())), preferred_element_type=jnp.float32
    )


def second_parts(q_ref, *refs):
    count = len(refs) // 2
    for tile_ref, part_ref in zip(refs[:count], refs[count:]):
        part_ref[...] = partial_message(q_ref, tile_ref)


def second_stacked(q_ref, *refs):
    for index, tile_ref in enumerate(refs[:-1]):
        refs[-1][index] = partial_message(q_ref, tile_ref)


def second_sums(given_ref, *refs):
    count = len(refs) // 2
    for index in range(count):
        refs[count + index][...] = refs[index][...] + given_ref[index]


def second_closing(q_ref, near_ref, compat_ref, *refs):
    probs_ref, pairwise_ref = refs[-2:]
    labels, own = probs_ref.shape
    total = refs[0][...]
    for part_ref in refs[1:-2]:
        total = total + part_ref[...]
    unary = near_ref[pl.ds(0, labels), :]
    probs, pairwise = finish(total, q_ref[:, pl.ds(0, own)], unary, compat_ref)
    probs_ref[...] = probs
    pairwise_ref[...] = pairwise


def swap(value, blk_steps, grp_steps=0):
    blks, grps = lax.axis_size("blk"), lax.axis_size("grp")
    pairs = [
        (
            blk * grps + grp,
            (blk ^ blk_steps if paired("blk") else (blk + blk_steps) % blks) * grps
            + (grp ^ grp_steps if paired("grp") else (grp + grp_steps) % grps),
        )
        for blk in range(blks)
        for grp in range(grps)
    ]
    return lax.ppermute(value, ("blk", "grp"), pairs)


def group_partners(value):
    count = lax.axis_size("grp")
    order = sorted(range(1, count), key=lambda steps: (steps != count - 1, steps))
    crossed = paired("blk") and paired("grp") and lax.axis_size("blk") > 1
    return [value] + [
        swap(value, 2 * steps // count if crossed else 0, steps) for steps in order
    ]


def paired(axis):
    count = lax.axis_size(axis)
    return count & (count - 1) == 0


def small(dims, kind):
    return math.prod(dims) * jnp.dtype(kind).itemsize <= KEPT_BYTES


def call(kernel, out_shapes, *operands):
    return pl.pallas_call(
        kernel,
        out_shape=tuple(out_shapes),
        cost_estimate=pl.CostEstimate(flops=SCHEDULE_COST, transcendentals=0, bytes_accessed=SCHEDULE_COST),
        compiler_params=pltpu.CompilerParams(vmem_limit_bytes=VMEM_LIMIT),
    )(*operands)


def hold(*operands):
    return [
        pltpu.with_memory_space_constraint(operand, pltpu.VMEM)
        if small(operand.shape, operand.dtype) else operand
        for operand in operands
    ]


def kept(dims, kind, copies=1):
    if small((copies,) + dims, kind):
        return pltpu.VMEM(dims, kind)
    return jax.ShapeDtypeStruct(dims, kind)


def shards(unary, member, features, compat):
    labels, own = unary.shape
    nears = lax.axis_size("grp")
    count = lax.axis_size("blk") * nears
    sent, held = call(
        prepare_kernel,
        [kept((labels + 8, own), jnp.float32), kept(compat.shape, jnp.float32)],
        features, member[None], unary, compat,
    )
    near = group_partners(sent)
    half = max(1, nears // 2)
    halves = [
        call(
            functools.partial(pack_kernel, labels),
            [
                kept((len(some), labels + 8, own), jnp.bfloat16),
                kept((AUX, len(some) * own), jnp.bfloat16),
            ],
            *hold(*some),
        )
        for some in (near[:half], near[half:])
    ]
    packed, rows = zip(*halves)
    parts = lax.axis_size("blk")
    tile_kind = kept((own, nears * own), jnp.bfloat16, parts)
    total_kind = kept((labels, nears * own), jnp.float32)
    tiles, totals = [], []

    def first(*stack):
        total, tile = call(
            functools.partial(first_middle if totals else first_opening, labels),
            [total_kind, tile_kind], *hold(*rows, *stack, *totals[-1:]),
        )
        tiles.append(tile)
        totals.append(total)
        return total

    def join(some):
        kind = kept((nears, labels + 8, own), jnp.bfloat16)
        return call(join_kernel, [kind], *hold(*some))[0]

    joined = join(packed)
    if paired("blk"):
        steps = list(range(3, parts, 2))
        far = [[swap(some, step) for step in steps] for some in packed]
        beside = swap(joined, 1)
        first(*packed)
        early, late = far
        *late, _ = lax.optimization_barrier((*late, first(beside)))
        stacks = list(zip(early, late))
        stacks += [(swap(join(some), 1),) for some in stacks]
        steps = [0, 1] + steps + [step - 1 for step in steps]
    else:
        steps = list(range(parts))
        stacks = [[swap(joined, step)] for step in steps[1:]]
        first(*packed)
        first(*stacks.pop(0))
    *middle, last = stacks
    for stack in middle:
        first(*stack)
    q_near, tile = call(
        functools.partial(first_closing, labels, nears, len(last)),
        [kept((labels, nears * own), jnp.bfloat16), tile_kind],
        *hold(*rows, *last, totals[-1], held, *near, *packed),
    )
    tiles.append(tile)

    if parts * math.prod(tile_kind.shape) * 2 <= KEPT_BYTES:
        tiles = hold(*tiles)
    part_kind = kept((labels, own), jnp.float32)
    tile_of = dict(zip(steps, tiles))
    if paired("blk"):
        even, odd = list(range(2, parts, 2)), list(range(3, parts, 2))
        (stacked,) = call(
            second_stacked, [kept((len(even), labels, own), jnp.float32)],
            *hold(q_near), *[tile_of[step] for step in even],
        )
        q_near, stacked = lax.optimization_barrier((q_near, stacked))
        here, beside, *mine = call(
            second_parts, [part_kind] * (2 + len(odd)),
            *hold(q_near), *[tile_of[step] for step in [0, 1] + odd],
        )
        sums = call(second_sums, [part_kind] * len(odd), *hold(swap(stacked, 1), *mine))
        beside, *sums = lax.optimization_barrier((beside, *sums))
        arrived = [swap(part, step) for part, step in zip(sums, odd)]
        arrived.append(swap(beside, 1))
    else:
        here, *away = call(
            second_parts, [part_kind] * parts, *hold(q_near), *[tile_of[step] for step in steps]
        )
        arrived = [swap(part, parts - step) for part, step in zip(away, steps[1:])]
    return call(
        second_closing,
        [jax.ShapeDtypeStruct((labels, own), jnp.float32)] * 2,
        *hold(q_near, sent, held, here, *arrived),
    )


def solution(mesh):
    in_specs = (P(None, ("scene", "blk", "grp")), P(("scene", "blk", "grp")), P(None, "scene"), P())
    out_specs = (P(None, ("scene", "blk", "grp")), P(None, ("scene", "blk", "grp")))
    return jax.shard_map(shards, mesh=mesh, in_specs=in_specs, out_specs=out_specs, check_vma=False)
```

```python
import functools
import math

import jax
import jax.numpy as jnp
from jax import lax
from jax.experimental import pallas as pl
from jax.experimental.pallas import tpu as pltpu
from jax.sharding import PartitionSpec as P

AUX = 16
LANES = 128
VMEM_LIMIT = 56 * 1024 * 1024
KEPT_BYTES = 4 * 1024 * 1024
SCHEDULE_COST = 10 ** 10


def normalize(logits):
    raised = jnp.exp(logits)
    return raised / jnp.sum(raised, axis=0, keepdims=True)


def three_parts(value):
    high = value.astype(jnp.bfloat16).astype(jnp.float32)
    middle = (value - high).astype(jnp.bfloat16).astype(jnp.float32)
    return [high, middle, value - high - middle]


def pick_features(features_ref, member):
    feats, points = features_ref.shape
    own = member.shape[1]
    groups = points // LANES
    wide = features_ref[...].astype(jnp.float32)
    wide = jnp.concatenate([wide, jnp.zeros((8 - feats, points), jnp.float32)], axis=0)
    table = jnp.concatenate(
        [wide[:, group * LANES:(group + 1) * LANES] for group in range(groups)], axis=0
    ).astype(jnp.bfloat16)
    lane = lax.broadcasted_iota(jnp.int32, (LANES, own), 0)
    chosen = jnp.where(lane == member % LANES, 1.0, 0.0).astype(jnp.bfloat16)
    found = jnp.dot(table, chosen, preferred_element_type=jnp.float32)
    found = found.reshape(groups, 8, own)
    group = lax.broadcasted_iota(jnp.int32, (groups, 8, own), 0)
    return jnp.sum(jnp.where(group == (member // LANES)[None], found, 0.0), axis=0)


def prepare_kernel(features_ref, member_ref, unary_ref, compat_ref, sent_ref, held_ref):
    labels = unary_ref.shape[0]
    sent_ref[pl.ds(0, labels), :] = unary_ref[...]
    sent_ref[pl.ds(labels, 8), :] = pick_features(features_ref, member_ref[...])
    held_ref[...] = compat_ref[...]


def half_norms(feats):
    return three_parts(-0.5 * jnp.sum(feats * feats, axis=0, keepdims=True))


def product_sides(feats):
    own = feats.shape[1]
    norms = half_norms(feats)
    ones = jnp.ones((3, own), jnp.float32)
    spare = jnp.zeros((AUX - 8 - 6, own), jnp.float32)
    columns = jnp.concatenate([feats] + norms + [ones, spare], axis=0)
    rows = jnp.concatenate([feats, ones] + norms + [spare], axis=0)
    return columns.astype(jnp.bfloat16), rows.astype(jnp.bfloat16)


def pack_kernel(labels, *refs):
    near_refs, packed_ref, rows_ref = refs[:-2], refs[-2], refs[-1]
    for place, near_ref in enumerate(near_refs):
        own = near_ref.shape[1]
        feats = near_ref[pl.ds(labels, 8), :]
        probs = normalize(-near_ref[pl.ds(0, labels), :])
        packed_ref[place] = jnp.concatenate([probs, feats], axis=0).astype(jnp.bfloat16)
        rows_ref[:, pl.ds(place * own, own)] = product_sides(feats)[1]


def join_kernel(*refs):
    joined_ref = refs[-1]
    base = 0
    for ref in refs[:-1]:
        joined_ref[pl.ds(base, ref.shape[0])] = ref[...]
        base += ref.shape[0]


def finish(message, qb, unary, compat_ref):
    message = message - qb.astype(jnp.float32)
    pairwise = jnp.dot(
        compat_ref[...], message, precision=lax.Precision.HIGHEST,
        preferred_element_type=jnp.float32,
    )
    return normalize(-unary - pairwise), pairwise


def first_part(labels, row_refs, stack_refs, total, tile_ref):
    blocks = [(ref, index) for ref in stack_refs for index in range(ref.shape[0])]
    rows = jnp.concatenate([ref[...] for ref in row_refs], axis=1)

    def exponents(place):
        ref, index = blocks[place]
        columns = product_sides(ref[index][labels:].astype(jnp.float32))[0]
        return lax.dot_general(
            columns, rows, (((0,), (0,)), ((), ())), preferred_element_type=jnp.float32
        )

    ahead = exponents(0)
    for place, (ref, index) in enumerate(blocks):
        exponent = ahead
        if place + 1 < len(blocks):
            ahead = exponents(place + 1)
        tile = jnp.exp(exponent).astype(jnp.bfloat16)
        if place == 0:
            tile_ref[...] = tile
        total = total + jnp.dot(ref[index][:labels], tile, preferred_element_type=jnp.float32)
    return total


def first_opening(labels, *refs):
    total_ref, tile_ref = refs[-2:]
    start = jnp.zeros(total_ref.shape, jnp.float32)
    total_ref[...] = first_part(labels, refs[:2], refs[2:-2], start, tile_ref)


def first_middle(labels, *refs):
    sum_ref, total_ref, tile_ref = refs[-3:]
    total_ref[...] = first_part(labels, refs[:2], refs[2:-3], sum_ref[...], tile_ref)


def first_closing(labels, nears, stacks, *refs):
    row_refs, refs = refs[:2], refs[2:]
    stack_refs, (sum_ref, compat_ref, *refs) = refs[:stacks], refs[stacks:]
    near_refs, refs = refs[:nears], refs[nears:]
    own_refs, (q_ref, tile_ref) = refs[:-2], refs[-2:]
    total = first_part(labels, row_refs, stack_refs, sum_ref[...], tile_ref)
    labels_now = [ref[index][:labels] for ref in own_refs for index in range(ref.shape[0])]
    unary = [near_ref[pl.ds(0, labels), :] for near_ref in near_refs]
    probs, _ = finish(
        total, jnp.concatenate(labels_now, axis=1), jnp.concatenate(unary, axis=1), compat_ref
    )
    q_ref[...] = probs.astype(jnp.bfloat16)


def partial_message(q_ref, tile_ref):
    return lax.dot_general(
        q_ref[...], tile_ref[...], (((1,), (1,)), ((), ())), preferred_element_type=jnp.float32
    )


def second_parts(q_ref, *refs):
    count = len(refs) // 2
    for tile_ref, part_ref in zip(refs[:count], refs[count:]):
        part_ref[...] = partial_message(q_ref, tile_ref)


def second_stacked(q_ref, *refs):
    for index, tile_ref in enumerate(refs[:-1]):
        refs[-1][index] = partial_message(q_ref, tile_ref)


def second_sums(given_ref, *refs):
    count = len(refs) // 2
    for index in range(count):
        refs[count + index][...] = refs[index][...] + given_ref[index]


def second_closing(q_ref, near_ref, compat_ref, *refs):
    probs_ref, pairwise_ref = refs[-2:]
    labels, own = probs_ref.shape
    total = refs[0][...]
    for part_ref in refs[1:-2]:
        total = total + part_ref[...]
    unary = near_ref[pl.ds(0, labels), :]
    probs, pairwise = finish(total, q_ref[:, pl.ds(0, own)], unary, compat_ref)
    probs_ref[...] = probs
    pairwise_ref[...] = pairwise


def swap(value, blk_steps, grp_steps=0):
    blks, grps = lax.axis_size("blk"), lax.axis_size("grp")
    pairs = [
        (
            blk * grps + grp,
            (blk ^ blk_steps if paired("blk") else (blk + blk_steps) % blks) * grps
            + (grp ^ grp_steps if paired("grp") else (grp + grp_steps) % grps),
        )
        for blk in range(blks)
        for grp in range(grps)
    ]
    return lax.ppermute(value, ("blk", "grp"), pairs)


def group_partners(value):
    count = lax.axis_size("grp")
    order = sorted(range(1, count), reverse=True)
    crossed = paired("blk") and paired("grp") and lax.axis_size("blk") > 1
    return [value] + [
        swap(value, 2 * steps // count if crossed else 0, steps) for steps in order
    ]


def paired(axis):
    count = lax.axis_size(axis)
    return count & (count - 1) == 0


def small(dims, kind):
    return math.prod(dims) * jnp.dtype(kind).itemsize <= KEPT_BYTES


def call(kernel, out_shapes, *operands):
    return pl.pallas_call(
        kernel,
        out_shape=tuple(out_shapes),
        cost_estimate=pl.CostEstimate(flops=SCHEDULE_COST, transcendentals=0, bytes_accessed=SCHEDULE_COST),
        compiler_params=pltpu.CompilerParams(vmem_limit_bytes=VMEM_LIMIT),
    )(*operands)


def hold(*operands):
    return [
        pltpu.with_memory_space_constraint(operand, pltpu.VMEM)
        if small(operand.shape, operand.dtype) else operand
        for operand in operands
    ]


def kept(dims, kind, copies=1):
    if small((copies,) + dims, kind):
        return pltpu.VMEM(dims, kind)
    return jax.ShapeDtypeStruct(dims, kind)


def shards(unary, member, features, compat):
    labels, own = unary.shape
    nears = lax.axis_size("grp")
    count = lax.axis_size("blk") * nears
    sent, held = call(
        prepare_kernel,
        [kept((labels + 8, own), jnp.float32), kept(compat.shape, jnp.float32)],
        features, member[None], unary, compat,
    )
    near = group_partners(sent)
    half = max(1, nears // 2)
    halves = [
        call(
            functools.partial(pack_kernel, labels),
            [
                kept((len(some), labels + 8, own), jnp.bfloat16),
                kept((AUX, len(some) * own), jnp.bfloat16),
            ],
            *hold(*some),
        )
        for some in (near[:half], near[half:])
    ]
    packed, rows = zip(*halves)
    parts = lax.axis_size("blk")
    tile_kind = kept((own, nears * own), jnp.bfloat16, parts)
    total_kind = kept((labels, nears * own), jnp.float32)
    tiles, totals = [], []

    def first(*stack):
        total, tile = call(
            functools.partial(first_middle if totals else first_opening, labels),
            [total_kind, tile_kind], *hold(*rows, *stack, *totals[-1:]),
        )
        tiles.append(tile)
        totals.append(total)
        return total

    def join(some):
        kind = kept((nears, labels + 8, own), jnp.bfloat16)
        return call(join_kernel, [kind], *hold(*some))[0]

    joined = join(packed)
    if paired("blk"):
        steps = list(range(3, parts, 2))
        far = [[swap(some, step) for step in steps] for some in packed]
        beside = swap(joined, 1)
        first(*packed)
        early, late = far
        *late, _ = lax.optimization_barrier((*late, first(beside)))
        stacks = list(zip(early, late))
        stacks += [(swap(join(some), 1),) for some in stacks]
        steps = [0, 1] + steps + [step - 1 for step in steps]
    else:
        steps = list(range(parts))
        stacks = [[swap(joined, step)] for step in steps[1:]]
        first(*packed)
        first(*stacks.pop(0))
    *middle, last = stacks
    for stack in middle:
        first(*stack)
    q_near, tile = call(
        functools.partial(first_closing, labels, nears, len(last)),
        [kept((labels, nears * own), jnp.bfloat16), tile_kind],
        *hold(*rows, *last, totals[-1], held, *near, *packed),
    )
    tiles.append(tile)

    if parts * math.prod(tile_kind.shape) * 2 <= KEPT_BYTES:
        tiles = hold(*tiles)
    part_kind = kept((labels, own), jnp.float32)
    tile_of = dict(zip(steps, tiles))
    if paired("blk"):
        even, odd = list(range(2, parts, 2)), list(range(3, parts, 2))
        (stacked,) = call(
            second_stacked, [kept((len(even), labels, own), jnp.float32)],
            *hold(q_near), *[tile_of[step] for step in even],
        )
        q_near, stacked = lax.optimization_barrier((q_near, stacked))
        here, beside, *mine = call(
            second_parts, [part_kind] * (2 + len(odd)),
            *hold(q_near), *[tile_of[step] for step in [0, 1] + odd],
        )
        sums = call(second_sums, [part_kind] * len(odd), *hold(swap(stacked, 1), *mine))
        beside, *sums = lax.optimization_barrier((beside, *sums))
        arrived = [swap(part, step) for part, step in zip(sums, odd)]
        arrived.append(swap(beside, 1))
    else:
        here, *away = call(
            second_parts, [part_kind] * parts, *hold(q_near), *[tile_of[step] for step in steps]
        )
        arrived = [swap(part, parts - step) for part, step in zip(away, steps[1:])]
    return call(
        second_closing,
        [jax.ShapeDtypeStruct((labels, own), jnp.float32)] * 2,
        *hold(q_near, sent, held, here, *arrived),
    )


def solution(mesh):
    in_specs = (P(None, ("scene", "blk", "grp")), P(("scene", "blk", "grp")), P(None, "scene"), P())
    out_specs = (P(None, ("scene", "blk", "grp")), P(None, ("scene", "blk", "grp")))
    return jax.shard_map(shards, mesh=mesh, in_specs=in_specs, out_specs=out_specs, check_vma=False)
```

```python
import functools
import math

import jax
import jax.numpy as jnp
from jax import lax
from jax.experimental import pallas as pl
from jax.experimental.pallas import tpu as pltpu
from jax.sharding import PartitionSpec as P

AUX = 16
LANES = 128
VMEM_LIMIT = 56 * 1024 * 1024
KEPT_BYTES = 4 * 1024 * 1024
SCHEDULE_COST = 10 ** 10


def normalize(logits):
    raised = jnp.exp(logits)
    return raised / jnp.sum(raised, axis=0, keepdims=True)


def three_parts(value):
    high = value.astype(jnp.bfloat16).astype(jnp.float32)
    middle = (value - high).astype(jnp.bfloat16).astype(jnp.float32)
    return [high, middle, value - high - middle]


def pick_features(features_ref, member):
    feats, points = features_ref.shape
    own = member.shape[1]
    groups = points // LANES
    wide = features_ref[...].astype(jnp.float32)
    wide = jnp.concatenate([wide, jnp.zeros((8 - feats, points), jnp.float32)], axis=0)
    table = jnp.concatenate(
        [wide[:, group * LANES:(group + 1) * LANES] for group in range(groups)], axis=0
    ).astype(jnp.bfloat16)
    lane = lax.broadcasted_iota(jnp.int32, (LANES, own), 0)
    chosen = jnp.where(lane == member % LANES, 1.0, 0.0).astype(jnp.bfloat16)
    found = jnp.dot(table, chosen, preferred_element_type=jnp.float32)
    found = found.reshape(groups, 8, own)
    group = lax.broadcasted_iota(jnp.int32, (groups, 8, own), 0)
    return jnp.sum(jnp.where(group == (member // LANES)[None], found, 0.0), axis=0)


def prepare_kernel(features_ref, member_ref, unary_ref, compat_ref, sent_ref, held_ref):
    labels = unary_ref.shape[0]
    sent_ref[pl.ds(0, labels), :] = unary_ref[...]
    sent_ref[pl.ds(labels, 8), :] = pick_features(features_ref, member_ref[...])
    held_ref[...] = compat_ref[...]


def half_norms(feats):
    return three_parts(-0.5 * jnp.sum(feats * feats, axis=0, keepdims=True))


def product_sides(feats):
    own = feats.shape[1]
    norms = half_norms(feats)
    ones = jnp.ones((3, own), jnp.float32)
    spare = jnp.zeros((AUX - 8 - 6, own), jnp.float32)
    columns = jnp.concatenate([feats] + norms + [ones, spare], axis=0)
    rows = jnp.concatenate([feats, ones] + norms + [spare], axis=0)
    return columns.astype(jnp.bfloat16), rows.astype(jnp.bfloat16)


def pack_kernel(labels, counts, unused, *refs):
    *near_refs, packed_ref, rows_ref, unary_ref = refs[unused:]
    for place, count in enumerate(counts):
        near = near_refs.pop(0)[...]
        for _ in range(count - 1):
            near = near + near_refs.pop(0)[...]
        own = near.shape[1]
        unary, feats = near[:labels], near[labels:]
        packed = jnp.concatenate([normalize(-unary), feats], axis=0)
        packed_ref[place] = packed.astype(jnp.bfloat16)
        rows_ref[:, pl.ds(place * own, own)] = product_sides(feats)[1]
        unary_ref[:, pl.ds(place * own, own)] = unary


def join_kernel(*refs):
    joined_ref = refs[-1]
    base = 0
    for ref in refs[:-1]:
        joined_ref[pl.ds(base, ref.shape[0])] = ref[...]
        base += ref.shape[0]


def finish(message, qb, unary, compat_ref):
    message = message - qb.astype(jnp.float32)
    pairwise = jnp.dot(
        compat_ref[...], message, precision=lax.Precision.HIGHEST,
        preferred_element_type=jnp.float32,
    )
    return normalize(-unary - pairwise), pairwise


def first_part(labels, own_place, row_refs, stack_refs, total, tile_ref):
    blocks = [(ref, index) for ref in stack_refs for index in range(ref.shape[0])]
    rows = jnp.concatenate([ref[...] for ref in row_refs], axis=1)

    def exponents(place):
        ref, index = blocks[place]
        columns = product_sides(ref[index][labels:].astype(jnp.float32))[0]
        return lax.dot_general(
            columns, rows, (((0,), (0,)), ((), ())), preferred_element_type=jnp.float32
        )

    ahead = exponents(0)
    for place, (ref, index) in enumerate(blocks):
        exponent = ahead
        if place + 1 < len(blocks):
            ahead = exponents(place + 1)
        tile = jnp.exp(exponent).astype(jnp.bfloat16)
        if place == own_place:
            tile_ref[...] = tile
        total = total + jnp.dot(ref[index][:labels], tile, preferred_element_type=jnp.float32)
    return total


def first_opening(labels, own_place, *refs):
    total_ref, tile_ref = refs[-2:]
    start = jnp.zeros(total_ref.shape, jnp.float32)
    total_ref[...] = first_part(labels, own_place, refs[:2], refs[2:-2], start, tile_ref)


def first_middle(labels, own_place, *refs):
    sum_ref, total_ref, tile_ref = refs[-3:]
    total_ref[...] = first_part(labels, own_place, refs[:2], refs[2:-3], sum_ref[...], tile_ref)


def first_closing(labels, own_place, stacks, *refs):
    row_refs, refs = refs[:2], refs[2:]
    stack_refs, (sum_ref, compat_ref, *refs) = refs[:stacks], refs[stacks:]
    unary_refs, own_refs, (q_ref, tile_ref) = refs[:2], refs[2:-2], refs[-2:]
    total = first_part(labels, own_place, row_refs, stack_refs, sum_ref[...], tile_ref)
    labels_now = [ref[index][:labels] for ref in own_refs for index in range(ref.shape[0])]
    unary = jnp.concatenate([ref[...] for ref in unary_refs], axis=1)
    probs, _ = finish(total, jnp.concatenate(labels_now, axis=1), unary, compat_ref)
    q_ref[...] = probs.astype(jnp.bfloat16)


def partial_message(q_ref, tile_ref):
    return lax.dot_general(
        q_ref[...], tile_ref[...], (((1,), (1,)), ((), ())), preferred_element_type=jnp.float32
    )


def second_parts(q_ref, *refs):
    count = len(refs) // 2
    for tile_ref, part_ref in zip(refs[:count], refs[count:]):
        part_ref[...] = partial_message(q_ref, tile_ref)


def second_stacked(q_ref, *refs):
    for index, tile_ref in enumerate(refs[:-1]):
        refs[-1][index] = partial_message(q_ref, tile_ref)


def second_sums(given_ref, *refs):
    count = len(refs) // 2
    for index in range(count):
        refs[count + index][...] = refs[index][...] + given_ref[index]


def second_closing(own_place, q_ref, near_ref, compat_ref, *refs):
    probs_ref, pairwise_ref = refs[-2:]
    labels, own = probs_ref.shape
    total = refs[0][...]
    for part_ref in refs[1:-2]:
        total = total + part_ref[...]
    unary = near_ref[pl.ds(0, labels), :]
    probs, pairwise = finish(
        total, q_ref[:, pl.ds(own_place * own, own)], unary, compat_ref
    )
    probs_ref[...] = probs
    pairwise_ref[...] = pairwise


def swap(value, blk_steps, grp_steps=0, rising=None):
    blks, grps = lax.axis_size("blk"), lax.axis_size("grp")
    pairs = [
        (
            blk * grps + grp,
            (blk ^ blk_steps if paired("blk") else (blk + blk_steps) % blks) * grps
            + (grp ^ grp_steps if paired("grp") else (grp + grp_steps) % grps),
        )
        for blk in range(blks)
        for grp in range(grps)
    ]
    if rising is not None:
        pairs = [pair for pair in pairs if (pair[0] % grps < pair[1] % grps) == rising]
    return lax.ppermute(value, ("blk", "grp"), pairs)


def group_partners(value):
    count = lax.axis_size("grp")
    crossed = paired("blk") and paired("grp") and lax.axis_size("blk") > 1
    step = lambda steps, rising=None: swap(
        value, 2 * steps // count if crossed else 0, steps, rising
    )
    if count < 4:
        near = [(value,)] + [(step(steps),) for steps in range(1, count)]
        return near[1:], near[:1]
    falling = step(count - 1, False)
    rising = step(count - 1, True)
    half = count // 2
    near = [(value,)] + [(step(steps),) for steps in range(half, count - 1)]
    rest = [(falling, rising)] + [(step(steps),) for steps in range(half - 1, 0, -1)]
    return rest, near, falling


def paired(axis):
    count = lax.axis_size(axis)
    return count & (count - 1) == 0


def small(dims, kind):
    return math.prod(dims) * jnp.dtype(kind).itemsize <= KEPT_BYTES


def call(kernel, out_shapes, *operands):
    return pl.pallas_call(
        kernel,
        out_shape=tuple(out_shapes),
        cost_estimate=pl.CostEstimate(flops=SCHEDULE_COST, transcendentals=0, bytes_accessed=SCHEDULE_COST),
        compiler_params=pltpu.CompilerParams(vmem_limit_bytes=VMEM_LIMIT),
    )(*operands)


def hold(*operands):
    return [
        pltpu.with_memory_space_constraint(operand, pltpu.VMEM)
        if small(operand.shape, operand.dtype) else operand
        for operand in operands
    ]


def kept(dims, kind, copies=1):
    if small((copies,) + dims, kind):
        return pltpu.VMEM(dims, kind)
    return jax.ShapeDtypeStruct(dims, kind)


def shards(unary, member, features, compat):
    labels, own = unary.shape
    nears = lax.axis_size("grp")
    count = lax.axis_size("blk") * nears
    sent, held = call(
        prepare_kernel,
        [kept((labels + 8, own), jnp.float32), kept(compat.shape, jnp.float32)],
        features, member[None], unary, compat,
    )
    late_half, early_half, *early_also = group_partners(sent)
    own_place = len(late_half)
    halves = [
        call(
            functools.partial(pack_kernel, labels, [len(arrays) for arrays in some], len(also)),
            [
                kept((len(some), labels + 8, own), jnp.bfloat16),
                kept((AUX, len(some) * own), jnp.bfloat16),
                kept((labels, len(some) * own), jnp.float32),
            ],
            *hold(*also, *[array for arrays in some for array in arrays]),
        )
        for some, also in ((late_half, []), (early_half, early_also))
    ]
    packed, rows, near_unary = zip(*halves)
    parts = lax.axis_size("blk")
    tile_kind = kept((own, nears * own), jnp.bfloat16, parts)
    total_kind = kept((labels, nears * own), jnp.float32)
    tiles, totals = [], []

    def first(*stack):
        total, tile = call(
            functools.partial(first_middle if totals else first_opening, labels, own_place),
            [total_kind, tile_kind], *hold(*rows, *stack, *totals[-1:]),
        )
        tiles.append(tile)
        totals.append(total)
        return total

    def join(some):
        kind = kept((nears, labels + 8, own), jnp.bfloat16)
        return call(join_kernel, [kind], *hold(*some))[0]

    joined = join(packed)
    if paired("blk"):
        steps = list(range(3, parts, 2))
        far = [[swap(some, step) for step in steps] for some in packed]
        beside = swap(joined, 1)
        first(*packed)
        late, early = far
        *late, _ = lax.optimization_barrier((*late, first(beside)))
        stacks = list(zip(late, early))
        stacks += [(swap(join(some), 1),) for some in stacks]
        steps = [0, 1] + steps + [step - 1 for step in steps]
    else:
        steps = list(range(parts))
        stacks = [[swap(joined, step)] for step in steps[1:]]
        first(*packed)
        first(*stacks.pop(0))
    *middle, last = stacks
    for stack in middle:
        first(*stack)
    q_near, tile = call(
        functools.partial(first_closing, labels, own_place, len(last)),
        [kept((labels, nears * own), jnp.bfloat16), tile_kind],
        *hold(*rows, *last, totals[-1], held, *near_unary, *packed),
    )
    tiles.append(tile)

    if parts * math.prod(tile_kind.shape) * 2 <= KEPT_BYTES:
        tiles = hold(*tiles)
    part_kind = kept((labels, own), jnp.float32)
    tile_of = dict(zip(steps, tiles))
    if paired("blk"):
        even, odd = list(range(2, parts, 2)), list(range(3, parts, 2))
        (stacked,) = call(
            second_stacked, [kept((len(even), labels, own), jnp.float32)],
            *hold(q_near), *[tile_of[step] for step in even],
        )
        q_near, stacked = lax.optimization_barrier((q_near, stacked))
        here, beside, *mine = call(
            second_parts, [part_kind] * (2 + len(odd)),
            *hold(q_near), *[tile_of[step] for step in [0, 1] + odd],
        )
        sums = call(second_sums, [part_kind] * len(odd), *hold(swap(stacked, 1), *mine))
        beside, *sums = lax.optimization_barrier((beside, *sums))
        arrived = [swap(part, step) for part, step in zip(sums, odd)]
        arrived.append(swap(beside, 1))
    else:
        here, *away = call(
            second_parts, [part_kind] * parts, *hold(q_near), *[tile_of[step] for step in steps]
        )
        arrived = [swap(part, parts - step) for part, step in zip(away, steps[1:])]
    return call(
        functools.partial(second_closing, own_place),
        [jax.ShapeDtypeStruct((labels, own), jnp.float32)] * 2,
        *hold(q_near, sent, held, here, *arrived),
    )


def solution(mesh):
    in_specs = (P(None, ("scene", "blk", "grp")), P(("scene", "blk", "grp")), P(None, "scene"), P())
    out_specs = (P(None, ("scene", "blk", "grp")), P(None, ("scene", "blk", "grp")))
    return jax.shard_map(shards, mesh=mesh, in_specs=in_specs, out_specs=out_specs, check_vma=False)
```

```python
import functools
import math

import jax
import jax.numpy as jnp
from jax import lax
from jax.experimental import pallas as pl
from jax.experimental.pallas import tpu as pltpu
from jax.sharding import PartitionSpec as P

AUX = 16
LANES = 128
VMEM_LIMIT = 56 * 1024 * 1024
KEPT_BYTES = 4 * 1024 * 1024
SCHEDULE_COST = 10 ** 10


def normalize(logits):
    raised = jnp.exp(logits)
    return raised / jnp.sum(raised, axis=0, keepdims=True)


def three_parts(value):
    high = value.astype(jnp.bfloat16).astype(jnp.float32)
    middle = (value - high).astype(jnp.bfloat16).astype(jnp.float32)
    return [high, middle, value - high - middle]


def pick_features(features_ref, member):
    feats, points = features_ref.shape
    own = member.shape[1]
    groups = points // LANES
    wide = features_ref[...].astype(jnp.float32)
    wide = jnp.concatenate([wide, jnp.zeros((8 - feats, points), jnp.float32)], axis=0)
    table = jnp.concatenate(
        [wide[:, group * LANES:(group + 1) * LANES] for group in range(groups)], axis=0
    ).astype(jnp.bfloat16)
    lane = lax.broadcasted_iota(jnp.int32, (LANES, own), 0)
    chosen = jnp.where(lane == member % LANES, 1.0, 0.0).astype(jnp.bfloat16)
    found = jnp.dot(table, chosen, preferred_element_type=jnp.float32)
    found = found.reshape(groups, 8, own)
    group = lax.broadcasted_iota(jnp.int32, (groups, 8, own), 0)
    return jnp.sum(jnp.where(group == (member // LANES)[None], found, 0.0), axis=0)


def prepare_kernel(features_ref, member_ref, unary_ref, compat_ref, sent_ref, held_ref):
    labels = unary_ref.shape[0]
    sent_ref[pl.ds(0, labels), :] = unary_ref[...]
    sent_ref[pl.ds(labels, 8), :] = pick_features(features_ref, member_ref[...])
    held_ref[...] = compat_ref[...]


def half_norms(feats):
    return three_parts(-0.5 * jnp.sum(feats * feats, axis=0, keepdims=True))


def product_sides(feats):
    own = feats.shape[1]
    norms = half_norms(feats)
    ones = jnp.ones((3, own), jnp.float32)
    spare = jnp.zeros((AUX - 8 - 6, own), jnp.float32)
    columns = jnp.concatenate([feats] + norms + [ones, spare], axis=0)
    rows = jnp.concatenate([feats, ones] + norms + [spare], axis=0)
    return columns.astype(jnp.bfloat16), rows.astype(jnp.bfloat16)


def pack_kernel(labels, *refs):
    near_refs, packed_ref, rows_ref = refs[:-2], refs[-2], refs[-1]
    for place, near_ref in enumerate(near_refs):
        own = near_ref.shape[1]
        feats = near_ref[pl.ds(labels, 8), :]
        probs = normalize(-near_ref[pl.ds(0, labels), :])
        packed_ref[place] = jnp.concatenate([probs, feats], axis=0).astype(jnp.bfloat16)
        rows_ref[:, pl.ds(place * own, own)] = product_sides(feats)[1]


def join_kernel(*refs):
    joined_ref = refs[-1]
    base = 0
    for ref in refs[:-1]:
        joined_ref[pl.ds(base, ref.shape[0])] = ref[...]
        base += ref.shape[0]


def finish(message, qb, unary, compat_ref):
    message = message - qb.astype(jnp.float32)
    pairwise = jnp.dot(
        compat_ref[...], message, precision=lax.Precision.HIGHEST,
        preferred_element_type=jnp.float32,
    )
    return normalize(-unary - pairwise), pairwise


def first_part(labels, row_refs, stack_refs, total, tile_ref):
    blocks = [(ref, index) for ref in stack_refs for index in range(ref.shape[0])]
    rows = jnp.concatenate([ref[...] for ref in row_refs], axis=1)

    def exponents(place):
        ref, index = blocks[place]
        columns = product_sides(ref[index][labels:].astype(jnp.float32))[0]
        return lax.dot_general(
            columns, rows, (((0,), (0,)), ((), ())), preferred_element_type=jnp.float32
        )

    ahead = exponents(0)
    for place, (ref, index) in enumerate(blocks):
        exponent = ahead
        if place + 1 < len(blocks):
            ahead = exponents(place + 1)
        tile = jnp.exp(exponent).astype(jnp.bfloat16)
        if place == 0 and tile_ref is not None:
            tile_ref[...] = tile
        total = total + jnp.dot(ref[index][:labels], tile, preferred_element_type=jnp.float32)
    return total


def first_early(labels, rows_ref, packed_ref, total_ref, tile_ref):
    start = jnp.zeros(total_ref.shape, jnp.float32)
    total_ref[...] = first_part(labels, [rows_ref], [packed_ref], start, tile_ref)


def first_opening(labels, *refs):
    near_rows, rest_rows, near_ref, rest_ref, sum_ref, early_tile_ref, total_ref, tile_ref = refs
    near, rest = near_rows.shape[1], rest_rows.shape[1]
    beyond = first_part(
        labels, [rest_rows], [near_ref], jnp.zeros((labels, rest), jnp.float32),
        tile_ref.at[:, pl.ds(near, rest)],
    )
    tile_ref[:, pl.ds(0, near)] = early_tile_ref[...]
    start = jnp.concatenate([sum_ref[...], beyond], axis=1)
    total_ref[...] = first_part(labels, [near_rows, rest_rows], [rest_ref], start, None)


def first_middle(labels, *refs):
    sum_ref, total_ref, tile_ref = refs[-3:]
    total_ref[...] = first_part(labels, refs[:2], refs[2:-3], sum_ref[...], tile_ref)


def first_closing(labels, nears, stacks, *refs):
    row_refs, refs = refs[:2], refs[2:]
    stack_refs, (sum_ref, compat_ref, *refs) = refs[:stacks], refs[stacks:]
    near_refs, refs = refs[:nears], refs[nears:]
    own_refs, (q_ref, tile_ref) = refs[:-2], refs[-2:]
    total = first_part(labels, row_refs, stack_refs, sum_ref[...], tile_ref)
    labels_now = [ref[index][:labels] for ref in own_refs for index in range(ref.shape[0])]
    unary = [near_ref[pl.ds(0, labels), :] for near_ref in near_refs]
    probs, _ = finish(
        total, jnp.concatenate(labels_now, axis=1), jnp.concatenate(unary, axis=1), compat_ref
    )
    q_ref[...] = probs.astype(jnp.bfloat16)


def partial_message(q_ref, tile_ref):
    return lax.dot_general(
        q_ref[...], tile_ref[...], (((1,), (1,)), ((), ())), preferred_element_type=jnp.float32
    )


def second_parts(q_ref, *refs):
    count = len(refs) // 2
    for tile_ref, part_ref in zip(refs[:count], refs[count:]):
        part_ref[...] = partial_message(q_ref, tile_ref)


def second_stacked(q_ref, *refs):
    for index, tile_ref in enumerate(refs[:-1]):
        refs[-1][index] = partial_message(q_ref, tile_ref)


def second_sums(given_ref, *refs):
    count = len(refs) // 2
    for index in range(count):
        refs[count + index][...] = refs[index][...] + given_ref[index]


def second_closing(q_ref, near_ref, compat_ref, *refs):
    probs_ref, pairwise_ref = refs[-2:]
    labels, own = probs_ref.shape
    total = refs[0][...]
    for part_ref in refs[1:-2]:
        total = total + part_ref[...]
    unary = near_ref[pl.ds(0, labels), :]
    probs, pairwise = finish(total, q_ref[:, pl.ds(0, own)], unary, compat_ref)
    probs_ref[...] = probs
    pairwise_ref[...] = pairwise


def swap(value, blk_steps, grp_steps=0):
    blks, grps = lax.axis_size("blk"), lax.axis_size("grp")
    pairs = [
        (
            blk * grps + grp,
            (blk ^ blk_steps if paired("blk") else (blk + blk_steps) % blks) * grps
            + (grp ^ grp_steps if paired("grp") else (grp + grp_steps) % grps),
        )
        for blk in range(blks)
        for grp in range(grps)
    ]
    return lax.ppermute(value, ("blk", "grp"), pairs)


def group_partners(value):
    count = lax.axis_size("grp")
    order = sorted(range(1, count), reverse=True)
    crossed = paired("blk") and paired("grp") and lax.axis_size("blk") > 1
    return [value] + [
        swap(value, 2 * steps // count if crossed else 0, steps) for steps in order
    ]


def paired(axis):
    count = lax.axis_size(axis)
    return count & (count - 1) == 0


def small(dims, kind):
    return math.prod(dims) * jnp.dtype(kind).itemsize <= KEPT_BYTES


def call(kernel, out_shapes, *operands):
    return pl.pallas_call(
        kernel,
        out_shape=tuple(out_shapes),
        cost_estimate=pl.CostEstimate(flops=SCHEDULE_COST, transcendentals=0, bytes_accessed=SCHEDULE_COST),
        compiler_params=pltpu.CompilerParams(vmem_limit_bytes=VMEM_LIMIT),
    )(*operands)


def hold(*operands):
    return [
        pltpu.with_memory_space_constraint(operand, pltpu.VMEM)
        if small(operand.shape, operand.dtype) else operand
        for operand in operands
    ]


def kept(dims, kind, copies=1):
    if small((copies,) + dims, kind):
        return pltpu.VMEM(dims, kind)
    return jax.ShapeDtypeStruct(dims, kind)


def shards(unary, member, features, compat):
    labels, own = unary.shape
    nears = lax.axis_size("grp")
    count = lax.axis_size("blk") * nears
    sent, held = call(
        prepare_kernel,
        [kept((labels + 8, own), jnp.float32), kept(compat.shape, jnp.float32)],
        features, member[None], unary, compat,
    )
    near = group_partners(sent)
    half = max(1, nears // 2)

    def pack_half(some):
        return call(
            functools.partial(pack_kernel, labels),
            [
                kept((len(some), labels + 8, own), jnp.bfloat16),
                kept((AUX, len(some) * own), jnp.bfloat16),
            ],
            *hold(*some),
        )

    near_packed, near_rows = pack_half(near[:half])
    early_sum, early_tile = call(
        functools.partial(first_early, labels),
        [kept((labels, half * own), jnp.float32), kept((own, half * own), jnp.bfloat16)],
        *hold(near_rows, near_packed),
    )
    early_sum, *rest = lax.optimization_barrier((early_sum, *near[half:]))
    rest_packed, rest_rows = pack_half(rest)
    packed, rows = (near_packed, rest_packed), (near_rows, rest_rows)
    parts = lax.axis_size("blk")
    tile_kind = kept((own, nears * own), jnp.bfloat16, parts)
    total_kind = kept((labels, nears * own), jnp.float32)
    tiles, totals = [], []

    def first(*stack):
        total, tile = call(
            functools.partial(first_middle if totals else first_opening, labels),
            [total_kind, tile_kind],
            *hold(*rows, *stack, *(totals[-1:] or [early_sum, early_tile])),
        )
        tiles.append(tile)
        totals.append(total)
        return total

    def join(some):
        kind = kept((nears, labels + 8, own), jnp.bfloat16)
        return call(join_kernel, [kind], *hold(*some))[0]

    joined = join(packed)
    if paired("blk"):
        steps = list(range(3, parts, 2))
        far = [[swap(some, step) for step in steps] for some in packed]
        beside = swap(joined, 1)
        first(*packed)
        early, late = far
        *late, _ = lax.optimization_barrier((*late, first(beside)))
        stacks = list(zip(early, late))
        stacks += [(swap(join(some), 1),) for some in stacks]
        steps = [0, 1] + steps + [step - 1 for step in steps]
    else:
        steps = list(range(parts))
        stacks = [[swap(joined, step)] for step in steps[1:]]
        first(*packed)
        first(*stacks.pop(0))
    *middle, last = stacks
    for stack in middle:
        first(*stack)
    q_near, tile = call(
        functools.partial(first_closing, labels, nears, len(last)),
        [kept((labels, nears * own), jnp.bfloat16), tile_kind],
        *hold(*rows, *last, totals[-1], held, *near, *packed),
    )
    tiles.append(tile)

    if parts * math.prod(tile_kind.shape) * 2 <= KEPT_BYTES:
        tiles = hold(*tiles)
    part_kind = kept((labels, own), jnp.float32)
    tile_of = dict(zip(steps, tiles))
    if paired("blk"):
        even, odd = list(range(2, parts, 2)), list(range(3, parts, 2))
        (stacked,) = call(
            second_stacked, [kept((len(even), labels, own), jnp.float32)],
            *hold(q_near), *[tile_of[step] for step in even],
        )
        q_near, stacked = lax.optimization_barrier((q_near, stacked))
        here, beside, *mine = call(
            second_parts, [part_kind] * (2 + len(odd)),
            *hold(q_near), *[tile_of[step] for step in [0, 1] + odd],
        )
        sums = call(second_sums, [part_kind] * len(odd), *hold(swap(stacked, 1), *mine))
        beside, *sums = lax.optimization_barrier((beside, *sums))
        arrived = [swap(part, step) for part, step in zip(sums, odd)]
        arrived.append(swap(beside, 1))
    else:
        here, *away = call(
            second_parts, [part_kind] * parts, *hold(q_near), *[tile_of[step] for step in steps]
        )
        arrived = [swap(part, parts - step) for part, step in zip(away, steps[1:])]
    return call(
        second_closing,
        [jax.ShapeDtypeStruct((labels, own), jnp.float32)] * 2,
        *hold(q_near, sent, held, here, *arrived),
    )


def solution(mesh):
    in_specs = (P(None, ("scene", "blk", "grp")), P(("scene", "blk", "grp")), P(None, "scene"), P())
    out_specs = (P(None, ("scene", "blk", "grp")), P(None, ("scene", "blk", "grp")))
    return jax.shard_map(shards, mesh=mesh, in_specs=in_specs, out_specs=out_specs, check_vma=False)
```

```python
import functools
import math

import jax
import jax.numpy as jnp
from jax import lax
from jax.experimental import pallas as pl
from jax.experimental.pallas import tpu as pltpu
from jax.sharding import PartitionSpec as P

AUX = 16
LANES = 128
VMEM_LIMIT = 56 * 1024 * 1024
KEPT_BYTES = 4 * 1024 * 1024
SCHEDULE_COST = 10 ** 10


def normalize(logits):
    raised = jnp.exp(logits)
    return raised / jnp.sum(raised, axis=0, keepdims=True)


def three_parts(value):
    high = value.astype(jnp.bfloat16).astype(jnp.float32)
    middle = (value - high).astype(jnp.bfloat16).astype(jnp.float32)
    return [high, middle, value - high - middle]


def pick_features(features_ref, member):
    feats, points = features_ref.shape
    own = member.shape[1]
    groups = points // LANES
    wide = features_ref[...].astype(jnp.float32)
    wide = jnp.concatenate([wide, jnp.zeros((8 - feats, points), jnp.float32)], axis=0)
    table = jnp.concatenate(
        [wide[:, group * LANES:(group + 1) * LANES] for group in range(groups)], axis=0
    ).astype(jnp.bfloat16)
    lane = lax.broadcasted_iota(jnp.int32, (LANES, own), 0)
    chosen = jnp.where(lane == member % LANES, 1.0, 0.0).astype(jnp.bfloat16)
    found = jnp.dot(table, chosen, preferred_element_type=jnp.float32)
    found = found.reshape(groups, 8, own)
    group = lax.broadcasted_iota(jnp.int32, (groups, 8, own), 0)
    return jnp.sum(jnp.where(group == (member // LANES)[None], found, 0.0), axis=0)


def prepare_kernel(features_ref, member_ref, unary_ref, compat_ref, sent_ref, held_ref):
    labels = unary_ref.shape[0]
    sent_ref[pl.ds(0, labels), :] = unary_ref[...]
    sent_ref[pl.ds(labels, 8), :] = pick_features(features_ref, member_ref[...])
    held_ref[...] = compat_ref[...]


def half_norms(feats):
    return three_parts(-0.5 * jnp.sum(feats * feats, axis=0, keepdims=True))


def product_sides(feats):
    own = feats.shape[1]
    norms = half_norms(feats)
    ones = jnp.ones((3, own), jnp.float32)
    spare = jnp.zeros((AUX - 8 - 6, own), jnp.float32)
    columns = jnp.concatenate([feats] + norms + [ones, spare], axis=0)
    rows = jnp.concatenate([feats, ones] + norms + [spare], axis=0)
    return columns.astype(jnp.bfloat16), rows.astype(jnp.bfloat16)


def pack_kernel(labels, *refs):
    near_refs, packed_ref, rows_ref = refs[:-2], refs[-2], refs[-1]
    for place, near_ref in enumerate(near_refs):
        own = near_ref.shape[1]
        feats = near_ref[pl.ds(labels, 8), :]
        probs = normalize(-near_ref[pl.ds(0, labels), :])
        packed_ref[place] = jnp.concatenate([probs, feats], axis=0).astype(jnp.bfloat16)
        rows_ref[:, pl.ds(place * own, own)] = product_sides(feats)[1]


def join_kernel(*refs):
    joined_ref = refs[-1]
    base = 0
    for ref in refs[:-1]:
        joined_ref[pl.ds(base, ref.shape[0])] = ref[...]
        base += ref.shape[0]


def finish(message, qb, unary, compat_ref):
    message = message - qb.astype(jnp.float32)
    pairwise = jnp.dot(
        compat_ref[...], message, precision=lax.Precision.HIGHEST,
        preferred_element_type=jnp.float32,
    )
    return normalize(-unary - pairwise), pairwise


def first_part(labels, row_refs, stack_refs, total, tile_ref):
    blocks = [(ref, index) for ref in stack_refs for index in range(ref.shape[0])]
    rows = jnp.concatenate([ref[...] for ref in row_refs], axis=1)

    def exponents(place):
        ref, index = blocks[place]
        columns = product_sides(ref[index][labels:].astype(jnp.float32))[0]
        return lax.dot_general(
            columns, rows, (((0,), (0,)), ((), ())), preferred_element_type=jnp.float32
        )

    ahead = exponents(0)
    for place, (ref, index) in enumerate(blocks):
        exponent = ahead
        if place + 1 < len(blocks):
            ahead = exponents(place + 1)
        tile = jnp.exp(exponent).astype(jnp.bfloat16)
        if place == 0 and tile_ref is not None:
            tile_ref[...] = tile
        total = total + jnp.dot(ref[index][:labels], tile, preferred_element_type=jnp.float32)
    return total


def first_early(labels, rows_ref, packed_ref, total_ref, tile_ref):
    start = jnp.zeros(total_ref.shape, jnp.float32)
    total_ref[...] = first_part(labels, [rows_ref], [packed_ref], start, tile_ref)


def first_opening(labels, *refs):
    near_rows, rest_rows, near_ref, rest_ref, sum_ref, early_tile_ref, total_ref, tile_ref = refs
    near, rest = near_rows.shape[1], rest_rows.shape[1]
    beyond = first_part(
        labels, [rest_rows], [near_ref], jnp.zeros((labels, rest), jnp.float32),
        tile_ref.at[:, pl.ds(near, rest)],
    )
    tile_ref[:, pl.ds(0, near)] = early_tile_ref[...]
    start = jnp.concatenate([sum_ref[...], beyond], axis=1)
    total_ref[...] = first_part(labels, [near_rows, rest_rows], [rest_ref], start, None)


def first_middle(labels, *refs):
    sum_ref, total_ref, tile_ref = refs[-3:]
    total_ref[...] = first_part(labels, refs[:2], refs[2:-3], sum_ref[...], tile_ref)


def first_closing(labels, nears, stacks, *refs):
    row_refs, refs = refs[:2], refs[2:]
    stack_refs, (sum_ref, compat_ref, *refs) = refs[:stacks], refs[stacks:]
    near_refs, refs = refs[:nears], refs[nears:]
    own_refs, (q_ref, tile_ref) = refs[:-2], refs[-2:]
    total = first_part(labels, row_refs, stack_refs, sum_ref[...], tile_ref)
    labels_now = [ref[index][:labels] for ref in own_refs for index in range(ref.shape[0])]
    unary = [near_ref[pl.ds(0, labels), :] for near_ref in near_refs]
    probs, _ = finish(
        total, jnp.concatenate(labels_now, axis=1), jnp.concatenate(unary, axis=1), compat_ref
    )
    q_ref[...] = probs.astype(jnp.bfloat16)


def partial_message(q_ref, tile_ref):
    return lax.dot_general(
        q_ref[...], tile_ref[...], (((1,), (1,)), ((), ())), preferred_element_type=jnp.float32
    )


def second_parts(q_ref, *refs):
    count = len(refs) // 2
    for tile_ref, part_ref in zip(refs[:count], refs[count:]):
        part_ref[...] = partial_message(q_ref, tile_ref)


def second_stacked(q_ref, *refs):
    for index, tile_ref in enumerate(refs[:-1]):
        refs[-1][index] = partial_message(q_ref, tile_ref)


def second_sums(given_ref, *refs):
    count = len(refs) // 2
    for index in range(count):
        refs[count + index][...] = refs[index][...] + given_ref[index]


def second_closing(q_ref, near_ref, compat_ref, *refs):
    probs_ref, pairwise_ref = refs[-2:]
    labels, own = probs_ref.shape
    total = refs[0][...]
    for part_ref in refs[1:-2]:
        total = total + part_ref[...]
    unary = near_ref[pl.ds(0, labels), :]
    probs, pairwise = finish(total, q_ref[:, pl.ds(0, own)], unary, compat_ref)
    probs_ref[...] = probs
    pairwise_ref[...] = pairwise


def swap(value, blk_steps, grp_steps=0):
    blks, grps = lax.axis_size("blk"), lax.axis_size("grp")
    pairs = [
        (
            blk * grps + grp,
            (blk ^ blk_steps if paired("blk") else (blk + blk_steps) % blks) * grps
            + (grp ^ grp_steps if paired("grp") else (grp + grp_steps) % grps),
        )
        for blk in range(blks)
        for grp in range(grps)
    ]
    return lax.ppermute(value, ("blk", "grp"), pairs)


def group_partners(value):
    count = lax.axis_size("grp")
    order = sorted(range(1, count), reverse=True)
    crossed = paired("blk") and paired("grp") and lax.axis_size("blk") > 1
    return [value] + [
        swap(value, 2 * steps // count if crossed else 0, steps) for steps in order
    ]


def paired(axis):
    count = lax.axis_size(axis)
    return count & (count - 1) == 0


def small(dims, kind):
    return math.prod(dims) * jnp.dtype(kind).itemsize <= KEPT_BYTES


def call(kernel, out_shapes, *operands):
    return pl.pallas_call(
        kernel,
        out_shape=tuple(out_shapes),
        cost_estimate=pl.CostEstimate(flops=SCHEDULE_COST, transcendentals=0, bytes_accessed=SCHEDULE_COST),
        compiler_params=pltpu.CompilerParams(vmem_limit_bytes=VMEM_LIMIT),
    )(*operands)


def hold(*operands):
    return [
        pltpu.with_memory_space_constraint(operand, pltpu.VMEM)
        if small(operand.shape, operand.dtype) else operand
        for operand in operands
    ]


def kept(dims, kind, copies=1):
    if small((copies,) + dims, kind):
        return pltpu.VMEM(dims, kind)
    return jax.ShapeDtypeStruct(dims, kind)


def shards(unary, member, features, compat):
    labels, own = unary.shape
    nears = lax.axis_size("grp")
    count = lax.axis_size("blk") * nears
    sent, held = call(
        prepare_kernel,
        [kept((labels + 8, own), jnp.float32), kept(compat.shape, jnp.float32)],
        features, member[None], unary, compat,
    )
    near = group_partners(sent)
    half = max(1, nears // 2)

    def pack_half(some):
        return call(
            functools.partial(pack_kernel, labels),
            [
                kept((len(some), labels + 8, own), jnp.bfloat16),
                kept((AUX, len(some) * own), jnp.bfloat16),
            ],
            *hold(*some),
        )

    near_packed, near_rows = pack_half(near[:half])
    copied = call(join_kernel, [kept(near_packed.shape, jnp.bfloat16)], *hold(near_packed))[0]
    beside_near = swap(copied, 1)
    early_sum, early_tile = call(
        functools.partial(first_early, labels),
        [kept((labels, half * own), jnp.float32), kept((own, half * own), jnp.bfloat16)],
        *hold(near_rows, near_packed),
    )
    early_sum, beside_near, *rest = lax.optimization_barrier(
        (early_sum, beside_near, *near[half:])
    )
    rest_packed, rest_rows = pack_half(rest)
    packed, rows = (near_packed, rest_packed), (near_rows, rest_rows)
    parts = lax.axis_size("blk")
    tile_kind = kept((own, nears * own), jnp.bfloat16, parts)
    total_kind = kept((labels, nears * own), jnp.float32)
    tiles, totals = [], []

    def first(*stack):
        total, tile = call(
            functools.partial(first_middle if totals else first_opening, labels),
            [total_kind, tile_kind],
            *hold(*rows, *stack, *(totals[-1:] or [early_sum, early_tile])),
        )
        tiles.append(tile)
        totals.append(total)
        return total

    def join(some):
        blocks = sum(stack.shape[0] for stack in some)
        kind = kept((blocks, labels + 8, own), jnp.bfloat16)
        return call(join_kernel, [kind], *hold(*some))[0]

    if paired("blk"):
        steps = list(range(3, parts, 2))
        far = [[swap(some, step) for step in steps] for some in packed]
        beside = [beside_near, swap(join([rest_packed]), 1)]
        first(*packed)
        early, late = far
        *late, _ = lax.optimization_barrier((*late, first(*beside)))
        stacks = list(zip(early, late))
        stacks += [(swap(join(some), 1),) for some in stacks]
        steps = [0, 1] + steps + [step - 1 for step in steps]
    else:
        steps = list(range(parts))
        joined = join(packed)
        stacks = [[swap(joined, step)] for step in steps[1:]]
        first(*packed)
        first(*stacks.pop(0))
    *middle, last = stacks
    for stack in middle:
        first(*stack)
    q_near, tile = call(
        functools.partial(first_closing, labels, nears, len(last)),
        [kept((labels, nears * own), jnp.bfloat16), tile_kind],
        *hold(*rows, *last, totals[-1], held, *near, *packed),
    )
    tiles.append(tile)

    if parts * math.prod(tile_kind.shape) * 2 <= KEPT_BYTES:
        tiles = hold(*tiles)
    part_kind = kept((labels, own), jnp.float32)
    tile_of = dict(zip(steps, tiles))
    if paired("blk"):
        even, odd = list(range(2, parts, 2)), list(range(3, parts, 2))
        (stacked,) = call(
            second_stacked, [kept((len(even), labels, own), jnp.float32)],
            *hold(q_near), *[tile_of[step] for step in even],
        )
        q_near, stacked = lax.optimization_barrier((q_near, stacked))
        here, beside, *mine = call(
            second_parts, [part_kind] * (2 + len(odd)),
            *hold(q_near), *[tile_of[step] for step in [0, 1] + odd],
        )
        sums = call(second_sums, [part_kind] * len(odd), *hold(swap(stacked, 1), *mine))
        beside, *sums = lax.optimization_barrier((beside, *sums))
        arrived = [swap(part, step) for part, step in zip(sums, odd)]
        arrived.append(swap(beside, 1))
    else:
        here, *away = call(
            second_parts, [part_kind] * parts, *hold(q_near), *[tile_of[step] for step in steps]
        )
        arrived = [swap(part, parts - step) for part, step in zip(away, steps[1:])]
    return call(
        second_closing,
        [jax.ShapeDtypeStruct((labels, own), jnp.float32)] * 2,
        *hold(q_near, sent, held, here, *arrived),
    )


def solution(mesh):
    in_specs = (P(None, ("scene", "blk", "grp")), P(("scene", "blk", "grp")), P(None, "scene"), P())
    out_specs = (P(None, ("scene", "blk", "grp")), P(None, ("scene", "blk", "grp")))
    return jax.shard_map(shards, mesh=mesh, in_specs=in_specs, out_specs=out_specs, check_vma=False)
```

```python
import functools
import math

import jax
import jax.numpy as jnp
from jax import lax
from jax.experimental import pallas as pl
from jax.experimental.pallas import tpu as pltpu
from jax.sharding import PartitionSpec as P

AUX = 16
LANES = 128
VMEM_LIMIT = 56 * 1024 * 1024
KEPT_BYTES = 4 * 1024 * 1024
SCHEDULE_COST = 10 ** 10


def normalize(logits):
    raised = jnp.exp(logits)
    return raised / jnp.sum(raised, axis=0, keepdims=True)


def three_parts(value):
    high = value.astype(jnp.bfloat16).astype(jnp.float32)
    middle = (value - high).astype(jnp.bfloat16).astype(jnp.float32)
    return [high, middle, value - high - middle]


def pick_features(features_ref, member):
    feats, points = features_ref.shape
    own = member.shape[1]
    groups = points // LANES
    wide = features_ref[...].astype(jnp.float32)
    wide = jnp.concatenate([wide, jnp.zeros((8 - feats, points), jnp.float32)], axis=0)
    table = jnp.concatenate(
        [wide[:, group * LANES:(group + 1) * LANES] for group in range(groups)], axis=0
    ).astype(jnp.bfloat16)
    lane = lax.broadcasted_iota(jnp.int32, (LANES, own), 0)
    chosen = jnp.where(lane == member % LANES, 1.0, 0.0).astype(jnp.bfloat16)
    found = jnp.dot(table, chosen, preferred_element_type=jnp.float32)
    found = found.reshape(groups, 8, own)
    group = lax.broadcasted_iota(jnp.int32, (groups, 8, own), 0)
    return jnp.sum(jnp.where(group == (member // LANES)[None], found, 0.0), axis=0)


def prepare_kernel(features_ref, member_ref, unary_ref, compat_ref, sent_ref, held_ref):
    labels = unary_ref.shape[0]
    sent_ref[pl.ds(0, labels), :] = unary_ref[...]
    sent_ref[pl.ds(labels, 8), :] = pick_features(features_ref, member_ref[...])
    held_ref[...] = compat_ref[...]


def half_norms(feats):
    return three_parts(-0.5 * jnp.sum(feats * feats, axis=0, keepdims=True))


def product_sides(feats):
    own = feats.shape[1]
    norms = half_norms(feats)
    ones = jnp.ones((3, own), jnp.float32)
    spare = jnp.zeros((AUX - 8 - 6, own), jnp.float32)
    columns = jnp.concatenate([feats] + norms + [ones, spare], axis=0)
    rows = jnp.concatenate([feats, ones] + norms + [spare], axis=0)
    return columns.astype(jnp.bfloat16), rows.astype(jnp.bfloat16)


def pack_kernel(labels, *refs):
    near_refs, packed_ref, rows_ref = refs[:-2], refs[-2], refs[-1]
    for place, near_ref in enumerate(near_refs):
        own = near_ref.shape[1]
        feats = near_ref[pl.ds(labels, 8), :]
        probs = normalize(-near_ref[pl.ds(0, labels), :])
        packed_ref[place] = jnp.concatenate([probs, feats], axis=0).astype(jnp.bfloat16)
        rows_ref[:, pl.ds(place * own, own)] = product_sides(feats)[1]


def join_kernel(*refs):
    joined_ref = refs[-1]
    base = 0
    for ref in refs[:-1]:
        joined_ref[pl.ds(base, ref.shape[0])] = ref[...]
        base += ref.shape[0]


def finish(message, qb, unary, compat_ref):
    message = message - qb.astype(jnp.float32)
    pairwise = jnp.dot(
        compat_ref[...], message, precision=lax.Precision.HIGHEST,
        preferred_element_type=jnp.float32,
    )
    return normalize(-unary - pairwise), pairwise


def first_part(labels, row_refs, stack_refs, total, tile_ref):
    blocks = [(ref, index) for ref in stack_refs for index in range(ref.shape[0])]
    rows = jnp.concatenate([ref[...] for ref in row_refs], axis=1)

    def exponents(place):
        ref, index = blocks[place]
        columns = product_sides(ref[index][labels:].astype(jnp.float32))[0]
        return lax.dot_general(
            columns, rows, (((0,), (0,)), ((), ())), preferred_element_type=jnp.float32
        )

    ahead = exponents(0)
    for place, (ref, index) in enumerate(blocks):
        exponent = ahead
        if place + 1 < len(blocks):
            ahead = exponents(place + 1)
        tile = jnp.exp(exponent).astype(jnp.bfloat16)
        if place == 0 and tile_ref is not None:
            tile_ref[...] = tile
        total = total + jnp.dot(ref[index][:labels], tile, preferred_element_type=jnp.float32)
    return total


def first_early(labels, rows_ref, packed_ref, total_ref, tile_ref):
    start = jnp.zeros(total_ref.shape, jnp.float32)
    total_ref[...] = first_part(labels, [rows_ref], [packed_ref], start, tile_ref)


def first_opening(labels, *refs):
    near_rows, rest_rows, near_ref, rest_ref, sum_ref, early_tile_ref, total_ref, tile_ref = refs
    near, rest = near_rows.shape[1], rest_rows.shape[1]
    beyond = first_part(
        labels, [rest_rows], [near_ref], jnp.zeros((labels, rest), jnp.float32),
        tile_ref.at[:, pl.ds(near, rest)],
    )
    tile_ref[:, pl.ds(0, near)] = early_tile_ref[...]
    start = jnp.concatenate([sum_ref[...], beyond], axis=1)
    total_ref[...] = first_part(labels, [near_rows, rest_rows], [rest_ref], start, None)


def first_middle(labels, *refs):
    sum_ref, total_ref, tile_ref = refs[-3:]
    total_ref[...] = first_part(labels, refs[:2], refs[2:-3], sum_ref[...], tile_ref)


def first_closing(labels, nears, stacks, *refs):
    row_refs, refs = refs[:2], refs[2:]
    stack_refs, (sum_ref, compat_ref, *refs) = refs[:stacks], refs[stacks:]
    near_refs, refs = refs[:nears], refs[nears:]
    own_refs, (q_ref, tile_ref) = refs[:-2], refs[-2:]
    total = first_part(labels, row_refs, stack_refs, sum_ref[...], tile_ref)
    labels_now = [ref[index][:labels] for ref in own_refs for index in range(ref.shape[0])]
    unary = [near_ref[pl.ds(0, labels), :] for near_ref in near_refs]
    probs, _ = finish(
        total, jnp.concatenate(labels_now, axis=1), jnp.concatenate(unary, axis=1), compat_ref
    )
    q_ref[...] = probs.astype(jnp.bfloat16)


def partial_message(q_ref, tile_ref):
    return lax.dot_general(
        q_ref[...], tile_ref[...], (((1,), (1,)), ((), ())), preferred_element_type=jnp.float32
    )


def second_parts(q_ref, *refs):
    count = len(refs) // 2
    for tile_ref, part_ref in zip(refs[:count], refs[count:]):
        part_ref[...] = partial_message(q_ref, tile_ref)


def second_stacked(q_ref, *refs):
    for index, tile_ref in enumerate(refs[:-1]):
        refs[-1][index] = partial_message(q_ref, tile_ref)


def second_sums(given_ref, *refs):
    count = len(refs) // 2
    for index in range(count):
        refs[count + index][...] = refs[index][...] + given_ref[index]


def second_closing(q_ref, near_ref, compat_ref, *refs):
    probs_ref, pairwise_ref = refs[-2:]
    labels, own = probs_ref.shape
    total = refs[0][...]
    for part_ref in refs[1:-2]:
        total = total + part_ref[...]
    unary = near_ref[pl.ds(0, labels), :]
    probs, pairwise = finish(total, q_ref[:, pl.ds(0, own)], unary, compat_ref)
    probs_ref[...] = probs
    pairwise_ref[...] = pairwise


def swap(value, blk_steps, grp_steps=0):
    blks, grps = lax.axis_size("blk"), lax.axis_size("grp")
    pairs = [
        (
            blk * grps + grp,
            (blk ^ blk_steps if paired("blk") else (blk + blk_steps) % blks) * grps
            + (grp ^ grp_steps if paired("grp") else (grp + grp_steps) % grps),
        )
        for blk in range(blks)
        for grp in range(grps)
    ]
    return lax.ppermute(value, ("blk", "grp"), pairs)


def group_partners(value):
    count = lax.axis_size("grp")
    order = sorted(range(1, count), key=lambda steps: (steps != count - 1, steps))
    crossed = paired("blk") and paired("grp") and lax.axis_size("blk") > 1
    return [value] + [
        swap(value, 2 * steps // count if crossed else 0, steps) for steps in order
    ]


def paired(axis):
    count = lax.axis_size(axis)
    return count & (count - 1) == 0


def small(dims, kind):
    return math.prod(dims) * jnp.dtype(kind).itemsize <= KEPT_BYTES


def call(kernel, out_shapes, *operands):
    return pl.pallas_call(
        kernel,
        out_shape=tuple(out_shapes),
        cost_estimate=pl.CostEstimate(flops=SCHEDULE_COST, transcendentals=0, bytes_accessed=SCHEDULE_COST),
        compiler_params=pltpu.CompilerParams(vmem_limit_bytes=VMEM_LIMIT),
    )(*operands)


def hold(*operands):
    return [
        pltpu.with_memory_space_constraint(operand, pltpu.VMEM)
        if small(operand.shape, operand.dtype) else operand
        for operand in operands
    ]


def kept(dims, kind, copies=1):
    if small((copies,) + dims, kind):
        return pltpu.VMEM(dims, kind)
    return jax.ShapeDtypeStruct(dims, kind)


def shards(unary, member, features, compat):
    labels, own = unary.shape
    nears = lax.axis_size("grp")
    count = lax.axis_size("blk") * nears
    sent, held = call(
        prepare_kernel,
        [kept((labels + 8, own), jnp.float32), kept(compat.shape, jnp.float32)],
        features, member[None], unary, compat,
    )
    near = group_partners(sent)
    half = max(1, nears // 2)

    def pack_half(some):
        return call(
            functools.partial(pack_kernel, labels),
            [
                kept((len(some), labels + 8, own), jnp.bfloat16),
                kept((AUX, len(some) * own), jnp.bfloat16),
            ],
            *hold(*some),
        )

    near_packed, near_rows = pack_half(near[:half])
    early_sum, early_tile = call(
        functools.partial(first_early, labels),
        [kept((labels, half * own), jnp.float32), kept((own, half * own), jnp.bfloat16)],
        *hold(near_rows, near_packed),
    )
    early_sum, *rest = lax.optimization_barrier((early_sum, *near[half:]))
    rest_packed, rest_rows = pack_half(rest)
    packed, rows = (near_packed, rest_packed), (near_rows, rest_rows)
    parts = lax.axis_size("blk")
    tile_kind = kept((own, nears * own), jnp.bfloat16, parts)
    total_kind = kept((labels, nears * own), jnp.float32)
    tiles, totals = [], []

    def first(*stack):
        total, tile = call(
            functools.partial(first_middle if totals else first_opening, labels),
            [total_kind, tile_kind],
            *hold(*rows, *stack, *(totals[-1:] or [early_sum, early_tile])),
        )
        tiles.append(tile)
        totals.append(total)
        return total

    def join(some):
        kind = kept((nears, labels + 8, own), jnp.bfloat16)
        return call(join_kernel, [kind], *hold(*some))[0]

    joined = join(packed)
    if paired("blk"):
        steps = list(range(3, parts, 2))
        far = [[swap(some, step) for step in steps] for some in packed]
        beside = swap(joined, 1)
        first(*packed)
        early, late = far
        *late, _ = lax.optimization_barrier((*late, first(beside)))
        stacks = list(zip(early, late))
        stacks += [(swap(join(some), 1),) for some in stacks]
        steps = [0, 1] + steps + [step - 1 for step in steps]
    else:
        steps = list(range(parts))
        stacks = [[swap(joined, step)] for step in steps[1:]]
        first(*packed)
        first(*stacks.pop(0))
    *middle, last = stacks
    for stack in middle:
        first(*stack)
    q_near, tile = call(
        functools.partial(first_closing, labels, nears, len(last)),
        [kept((labels, nears * own), jnp.bfloat16), tile_kind],
        *hold(*rows, *last, totals[-1], held, *near, *packed),
    )
    tiles.append(tile)

    if parts * math.prod(tile_kind.shape) * 2 <= KEPT_BYTES:
        tiles = hold(*tiles)
    part_kind = kept((labels, own), jnp.float32)
    tile_of = dict(zip(steps, tiles))
    if paired("blk"):
        even, odd = list(range(2, parts, 2)), list(range(3, parts, 2))
        (stacked,) = call(
            second_stacked, [kept((len(even), labels, own), jnp.float32)],
            *hold(q_near), *[tile_of[step] for step in even],
        )
        q_near, stacked = lax.optimization_barrier((q_near, stacked))
        here, beside, *mine = call(
            second_parts, [part_kind] * (2 + len(odd)),
            *hold(q_near), *[tile_of[step] for step in [0, 1] + odd],
        )
        sums = call(second_sums, [part_kind] * len(odd), *hold(swap(stacked, 1), *mine))
        beside, *sums = lax.optimization_barrier((beside, *sums))
        arrived = [swap(part, step) for part, step in zip(sums, odd)]
        arrived.append(swap(beside, 1))
    else:
        here, *away = call(
            second_parts, [part_kind] * parts, *hold(q_near), *[tile_of[step] for step in steps]
        )
        arrived = [swap(part, parts - step) for part, step in zip(away, steps[1:])]
    return call(
        second_closing,
        [jax.ShapeDtypeStruct((labels, own), jnp.float32)] * 2,
        *hold(q_near, sent, held, here, *arrived),
    )


def solution(mesh):
    in_specs = (P(None, ("scene", "blk", "grp")), P(("scene", "blk", "grp")), P(None, "scene"), P())
    out_specs = (P(None, ("scene", "blk", "grp")), P(None, ("scene", "blk", "grp")))
    return jax.shard_map(shards, mesh=mesh, in_specs=in_specs, out_specs=out_specs, check_vma=False)
```

```python
import functools
import math

import jax
import jax.numpy as jnp
from jax import lax
from jax.experimental import pallas as pl
from jax.experimental.pallas import tpu as pltpu
from jax.sharding import PartitionSpec as P

AUX = 16
LANES = 128
VMEM_LIMIT = 56 * 1024 * 1024
KEPT_BYTES = 4 * 1024 * 1024
SCHEDULE_COST = 10 ** 10


def normalize(logits):
    raised = jnp.exp(logits)
    return raised / jnp.sum(raised, axis=0, keepdims=True)


def three_parts(value):
    high = value.astype(jnp.bfloat16).astype(jnp.float32)
    middle = (value - high).astype(jnp.bfloat16).astype(jnp.float32)
    return [high, middle, value - high - middle]


def pick_features(features_ref, member):
    feats, points = features_ref.shape
    own = member.shape[1]
    groups = points // LANES
    wide = features_ref[...].astype(jnp.float32)
    wide = jnp.concatenate([wide, jnp.zeros((8 - feats, points), jnp.float32)], axis=0)
    table = jnp.concatenate(
        [wide[:, group * LANES:(group + 1) * LANES] for group in range(groups)], axis=0
    ).astype(jnp.bfloat16)
    lane = lax.broadcasted_iota(jnp.int32, (LANES, own), 0)
    chosen = jnp.where(lane == member % LANES, 1.0, 0.0).astype(jnp.bfloat16)
    found = jnp.dot(table, chosen, preferred_element_type=jnp.float32)
    found = found.reshape(groups, 8, own)
    group = lax.broadcasted_iota(jnp.int32, (groups, 8, own), 0)
    return jnp.sum(jnp.where(group == (member // LANES)[None], found, 0.0), axis=0)


def prepare_kernel(
    features_ref, member_ref, unary_ref, compat_ref, sent_ref, held_ref, held_unary_ref
):
    unary = unary_ref[...]
    high, low, _ = three_parts(unary)
    feats = pick_features(features_ref, member_ref[...])
    sent_ref[...] = jnp.concatenate([high, low, feats], axis=0).astype(jnp.bfloat16)
    held_ref[...] = compat_ref[...]
    held_unary_ref[...] = unary


def unary_of(near, labels):
    return near[:labels].astype(jnp.float32) + near[labels:2 * labels].astype(jnp.float32)


def half_norms(feats):
    return three_parts(-0.5 * jnp.sum(feats * feats, axis=0, keepdims=True))


def product_sides(feats):
    own = feats.shape[1]
    norms = half_norms(feats)
    ones = jnp.ones((3, own), jnp.float32)
    spare = jnp.zeros((AUX - 8 - 6, own), jnp.float32)
    columns = jnp.concatenate([feats] + norms + [ones, spare], axis=0)
    rows = jnp.concatenate([feats, ones] + norms + [spare], axis=0)
    return columns.astype(jnp.bfloat16), rows.astype(jnp.bfloat16)


def pack_kernel(labels, *refs):
    near_refs, packed_ref, rows_ref = refs[:-2], refs[-2], refs[-1]
    for place, near_ref in enumerate(near_refs):
        own = near_ref.shape[1]
        near = near_ref[...]
        feats = near[2 * labels:].astype(jnp.float32)
        probs = normalize(-unary_of(near, labels))
        packed_ref[place] = jnp.concatenate([probs, feats], axis=0).astype(jnp.bfloat16)
        rows_ref[:, pl.ds(place * own, own)] = product_sides(feats)[1]


def join_kernel(*refs):
    joined_ref = refs[-1]
    base = 0
    for ref in refs[:-1]:
        joined_ref[pl.ds(base, ref.shape[0])] = ref[...]
        base += ref.shape[0]


def finish(message, qb, unary, compat_ref):
    message = message - qb.astype(jnp.float32)
    pairwise = jnp.dot(
        compat_ref[...], message, precision=lax.Precision.HIGHEST,
        preferred_element_type=jnp.float32,
    )
    return normalize(-unary - pairwise), pairwise


def first_part(labels, row_refs, stack_refs, total, tile_ref):
    blocks = [(ref, index) for ref in stack_refs for index in range(ref.shape[0])]
    rows = jnp.concatenate([ref[...] for ref in row_refs], axis=1)

    def exponents(place):
        ref, index = blocks[place]
        columns = product_sides(ref[index][labels:].astype(jnp.float32))[0]
        return lax.dot_general(
            columns, rows, (((0,), (0,)), ((), ())), preferred_element_type=jnp.float32
        )

    ahead = exponents(0)
    for place, (ref, index) in enumerate(blocks):
        exponent = ahead
        if place + 1 < len(blocks):
            ahead = exponents(place + 1)
        tile = jnp.exp(exponent).astype(jnp.bfloat16)
        if place == 0 and tile_ref is not None:
            tile_ref[...] = tile
        total = total + jnp.dot(ref[index][:labels], tile, preferred_element_type=jnp.float32)
    return total


def first_early(labels, rows_ref, packed_ref, total_ref, tile_ref):
    start = jnp.zeros(total_ref.shape, jnp.float32)
    total_ref[...] = first_part(labels, [rows_ref], [packed_ref], start, tile_ref)


def first_opening(labels, *refs):
    near_rows, rest_rows, near_ref, rest_ref, sum_ref, early_tile_ref, total_ref, tile_ref = refs
    near, rest = near_rows.shape[1], rest_rows.shape[1]
    beyond = first_part(
        labels, [rest_rows], [near_ref], jnp.zeros((labels, rest), jnp.float32),
        tile_ref.at[:, pl.ds(near, rest)],
    )
    tile_ref[:, pl.ds(0, near)] = early_tile_ref[...]
    start = jnp.concatenate([sum_ref[...], beyond], axis=1)
    total_ref[...] = first_part(labels, [near_rows, rest_rows], [rest_ref], start, None)


def first_middle(labels, *refs):
    sum_ref, total_ref, tile_ref = refs[-3:]
    total_ref[...] = first_part(labels, refs[:2], refs[2:-3], sum_ref[...], tile_ref)


def first_closing(labels, nears, stacks, *refs):
    row_refs, refs = refs[:2], refs[2:]
    stack_refs, (sum_ref, compat_ref, *refs) = refs[:stacks], refs[stacks:]
    near_refs, refs = refs[:nears], refs[nears:]
    own_refs, (q_ref, tile_ref) = refs[:-2], refs[-2:]
    total = first_part(labels, row_refs, stack_refs, sum_ref[...], tile_ref)
    labels_now = [ref[index][:labels] for ref in own_refs for index in range(ref.shape[0])]
    unary = [unary_of(near_ref[...], labels) for near_ref in near_refs]
    probs, _ = finish(
        total, jnp.concatenate(labels_now, axis=1), jnp.concatenate(unary, axis=1), compat_ref
    )
    q_ref[...] = probs.astype(jnp.bfloat16)


def partial_message(q_ref, tile_ref):
    return lax.dot_general(
        q_ref[...], tile_ref[...], (((1,), (1,)), ((), ())), preferred_element_type=jnp.float32
    )


def second_parts(q_ref, *refs):
    count = len(refs) // 2
    for tile_ref, part_ref in zip(refs[:count], refs[count:]):
        part_ref[...] = partial_message(q_ref, tile_ref)


def second_stacked(q_ref, *refs):
    for index, tile_ref in enumerate(refs[:-1]):
        refs[-1][index] = partial_message(q_ref, tile_ref)


def second_sums(given_ref, *refs):
    count = len(refs) // 2
    for index in range(count):
        refs[count + index][...] = refs[index][...] + given_ref[index]


def second_closing(q_ref, near_ref, compat_ref, *refs):
    probs_ref, pairwise_ref = refs[-2:]
    labels, own = probs_ref.shape
    total = refs[0][...]
    for part_ref in refs[1:-2]:
        total = total + part_ref[...]
    unary = near_ref[...]
    probs, pairwise = finish(total, q_ref[:, pl.ds(0, own)], unary, compat_ref)
    probs_ref[...] = probs
    pairwise_ref[...] = pairwise


def swap(value, blk_steps, grp_steps=0):
    blks, grps = lax.axis_size("blk"), lax.axis_size("grp")
    pairs = [
        (
            blk * grps + grp,
            (blk ^ blk_steps if paired("blk") else (blk + blk_steps) % blks) * grps
            + (grp ^ grp_steps if paired("grp") else (grp + grp_steps) % grps),
        )
        for blk in range(blks)
        for grp in range(grps)
    ]
    return lax.ppermute(value, ("blk", "grp"), pairs)


def group_partners(value):
    count = lax.axis_size("grp")
    order = sorted(range(1, count), key=lambda steps: (steps != count - 1, steps))
    crossed = paired("blk") and paired("grp") and lax.axis_size("blk") > 1
    return [value] + [
        swap(value, 2 * steps // count if crossed else 0, steps) for steps in order
    ]


def paired(axis):
    count = lax.axis_size(axis)
    return count & (count - 1) == 0


def small(dims, kind):
    return math.prod(dims) * jnp.dtype(kind).itemsize <= KEPT_BYTES


def call(kernel, out_shapes, *operands):
    return pl.pallas_call(
        kernel,
        out_shape=tuple(out_shapes),
        cost_estimate=pl.CostEstimate(flops=SCHEDULE_COST, transcendentals=0, bytes_accessed=SCHEDULE_COST),
        compiler_params=pltpu.CompilerParams(vmem_limit_bytes=VMEM_LIMIT),
    )(*operands)


def hold(*operands):
    return [
        pltpu.with_memory_space_constraint(operand, pltpu.VMEM)
        if small(operand.shape, operand.dtype) else operand
        for operand in operands
    ]


def kept(dims, kind, copies=1):
    if small((copies,) + dims, kind):
        return pltpu.VMEM(dims, kind)
    return jax.ShapeDtypeStruct(dims, kind)


def shards(unary, member, features, compat):
    labels, own = unary.shape
    nears = lax.axis_size("grp")
    count = lax.axis_size("blk") * nears
    sent, held, held_unary = call(
        prepare_kernel,
        [
            kept((2 * labels + 8, own), jnp.bfloat16),
            kept(compat.shape, jnp.float32),
            kept(unary.shape, jnp.float32),
        ],
        features, member[None], unary, compat,
    )
    near = group_partners(sent)
    half = max(1, nears // 2)

    def pack_half(some):
        return call(
            functools.partial(pack_kernel, labels),
            [
                kept((len(some), labels + 8, own), jnp.bfloat16),
                kept((AUX, len(some) * own), jnp.bfloat16),
            ],
            *hold(*some),
        )

    near_packed, near_rows = pack_half(near[:half])
    early_sum, early_tile = call(
        functools.partial(first_early, labels),
        [kept((labels, half * own), jnp.float32), kept((own, half * own), jnp.bfloat16)],
        *hold(near_rows, near_packed),
    )
    early_sum, *rest = lax.optimization_barrier((early_sum, *near[half:]))
    rest_packed, rest_rows = pack_half(rest)
    packed, rows = (near_packed, rest_packed), (near_rows, rest_rows)
    parts = lax.axis_size("blk")
    tile_kind = kept((own, nears * own), jnp.bfloat16, parts)
    total_kind = kept((labels, nears * own), jnp.float32)
    tiles, totals = [], []

    def first(*stack):
        total, tile = call(
            functools.partial(first_middle if totals else first_opening, labels),
            [total_kind, tile_kind],
            *hold(*rows, *stack, *(totals[-1:] or [early_sum, early_tile])),
        )
        tiles.append(tile)
        totals.append(total)
        return total

    def join(some):
        kind = kept((nears, labels + 8, own), jnp.bfloat16)
        return call(join_kernel, [kind], *hold(*some))[0]

    joined = join(packed)
    if paired("blk"):
        steps = list(range(3, parts, 2))
        far = [[swap(some, step) for step in steps] for some in packed]
        beside = swap(joined, 1)
        first(*packed)
        early, late = far
        *late, _ = lax.optimization_barrier((*late, first(beside)))
        stacks = list(zip(early, late))
        stacks += [(swap(join(some), 1),) for some in stacks]
        steps = [0, 1] + steps + [step - 1 for step in steps]
    else:
        steps = list(range(parts))
        stacks = [[swap(joined, step)] for step in steps[1:]]
        first(*packed)
        first(*stacks.pop(0))
    *middle, last = stacks
    for stack in middle:
        first(*stack)
    q_near, tile = call(
        functools.partial(first_closing, labels, nears, len(last)),
        [kept((labels, nears * own), jnp.bfloat16), tile_kind],
        *hold(*rows, *last, totals[-1], held, *near, *packed),
    )
    tiles.append(tile)

    if parts * math.prod(tile_kind.shape) * 2 <= KEPT_BYTES:
        tiles = hold(*tiles)
    part_kind = kept((labels, own), jnp.float32)
    tile_of = dict(zip(steps, tiles))
    if paired("blk"):
        even, odd = list(range(2, parts, 2)), list(range(3, parts, 2))
        (stacked,) = call(
            second_stacked, [kept((len(even), labels, own), jnp.float32)],
            *hold(q_near), *[tile_of[step] for step in even],
        )
        q_near, stacked = lax.optimization_barrier((q_near, stacked))
        here, beside, *mine = call(
            second_parts, [part_kind] * (2 + len(odd)),
            *hold(q_near), *[tile_of[step] for step in [0, 1] + odd],
        )
        sums = call(second_sums, [part_kind] * len(odd), *hold(swap(stacked, 1), *mine))
        beside, *sums = lax.optimization_barrier((beside, *sums))
        arrived = [swap(part, step) for part, step in zip(sums, odd)]
        arrived.append(swap(beside, 1))
    else:
        here, *away = call(
            second_parts, [part_kind] * parts, *hold(q_near), *[tile_of[step] for step in steps]
        )
        arrived = [swap(part, parts - step) for part, step in zip(away, steps[1:])]
    return call(
        second_closing,
        [jax.ShapeDtypeStruct((labels, own), jnp.float32)] * 2,
        *hold(q_near, held_unary, held, here, *arrived),
    )


def solution(mesh):
    in_specs = (P(None, ("scene", "blk", "grp")), P(("scene", "blk", "grp")), P(None, "scene"), P())
    out_specs = (P(None, ("scene", "blk", "grp")), P(None, ("scene", "blk", "grp")))
    return jax.shard_map(shards, mesh=mesh, in_specs=in_specs, out_specs=out_specs, check_vma=False)
```

```python
import functools
import math

import jax
import jax.numpy as jnp
from jax import lax
from jax.experimental import pallas as pl
from jax.experimental.pallas import tpu as pltpu
from jax.sharding import PartitionSpec as P

AUX = 16
LANES = 128
VMEM_LIMIT = 56 * 1024 * 1024
KEPT_BYTES = 4 * 1024 * 1024
SCHEDULE_COST = 10 ** 10


def normalize(logits):
    raised = jnp.exp(logits)
    return raised / jnp.sum(raised, axis=0, keepdims=True)


def three_parts(value):
    high = value.astype(jnp.bfloat16).astype(jnp.float32)
    middle = (value - high).astype(jnp.bfloat16).astype(jnp.float32)
    return [high, middle, value - high - middle]


def pick_features(features_ref, member):
    feats, points = features_ref.shape
    own = member.shape[1]
    groups = points // LANES
    wide = features_ref[...].astype(jnp.float32)
    wide = jnp.concatenate([wide, jnp.zeros((8 - feats, points), jnp.float32)], axis=0)
    table = jnp.concatenate(
        [wide[:, group * LANES:(group + 1) * LANES] for group in range(groups)], axis=0
    ).astype(jnp.bfloat16)
    lane = lax.broadcasted_iota(jnp.int32, (LANES, own), 0)
    chosen = jnp.where(lane == member % LANES, 1.0, 0.0).astype(jnp.bfloat16)
    found = jnp.dot(table, chosen, preferred_element_type=jnp.float32)
    found = found.reshape(groups, 8, own)
    group = lax.broadcasted_iota(jnp.int32, (groups, 8, own), 0)
    return jnp.sum(jnp.where(group == (member // LANES)[None], found, 0.0), axis=0)


def prepare_kernel(
    features_ref, member_ref, unary_ref, compat_ref, sent_ref, held_ref, held_unary_ref
):
    unary = unary_ref[...]
    high, low, _ = three_parts(unary)
    feats = pick_features(features_ref, member_ref[...])
    sent_ref[...] = jnp.concatenate([high, low, feats], axis=0).astype(jnp.bfloat16)
    held_ref[...] = compat_ref[...]
    held_unary_ref[...] = unary


def unary_of(near, labels):
    return near[:labels].astype(jnp.float32) + near[labels:2 * labels].astype(jnp.float32)


def half_norms(feats):
    return three_parts(-0.5 * jnp.sum(feats * feats, axis=0, keepdims=True))


def product_sides(feats):
    own = feats.shape[1]
    norms = half_norms(feats)
    ones = jnp.ones((3, own), jnp.float32)
    spare = jnp.zeros((AUX - 8 - 6, own), jnp.float32)
    columns = jnp.concatenate([feats] + norms + [ones, spare], axis=0)
    rows = jnp.concatenate([feats, ones] + norms + [spare], axis=0)
    return columns.astype(jnp.bfloat16), rows.astype(jnp.bfloat16)


def pack_kernel(labels, *refs):
    near_refs, packed_ref, rows_ref = refs[:-2], refs[-2], refs[-1]
    for place, near_ref in enumerate(near_refs):
        own = near_ref.shape[1]
        near = near_ref[...]
        feats = near[2 * labels:].astype(jnp.float32)
        probs = normalize(-unary_of(near, labels))
        packed_ref[place] = jnp.concatenate([probs, feats], axis=0).astype(jnp.bfloat16)
        rows_ref[:, pl.ds(place * own, own)] = product_sides(feats)[1]


def join_kernel(*refs):
    joined_ref = refs[-1]
    base = 0
    for ref in refs[:-1]:
        joined_ref[pl.ds(base, ref.shape[0])] = ref[...]
        base += ref.shape[0]


def finish(message, qb, unary, compat_ref):
    message = message - qb.astype(jnp.float32)
    pairwise = jnp.dot(
        compat_ref[...], message, precision=lax.Precision.HIGHEST,
        preferred_element_type=jnp.float32,
    )
    return normalize(-unary - pairwise), pairwise


def first_part(labels, row_refs, stack_refs, total, tile_ref):
    blocks = [(ref, index) for ref in stack_refs for index in range(ref.shape[0])]
    rows = jnp.concatenate([ref[...] for ref in row_refs], axis=1)

    def exponents(place):
        ref, index = blocks[place]
        columns = product_sides(ref[index][labels:].astype(jnp.float32))[0]
        return lax.dot_general(
            columns, rows, (((0,), (0,)), ((), ())), preferred_element_type=jnp.float32
        )

    ahead = exponents(0)
    for place, (ref, index) in enumerate(blocks):
        exponent = ahead
        if place + 1 < len(blocks):
            ahead = exponents(place + 1)
        tile = jnp.exp(exponent).astype(jnp.bfloat16)
        if place == 0 and tile_ref is not None:
            tile_ref[...] = tile
        total = total + jnp.dot(ref[index][:labels], tile, preferred_element_type=jnp.float32)
    return total


def first_early(labels, rows_ref, packed_ref, total_ref, tile_ref):
    start = jnp.zeros(total_ref.shape, jnp.float32)
    total_ref[...] = first_part(labels, [rows_ref], [packed_ref], start, tile_ref)


def first_opening(labels, *refs):
    near_rows, rest_rows, near_ref, rest_ref, sum_ref, early_tile_ref, total_ref, tile_ref = refs
    near, rest = near_rows.shape[1], rest_rows.shape[1]
    blocks, _, own = near_ref.shape
    packed = jnp.concatenate([near_ref[index] for index in range(blocks)], axis=1)
    columns = product_sides(packed[labels:].astype(jnp.float32))[0]
    exponent = lax.dot_general(
        columns, rest_rows[...], (((0,), (0,)), ((), ())), preferred_element_type=jnp.float32
    )
    tile = jnp.exp(exponent).astype(jnp.bfloat16)
    tile_ref[:, pl.ds(near, rest)] = tile[:own]
    beyond = jnp.dot(packed[:labels], tile, preferred_element_type=jnp.float32)
    tile_ref[:, pl.ds(0, near)] = early_tile_ref[...]
    start = jnp.concatenate([sum_ref[...], beyond], axis=1)
    total_ref[...] = first_part(labels, [near_rows, rest_rows], [rest_ref], start, None)


def first_middle(labels, *refs):
    sum_ref, total_ref, tile_ref = refs[-3:]
    total_ref[...] = first_part(labels, refs[:2], refs[2:-3], sum_ref[...], tile_ref)


def first_closing(labels, nears, stacks, *refs):
    row_refs, refs = refs[:2], refs[2:]
    stack_refs, (sum_ref, compat_ref, *refs) = refs[:stacks], refs[stacks:]
    near_refs, refs = refs[:nears], refs[nears:]
    own_refs, (q_ref, tile_ref) = refs[:-2], refs[-2:]
    total = first_part(labels, row_refs, stack_refs, sum_ref[...], tile_ref)
    labels_now = [ref[index][:labels] for ref in own_refs for index in range(ref.shape[0])]
    unary = [unary_of(near_ref[...], labels) for near_ref in near_refs]
    probs, _ = finish(
        total, jnp.concatenate(labels_now, axis=1), jnp.concatenate(unary, axis=1), compat_ref
    )
    q_ref[...] = probs.astype(jnp.bfloat16)


def partial_message(q_ref, tile_ref):
    return lax.dot_general(
        q_ref[...], tile_ref[...], (((1,), (1,)), ((), ())), preferred_element_type=jnp.float32
    )


def second_parts(q_ref, *refs):
    count = len(refs) // 2
    for tile_ref, part_ref in zip(refs[:count], refs[count:]):
        part_ref[...] = partial_message(q_ref, tile_ref)


def second_stacked(q_ref, *refs):
    for index, tile_ref in enumerate(refs[:-1]):
        refs[-1][index] = partial_message(q_ref, tile_ref)


def second_sums(given_ref, *refs):
    count = len(refs) // 2
    for index in range(count):
        refs[count + index][...] = refs[index][...] + given_ref[index]


def second_closing(q_ref, near_ref, compat_ref, *refs):
    probs_ref, pairwise_ref = refs[-2:]
    labels, own = probs_ref.shape
    total = refs[0][...]
    for part_ref in refs[1:-2]:
        total = total + part_ref[...]
    unary = near_ref[...]
    probs, pairwise = finish(total, q_ref[:, pl.ds(0, own)], unary, compat_ref)
    probs_ref[...] = probs
    pairwise_ref[...] = pairwise


def swap(value, blk_steps, grp_steps=0):
    blks, grps = lax.axis_size("blk"), lax.axis_size("grp")
    pairs = [
        (
            blk * grps + grp,
            (blk ^ blk_steps if paired("blk") else (blk + blk_steps) % blks) * grps
            + (grp ^ grp_steps if paired("grp") else (grp + grp_steps) % grps),
        )
        for blk in range(blks)
        for grp in range(grps)
    ]
    return lax.ppermute(value, ("blk", "grp"), pairs)


def group_partners(value):
    count = lax.axis_size("grp")
    order = sorted(range(1, count), key=lambda steps: (steps != count - 1, steps))
    crossed = paired("blk") and paired("grp") and lax.axis_size("blk") > 1
    return [value] + [
        swap(value, 2 * steps // count if crossed else 0, steps) for steps in order
    ]


def paired(axis):
    count = lax.axis_size(axis)
    return count & (count - 1) == 0


def small(dims, kind):
    return math.prod(dims) * jnp.dtype(kind).itemsize <= KEPT_BYTES


def call(kernel, out_shapes, *operands):
    return pl.pallas_call(
        kernel,
        out_shape=tuple(out_shapes),
        cost_estimate=pl.CostEstimate(flops=SCHEDULE_COST, transcendentals=0, bytes_accessed=SCHEDULE_COST),
        compiler_params=pltpu.CompilerParams(vmem_limit_bytes=VMEM_LIMIT),
    )(*operands)


def hold(*operands):
    return [
        pltpu.with_memory_space_constraint(operand, pltpu.VMEM)
        if small(operand.shape, operand.dtype) else operand
        for operand in operands
    ]


def kept(dims, kind, copies=1):
    if small((copies,) + dims, kind):
        return pltpu.VMEM(dims, kind)
    return jax.ShapeDtypeStruct(dims, kind)


def shards(unary, member, features, compat):
    labels, own = unary.shape
    nears = lax.axis_size("grp")
    count = lax.axis_size("blk") * nears
    sent, held, held_unary = call(
        prepare_kernel,
        [
            kept((2 * labels + 8, own), jnp.bfloat16),
            kept(compat.shape, jnp.float32),
            kept(unary.shape, jnp.float32),
        ],
        features, member[None], unary, compat,
    )
    near = group_partners(sent)
    half = max(1, nears // 2)

    def pack_half(some):
        return call(
            functools.partial(pack_kernel, labels),
            [
                kept((len(some), labels + 8, own), jnp.bfloat16),
                kept((AUX, len(some) * own), jnp.bfloat16),
            ],
            *hold(*some),
        )

    near_packed, near_rows = pack_half(near[:half])
    early_sum, early_tile = call(
        functools.partial(first_early, labels),
        [kept((labels, half * own), jnp.float32), kept((own, half * own), jnp.bfloat16)],
        *hold(near_rows, near_packed),
    )
    early_sum, *rest = lax.optimization_barrier((early_sum, *near[half:]))
    rest_packed, rest_rows = pack_half(rest)
    packed, rows = (near_packed, rest_packed), (near_rows, rest_rows)
    parts = lax.axis_size("blk")
    tile_kind = kept((own, nears * own), jnp.bfloat16, parts)
    total_kind = kept((labels, nears * own), jnp.float32)
    tiles, totals = [], []

    def first(*stack):
        total, tile = call(
            functools.partial(first_middle if totals else first_opening, labels),
            [total_kind, tile_kind],
            *hold(*rows, *stack, *(totals[-1:] or [early_sum, early_tile])),
        )
        tiles.append(tile)
        totals.append(total)
        return total

    def join(some):
        kind = kept((nears, labels + 8, own), jnp.bfloat16)
        return call(join_kernel, [kind], *hold(*some))[0]

    joined = join(packed)
    if paired("blk"):
        steps = list(range(3, parts, 2))
        far = [[swap(some, step) for step in steps] for some in packed]
        beside = swap(joined, 1)
        first(*packed)
        early, late = far
        *late, _ = lax.optimization_barrier((*late, first(beside)))
        stacks = list(zip(early, late))
        stacks += [(swap(join(some), 1),) for some in stacks]
        steps = [0, 1] + steps + [step - 1 for step in steps]
    else:
        steps = list(range(parts))
        stacks = [[swap(joined, step)] for step in steps[1:]]
        first(*packed)
        first(*stacks.pop(0))
    *middle, last = stacks
    for stack in middle:
        first(*stack)
    q_near, tile = call(
        functools.partial(first_closing, labels, nears, len(last)),
        [kept((labels, nears * own), jnp.bfloat16), tile_kind],
        *hold(*rows, *last, totals[-1], held, *near, *packed),
    )
    tiles.append(tile)

    if parts * math.prod(tile_kind.shape) * 2 <= KEPT_BYTES:
        tiles = hold(*tiles)
    part_kind = kept((labels, own), jnp.float32)
    tile_of = dict(zip(steps, tiles))
    if paired("blk"):
        even, odd = list(range(2, parts, 2)), list(range(3, parts, 2))
        (stacked,) = call(
            second_stacked, [kept((len(even), labels, own), jnp.float32)],
            *hold(q_near), *[tile_of[step] for step in even],
        )
        q_near, stacked = lax.optimization_barrier((q_near, stacked))
        here, beside, *mine = call(
            second_parts, [part_kind] * (2 + len(odd)),
            *hold(q_near), *[tile_of[step] for step in [0, 1] + odd],
        )
        sums = call(second_sums, [part_kind] * len(odd), *hold(swap(stacked, 1), *mine))
        beside, *sums = lax.optimization_barrier((beside, *sums))
        arrived = [swap(part, step) for part, step in zip(sums, odd)]
        arrived.append(swap(beside, 1))
    else:
        here, *away = call(
            second_parts, [part_kind] * parts, *hold(q_near), *[tile_of[step] for step in steps]
        )
        arrived = [swap(part, parts - step) for part, step in zip(away, steps[1:])]
    return call(
        second_closing,
        [jax.ShapeDtypeStruct((labels, own), jnp.float32)] * 2,
        *hold(q_near, held_unary, held, here, *arrived),
    )


def solution(mesh):
    in_specs = (P(None, ("scene", "blk", "grp")), P(("scene", "blk", "grp")), P(None, "scene"), P())
    out_specs = (P(None, ("scene", "blk", "grp")), P(None, ("scene", "blk", "grp")))
    return jax.shard_map(shards, mesh=mesh, in_specs=in_specs, out_specs=out_specs, check_vma=False)
```
